128 devices in a mesh: dp: 32 (over x, y, core), mp: 4 (over z).
Axes of the slice: x: 4, y: 4, z: 4, core: 2. Of those that a mesh axis runs over, the one named last changes fastest.
Arguments:
- id_lists: int32 [8, 39, 8192], P(None, None, 'dp'), may hold values from 0 to 1023
- id_counts: int32 [39, 8192], P(None, 'dp'), may hold values from 1 to 8, as said below
- embed_rows: bfloat16 [32768, 10], P('dp'), may hold values from -6 to 6
- logit_grad: bfloat16 [8192], P('dp'), may hold values from -12 to 12
- bilinear: float32 [10, 10], replicated, may hold values from -2 to 2
- bilinear_momentum: float32 [10, 10], replicated, may hold values from -56 to 56
- bilinear_average: float32 [10, 10], replicated, may hold values from -2 to 2
- squeezer: float32 [39, 13], replicated, may hold values from -3 to 3
- squeezer_momentum: float32 [39, 13], replicated, may hold values from -5 to 5
- squeezer_average: float32 [39, 13], replicated, may hold values from -3 to 3
- exciter: float32 [13, 39], replicated, may hold values from -4 to 4
- exciter_momentum: float32 [13, 39], replicated, may hold values from -5 to 5
- exciter_average: float32 [13, 39], replicated, may hold values from -4 to 4
- pairwise: float32 [20, 741, 400], P('mp'), may hold values from -0.046875 to 0.046875
- pairwise_momentum: float32 [20, 741, 400], P('mp'), may hold values from -2.5 to 2.5
- pairwise_average: float32 [20, 741, 400], P('mp'), may hold values from -0.046875 to 0.046875
- fieldwise: float32 [10, 39, 400], P(None, None, 'mp'), may hold values from -0.3125 to 0.3125
- fieldwise_momentum: float32 [10, 39, 400], P(None, None, 'mp'), may hold values from -4 to 4
- fieldwise_average: float32 [10, 39, 400], P(None, None, 'mp'), may hold values from -0.3125 to 0.3125
- hidden: float32 [2, 400, 400], P(None, None, 'mp'), may hold values from -0.3125 to 0.3125
- hidden_momentum: float32 [2, 400, 400], P(None, None, 'mp'), may hold values from -4 to 4
- hidden_average: float32 [2, 400, 400], P(None, None, 'mp'), may hold values from -0.3125 to 0.3125
- biases: float32 [3, 400], P(None, 'mp'), may hold values from -3 to 3
- biases_momentum: float32 [3, 400], P(None, 'mp'), may hold values from -10 to 10
- biases_average: float32 [3, 400], P(None, 'mp'), may hold values from -3 to 3
- readout: float32 [400], P('mp'), may hold values from -0.3125 to 0.3125
- readout_momentum: float32 [400], P('mp'), may hold values from -256 to 256
- readout_average: float32 [400], P('mp'), may hold values from -0.3125 to 0.3125
- offset: float32 [1], replicated, may hold values from -6 to 6
- offset_momentum: float32 [1], replicated, may hold values from -1024 to 1024
- offset_average: float32 [1], replicated, may hold values from -6 to 6
Outputs:
- logits: float32 [8192], P('dp')
- embed_grad: float32 [10, 39, 8192], P(None, None, 'dp')
- bilinear_velocity: float32 [10, 10], replicated
- bilinear_smoothed: float32 [10, 10], replicated
- bilinear_updated: float32 [10, 10], replicated
- squeezer_velocity: float32 [39, 13], replicated
- squeezer_smoothed: float32 [39, 13], replicated
- squeezer_updated: float32 [39, 13], replicated
- exciter_velocity: float32 [13, 39], replicated
- exciter_smoothed: float32 [13, 39], replicated
- exciter_updated: float32 [13, 39], replicated
- pairwise_velocity: float32 [20, 741, 400], P('mp')
- pairwise_smoothed: float32 [20, 741, 400], P('mp')
- pairwise_updated: float32 [20, 741, 400], P('mp')
- fieldwise_velocity: float32 [10, 39, 400], P(None, None, 'mp')
- fieldwise_smoothed: float32 [10, 39, 400], P(None, None, 'mp')
- fieldwise_updated: float32 [10, 39, 400], P(None, None, 'mp')
- hidden_velocity: float32 [2, 400, 400], P(None, None, 'mp')
- hidden_smoothed: float32 [2, 400, 400], P(None, None, 'mp')
- hidden_updated: float32 [2, 400, 400], P(None, None, 'mp')
- biases_velocity: float32 [3, 400], P(None, 'mp')
- biases_smoothed: float32 [3, 400], P(None, 'mp')
- biases_updated: float32 [3, 400], P(None, 'mp')
- readout_velocity: float32 [400], P('mp')
- readout_smoothed: float32 [400], P('mp')
- readout_updated: float32 [400], P('mp')
- offset_velocity: float32 [1], replicated
- offset_smoothed: float32 [1], replicated
- offset_updated: float32 [1], replicated
The draws below stay inside these ranges and needn't reach their ends.
Inputs may be any that keep to these rules, and one draw needn't show every extreme that they name: `id_lists`: an id of event n indexes the 1024 rows fetched for block n // 256. `id_counts`: slots at or past the count are padding and are ignored.
All inputs are finite; a program needn't handle non-finite values.
Results may differ from the reference program's by a relative error of at most 0.018.
Values may be sent and summed in bfloat16 or wider, within the bound.
A program may use at most 128 MiB of HBM per device.

```python
import jax
import jax.numpy as jnp
import numpy as np
from jax import lax

EMB = 10
FIELDS = 39
REDUCED = 13
UNITS = 400
MAXIDS = 8
BATCH_DEV = 256
PAIRS = 741
EVENTS = 8192
FETCH_ROWS = 1024
N_DP = 32


def draw_id_counts(key, part):
    key = jax.random.fold_in(key, 11)
    counted = jax.random.randint(key, (FIELDS, EVENTS), 1, MAXIDS + 1)
    return counted.at[:, 0].set(MAXIDS).astype(jnp.int32)


def draw_logit_grad(key, part):
    key = jax.random.fold_in(key, 23)
    place = jnp.arange(EVENTS, dtype=jnp.float32) / max(EVENTS - 1, 1)
    values = jnp.clip(jax.random.normal(key, (EVENTS,), jnp.float32), -4.0, 4.0) * (1.0 + 2.0 * place)
    return values.astype(jnp.bfloat16)


def with_ends(array, stream_key, least, high):
    spot = [jax.random.randint(jax.random.fold_in(stream_key, axis), (), 0, length) for axis, length in enumerate(array.shape)]
    widest = array.shape.index(max(array.shape))
    beside = spot[:widest] + [(spot[widest] + 1) % array.shape[widest]] + spot[widest + 1:]
    return array.at[tuple(spot)].set(least).at[tuple(beside)].set(high)


def block_scale(rng, dims, shards, low, high):
    def one(axis_at, shards_of):
        draws = jax.random.uniform(jax.random.fold_in(jax.random.fold_in(rng, 6), axis_at), (shards_of,), jnp.float32, low / len(shards), high / len(shards))
        return jnp.repeat(jnp.exp(draws), dims[axis_at] // shards_of).reshape((-1,) + (1,) * (len(dims) - axis_at - 1))

    level = one(*shards[0])
    for cut in shards[1:]:
        level = level * one(*cut)
    return level


def centred(rng, dims, spread, limit, cuts=(), kind=jnp.bfloat16):
    array = spread * jax.random.normal(rng, dims, jnp.float32)
    if cuts:
        array = array * block_scale(rng, dims, cuts, -0.22, 0.18)
    return jnp.clip(array, -limit, limit).astype(kind)


def setup_inputs(seed: int = 0) -> dict:
    arg_keys = jax.random.split(jax.random.key(seed), 32)
    id_lists = with_ends(jax.random.randint(arg_keys[0], (MAXIDS, FIELDS, EVENTS), 0, FETCH_ROWS), jax.random.fold_in(arg_keys[0], 1), 0, FETCH_ROWS - 1).astype(jnp.int32)
    id_counts = draw_id_counts(jax.random.fold_in(arg_keys[31], 71), 0)
    embed_rows = centred(arg_keys[2], (N_DP * FETCH_ROWS, EMB), 1.0, 6.0, ((0, 32),))
    logit_grad = draw_logit_grad(jax.random.fold_in(arg_keys[31], 71), 0)
    bilinear = centred(arg_keys[4], (EMB, EMB), EMB ** -0.5, 2.0, (), jnp.float32)
    bilinear_momentum = centred(arg_keys[5], (EMB, EMB), (0.1 * EVENTS ** 0.5), 56.0, (), jnp.float32)
    bilinear_average = centred(arg_keys[6], (EMB, EMB), EMB ** -0.5, 2.0, (), jnp.float32)
    squeezer = centred(arg_keys[7], (FIELDS, REDUCED), 4 ** -0.5, 3.0, (), jnp.float32)
    squeezer_momentum = centred(arg_keys[8], (FIELDS, REDUCED), (0.01 * EVENTS ** 0.5), 5.0, (), jnp.float32)
    squeezer_average = centred(arg_keys[9], (FIELDS, REDUCED), 4 ** -0.5, 3.0, (), jnp.float32)
    exciter = centred(arg_keys[10], (REDUCED, FIELDS), 2 ** -0.5, 4.0, (), jnp.float32)
    exciter_momentum = centred(arg_keys[11], (REDUCED, FIELDS), (0.01 * EVENTS ** 0.5), 5.0, (), jnp.float32)
    exciter_average = centred(arg_keys[12], (REDUCED, FIELDS), 2 ** -0.5, 4.0, (), jnp.float32)
    pairwise = centred(arg_keys[13], (2 * EMB, PAIRS, UNITS), (2 * EMB * PAIRS) ** -0.5, 0.046875, ((0, 4),), jnp.float32)
    pairwise_momentum = centred(arg_keys[14], (2 * EMB, PAIRS, UNITS), (0.005 * EVENTS ** 0.5), 2.5, ((0, 4),), jnp.float32)
    pairwise_average = centred(arg_keys[15], (2 * EMB, PAIRS, UNITS), (2 * EMB * PAIRS) ** -0.5, 0.046875, ((0, 4),), jnp.float32)
    fieldwise = centred(arg_keys[16], (EMB, FIELDS, UNITS), (EMB * FIELDS) ** -0.5, 0.3125, ((2, 4),), jnp.float32)
    fieldwise_momentum = centred(arg_keys[17], (EMB, FIELDS, UNITS), (0.008 * EVENTS ** 0.5), 4.0, ((2, 4),), jnp.float32)
    fieldwise_average = centred(arg_keys[18], (EMB, FIELDS, UNITS), (EMB * FIELDS) ** -0.5, 0.3125, ((2, 4),), jnp.float32)
    hidden = centred(arg_keys[19], (2, UNITS, UNITS), UNITS ** -0.5, 0.3125, ((2, 4),), jnp.float32)
    hidden_momentum = centred(arg_keys[20], (2, UNITS, UNITS), (0.008 * EVENTS ** 0.5), 4.0, ((2, 4),), jnp.float32)
    hidden_average = centred(arg_keys[21], (2, UNITS, UNITS), UNITS ** -0.5, 0.3125, ((2, 4),), jnp.float32)
    biases = centred(arg_keys[22], (3, UNITS), 0.5, 3.0, ((1, 4),), jnp.float32)
    biases_momentum = centred(arg_keys[23], (3, UNITS), (0.02 * EVENTS ** 0.5), 10.0, ((1, 4),), jnp.float32)
    biases_average = centred(arg_keys[24], (3, UNITS), 0.5, 3.0, ((1, 4),), jnp.float32)
    readout = centred(arg_keys[25], (UNITS,), UNITS ** -0.5, 0.3125, ((0, 4),), jnp.float32)
    readout_momentum = centred(arg_keys[26], (UNITS,), (0.5 * EVENTS ** 0.5), 256.0, ((0, 4),), jnp.float32)
    readout_average = centred(arg_keys[27], (UNITS,), UNITS ** -0.5, 0.3125, ((0, 4),), jnp.float32)
    offset = centred(arg_keys[28], (1,), 1.0, 6.0, (), jnp.float32)
    offset_momentum = centred(arg_keys[29], (1,), (2.0 * EVENTS ** 0.5), 1024.0, (), jnp.float32)
    offset_average = centred(arg_keys[30], (1,), 1.0, 6.0, (), jnp.float32)
    return {"id_lists": id_lists, "id_counts": id_counts, "embed_rows": embed_rows, "logit_grad": logit_grad, "bilinear": bilinear, "bilinear_momentum": bilinear_momentum, "bilinear_average": bilinear_average, "squeezer": squeezer, "squeezer_momentum": squeezer_momentum, "squeezer_average": squeezer_average, "exciter": exciter, "exciter_momentum": exciter_momentum, "exciter_average": exciter_average, "pairwise": pairwise, "pairwise_momentum": pairwise_momentum, "pairwise_average": pairwise_average, "fieldwise": fieldwise, "fieldwise_momentum": fieldwise_momentum, "fieldwise_average": fieldwise_average, "hidden": hidden, "hidden_momentum": hidden_momentum, "hidden_average": hidden_average, "biases": biases, "biases_momentum": biases_momentum, "biases_average": biases_average, "readout": readout, "readout_momentum": readout_momentum, "readout_average": readout_average, "offset": offset, "offset_momentum": offset_momentum, "offset_average": offset_average}


MOMENTUM = 0.9
RATE = 0.01
FAST_RATE = 0.05
DECAY = 0.8
HIGHEST = lax.Precision.HIGHEST

@jax.custom_vjp
def low(v):
    return lax.optimization_barrier(v.astype(jnp.bfloat16)).astype(jnp.float32)

@jax.custom_vjp
def low_back(v):
    return v

def low_keep(v):
    return (low(v), None)

def low_pass(kept, grad):
    return (grad,)

def back_keep(v):
    return (v, None)

def back_low(kept, grad):
    return (low(grad),)
low.defvjp(low_keep, low_pass)
low_back.defvjp(back_keep, back_low)

def pooling(id_block, count_block, table_block):
    gathered = jnp.take(table_block.T, id_block, axis=1).astype(jnp.float32)
    slots = lax.broadcasted_iota(jnp.int32, id_block.shape, 0)
    keeper = (slots < count_block[None]).astype(jnp.float32)
    totals = lax.optimization_barrier(jnp.sum(gathered * keeper[None], axis=1))
    return totals / count_block.astype(jnp.float32)[None]

def senet(embedded, squeezer, exciter):
    squeezed = lax.optimization_barrier(jnp.mean(embedded, axis=0))
    excited = jax.nn.silu(jnp.einsum('fe,fr->re', squeezed, squeezer, precision=HIGHEST))
    scales = jax.nn.softplus(jnp.einsum('re,rf->fe', excited, exciter, precision=HIGHEST))
    return embedded * scales[None]

def forward(pooled, bilinear, squeezer, exciter, pairwise, fieldwise, hidden, biases, readout, offset):
    embedded = low(pooled)
    reweighted = senet(embedded, squeezer, exciter)
    first_index, second_index = np.triu_indices(FIELDS, 1)

    def all_pairs(source):
        projected = jnp.einsum('lfe,lk->kfe', source, bilinear, precision=HIGHEST)
        return projected[:, first_index, :] * source[:, second_index, :]
    features = low(jnp.concatenate([all_pairs(embedded), all_pairs(reweighted)], axis=0))
    pre_first = jnp.einsum('cpe,cpo->oe', features, low(pairwise), precision=HIGHEST) + jnp.einsum('kfe,kfo->oe', embedded, low(fieldwise), precision=HIGHEST) + biases[0][:, None]
    pre_first = low_back(pre_first)
    active = low(jax.nn.silu(pre_first))
    hidden_low = low(hidden)
    pre_second = low_back(jnp.einsum('ie,io->oe', active, hidden_low[0], precision=HIGHEST) + biases[1][:, None])
    active = low(jax.nn.silu(pre_second))
    pre_third = low_back(jnp.einsum('ie,io->oe', active, hidden_low[1], precision=HIGHEST) + biases[2][:, None])
    active = low(jax.nn.silu(pre_third))
    return jnp.einsum('oe,o->e', active, low(readout), precision=HIGHEST) + offset[0]

def nesterov(weight, momentum, average, grad, step_rate):
    velocity = MOMENTUM * momentum + grad
    updated = weight - step_rate * (grad + MOMENTUM * velocity)
    smoothed = DECAY * average + (1.0 - DECAY) * updated
    return (velocity, smoothed, updated)

def reference(id_lists, id_counts, embed_rows, logit_grad, bilinear, bilinear_momentum, bilinear_average, squeezer, squeezer_momentum, squeezer_average, exciter, exciter_momentum, exciter_average, pairwise, pairwise_momentum, pairwise_average, fieldwise, fieldwise_momentum, fieldwise_average, hidden, hidden_momentum, hidden_average, biases, biases_momentum, biases_average, readout, readout_momentum, readout_average, offset, offset_momentum, offset_average):
    weights = (bilinear, squeezer, exciter, pairwise, fieldwise, hidden, biases, readout, offset)
    list_blocks = id_lists.reshape(MAXIDS, FIELDS, N_DP, BATCH_DEV).transpose(2, 0, 1, 3)
    count_blocks = id_counts.reshape(FIELDS, N_DP, BATCH_DEV).transpose(1, 0, 2)
    table_blocks = embed_rows.reshape(N_DP, FETCH_ROWS, EMB)
    grad_blocks = logit_grad.astype(jnp.float32).reshape(N_DP, BATCH_DEV)

    def one_block(totals, block):
        id_block, count_block, table_block, grad_block = block
        pooled = pooling(id_block, count_block, table_block)
        block_logits, backward = jax.vjp(forward, pooled, *weights)
        grads = backward(grad_block)
        totals = jax.tree.map(jnp.add, totals, tuple(grads[1:]))
        return (totals, (block_logits, grads[0]))
    zeros = tuple((jnp.zeros_like(weight) for weight in weights))
    totals, (logit_blocks, pooled_blocks) = lax.scan(one_block, zeros, (list_blocks, count_blocks, table_blocks, grad_blocks))
    logits = logit_blocks.reshape(EVENTS)
    embed_grad = pooled_blocks.transpose(1, 2, 0, 3).reshape(EMB, FIELDS, EVENTS)
    up_bil = nesterov(bilinear, bilinear_momentum, bilinear_average, totals[0], RATE)
    up_squ = nesterov(squeezer, squeezer_momentum, squeezer_average, totals[1], FAST_RATE)
    up_exc = nesterov(exciter, exciter_momentum, exciter_average, totals[2], FAST_RATE)
    up_pair = nesterov(pairwise, pairwise_momentum, pairwise_average, totals[3], RATE)
    up_field = nesterov(fieldwise, fieldwise_momentum, fieldwise_average, totals[4], RATE)
    up_hidden = nesterov(hidden, hidden_momentum, hidden_average, totals[5], RATE)
    up_bias = nesterov(biases, biases_momentum, biases_average, totals[6], FAST_RATE)
    up_read = nesterov(readout, readout_momentum, readout_average, totals[7], RATE)
    up_off = nesterov(offset, offset_momentum, offset_average, totals[8], RATE)
    return (logits, embed_grad, up_bil[0], up_bil[1], up_bil[2], up_squ[0], up_squ[1], up_squ[2], up_exc[0], up_exc[1], up_exc[2], up_pair[0], up_pair[1], up_pair[2], up_field[0], up_field[1], up_field[2], up_hidden[0], up_hidden[1], up_hidden[2], up_bias[0], up_bias[1], up_bias[2], up_read[0], up_read[1], up_read[2], up_off[0], up_off[1], up_off[2])
```

```python
import jax
import jax.numpy as jnp
import numpy as np
from jax import lax
from jax.experimental import pallas as pl
from jax.experimental.pallas import tpu as pltpu
from jax.sharding import PartitionSpec as P

MOMENTUM = 0.9
RATE = 0.01
FAST_RATE = 0.05
DECAY = 0.8
HIGHEST = lax.Precision.HIGHEST
F32 = jnp.float32
LOW = jnp.bfloat16
MESH = pl.DeviceIdType.MESH
MIB = 1024 * 1024

EMB = 10
FIELDS = 39
FPAD = 40
REDUCED = 13
UNITS = 400
UPAD = 512
UDEV = 100
SLOTS = 8
BATCH = 256
FETCH = 1024
PAIRS = 741
PPAD = 768
HALF = 384
ROWS = 5
TILES = 448
QUART = TILES // 4
KTILES = 75
AUX = 38
SMALL = 104


def dot(left, right, contract, precision=None):
    return lax.dot_general(
        left, right, ((contract[0], contract[1]), ((), ())),
        precision=precision, preferred_element_type=F32,
    )


def nn(left, right, precision=None):
    return dot(left, right, ((1,), (0,)), precision)


def nt(left, right, precision=None):
    return dot(left, right, ((1,), (1,)), precision)


def tn(left, right, precision=None):
    return dot(left, right, ((0,), (0,)), precision)


def nesterov(weight, momentum, average, grad, step_rate):
    velocity = MOMENTUM * momentum + grad
    updated = weight - step_rate * (grad + MOMENTUM * velocity)
    smoothed = DECAY * average + (1.0 - DECAY) * updated
    return (velocity, smoothed, updated)


def pool_kernel(ids_ref, count_ref, rows_ref, out_ref, table, ids_live, counts):
    for chunk in range(8):
        turned = jnp.transpose(rows_ref[128 * chunk:128 * (chunk + 1), :].astype(F32))
        for k in range(EMB):
            table[k, chunk:chunk + 1, :] = turned[k:k + 1, :]
    count = count_ref[...]
    counts[0:FIELDS, :] = count
    counts[FIELDS:FPAD, :] = jnp.ones((1, BATCH), jnp.int32)
    for slot in range(SLOTS):
        ids_live[slot, 0:FIELDS, :] = jnp.where(count > slot, ids_ref[slot], 8 * FETCH)
        ids_live[slot, FIELDS:FPAD, :] = jnp.full((1, BATCH), 8 * FETCH, jnp.int32)
    sublane = lax.broadcasted_iota(jnp.int32, (8, 128), 0)

    def step(it, carry):
        rows = pl.ds(pl.multiple_of(8 * (it // 2), 8), 8)
        lanes = pl.ds(pl.multiple_of(128 * (it % 2), 128), 128)
        ids = [ids_live[slot, rows, lanes] for slot in range(SLOTS)]
        count_now = counts[rows, lanes].astype(F32)
        found = [[] for _ in range(EMB)]
        for row in range(8):
            totals = [None] * EMB
            for slot in range(SLOTS):
                wide = jnp.broadcast_to(ids[slot][row:row + 1, :], (8, 128))
                lane = wide & 127
                hit = (wide >> 7) == sublane
                for k in range(EMB):
                    value = jnp.take_along_axis(table[k], lane, axis=1, mode="promise_in_bounds")
                    value = jnp.where(hit, value, 0.0)
                    totals[k] = value if totals[k] is None else totals[k] + value
            for k in range(EMB):
                found[k].append(jnp.sum(totals[k], axis=0, keepdims=True))
        for k in range(EMB):
            pooled = jnp.concatenate(found[k], axis=0) / count_now
            out_ref[k, rows, lanes] = pooled.astype(LOW).astype(F32)
        return carry

    lax.fori_loop(0, 10, step, 0)


def pool(id_lists, id_counts, embed_rows):
    return pl.pallas_call(
        pool_kernel,
        out_shape=jax.ShapeDtypeStruct((EMB, FPAD, BATCH), F32),
        scratch_shapes=[
            pltpu.VMEM((EMB, 8, 128), F32),
            pltpu.VMEM((SLOTS, FPAD, BATCH), jnp.int32),
            pltpu.VMEM((FPAD, BATCH), jnp.int32),
        ],
        name="pooling",
    )(id_lists, id_counts, embed_rows)


def silu_slope(before):
    gate = jax.nn.sigmoid(before)
    return gate * (1.0 + before * (1.0 - gate))


def softplus(value):
    return jnp.maximum(value, 0.0) + jnp.log1p(jnp.exp(-jnp.abs(value)))


def split(value):
    high = value.astype(LOW).astype(F32)
    return jnp.concatenate([high, value - high], axis=0).astype(LOW)


def step_kernel(
    emb_ref, pair_ref, field_ref, hidden_ref, bias_ref, readout_ref, offset_ref, grad_ref,
    bil_ref, squ_ref, exc_ref, first_ref, second_ref, first_t_ref, second_t_ref, place_ref,
    gout_ref, small_ref, egrad_ref, logit_ref,
    w_full, w_low, left, right, feats, feats_peer, source, scale_s, sq_s, z1_s, z2_s, squ_pad, exc_pad, fpad, fplaced,
    hid_own, hid_all, vec_own, vec_all, hid_full, vec_full,
    pre_part, rs_in, pre_full, gf, gf_peer,
    acc, rs0, rs1, rs2, rs3, aux, aux_in,
    dsrc, eterm, zsend, zrecv, zsend2, zrecv2, zsend3, zrecv3, smalls, small_in,
    w_sem, hid_send, hid_recv, vec_send, vec_recv, feat_sem, rsz_send, rsz_recv, agz_send, agz_recv,
    gf_sem, aux_sem, red_send, red_recv, own_sem, gat_send, gat_recv, core_send, core_recv,
    zs_send, zs_recv, sm_send, sm_recv,
):
    dp = lax.axis_index("dp")
    me = lax.axis_index("mp")
    core = dp % 2
    yy = (dp // 2) % 4
    xx = dp // 8

    def at_dp(x, y, c):
        return (x * 4 + y) * 2 + c

    def low_bit(pos):
        return ((pos + 1) // 2) % 2

    def flip(pos):
        return pos + 1 - 2 * (pos % 2)

    partner = [
        at_dp(flip(xx), yy, core),
        at_dp(xx, flip(yy), core),
        at_dp(3 - xx, yy, core),
        at_dp(xx, 3 - yy, core),
    ]
    bits = [low_bit(xx), low_bit(yy), xx // 2, yy // 2]
    twin = at_dp(xx, yy, 1 - core)
    peers = [(me + off) % 4 for off in (1, 2, 3)]
    stream = me // 2
    columns = (me % 2) * ROWS
    half = ((me + 1) // 2) % 2
    near = flip(me)
    cross = 3 - me

    def remote(src, dst, send, recv, **where):
        return pltpu.make_async_remote_copy(
            src_ref=src, dst_ref=dst, send_sem=send, recv_sem=recv, device_id=where, device_id_type=MESH
        )

    w_copies = []
    for k in range(ROWS):
        w_copies.append(pltpu.make_async_copy(pair_ref.at[k], w_full.at[k], w_sem.at[k]))
        w_copies[k].start()
    barrier = pltpu.get_barrier_semaphore()
    for peer in peers:
        pl.semaphore_signal(barrier, inc=1, device_id={"mp": peer}, device_id_type=MESH)
    for dev in partner + [twin]:
        pl.semaphore_signal(barrier, inc=1, device_id={"dp": dev}, device_id_type=MESH)

    hid_own[...] = jnp.zeros_like(hid_own)
    for layer in range(2):
        hid_own[layer, 0:UNITS, 0:UDEV] = hidden_ref[layer].astype(LOW)
    vec_own[...] = jnp.zeros_like(vec_own)
    vec_own[0:3, 0:UDEV] = bias_ref[...]
    vec_own[3:4, 0:UDEV] = readout_ref[...].astype(LOW).astype(F32)
    pl.semaphore_wait(barrier, 8)

    hid_copies = []
    for n, peer in enumerate(peers):
        hid_copies.append(remote(hid_own, hid_all.at[n], hid_send.at[n], hid_recv.at[n], mp=peer))
        hid_copies.append(remote(vec_own, vec_all.at[n], vec_send.at[n], vec_recv.at[n], mp=peer))
    for copy in hid_copies:
        copy.start()

    squ_pad[...] = jnp.zeros_like(squ_pad)
    squ_pad[0:FIELDS, 0:REDUCED] = squ_ref[...]
    exc_pad[...] = jnp.zeros_like(exc_pad)
    exc_pad[0:REDUCED, 0:FIELDS] = exc_ref[...]
    squeezer = squ_pad[:, 0:16]
    exciter = exc_pad[:, 0:FPAD]
    emb = emb_ref[...]
    squeezed = jnp.sum(emb, axis=0) * (1.0 / EMB)
    z1 = tn(squeezer, squeezed, HIGHEST)
    excited = z1 * jax.nn.sigmoid(z1)
    z2 = tn(exciter, excited, HIGHEST)
    scales = softplus(z2)
    sq_s[...] = squeezed
    z1_s[...] = z1
    z2_s[...] = z2
    scale_s[...] = scales
    factor = jnp.where(stream == 0, jnp.ones_like(scales), scales)
    for k in range(EMB):
        source[k] = emb_ref[k] * factor

    fpad[...] = jnp.zeros_like(fpad)
    for k in range(EMB):
        fpad[FPAD * k:FPAD * k + FIELDS, 0:UDEV] = field_ref[k]
    place_own = place_ref[pl.ds(pl.multiple_of(128 * me, 128), 128), :]
    fplaced[...] = nn(fpad[...].astype(LOW), place_own).astype(LOW)
    emb_low = emb.reshape(EMB * FPAD, BATCH).astype(LOW)
    pre = tn(emb_low, fplaced[...])
    for k in range(ROWS):
        projected = source[0] * bil_ref[0, columns + k]
        for l in range(1, EMB):
            projected = projected + source[l] * bil_ref[l, columns + k]
        left_k = nn(first_ref[...], split(projected))
        right_k = nn(second_ref[...], split(source[columns + k]))
        left[k] = left_k
        right[k] = right_k
        feats[k] = (left_k * right_k).astype(LOW)
        w_copies[k].wait()
        w_low[k, 0:736, :] = w_full[k, 0:736, :].astype(LOW)
        rest = jnp.concatenate([w_full[k, 736:PAIRS, :], jnp.zeros((PPAD - PAIRS, UNITS), F32)], axis=0)
        w_low[k, 736:PPAD, :] = rest.astype(LOW)
    feat_copy = remote(
        feats.at[:, pl.ds(pl.multiple_of(HALF * (1 - core), HALF), HALF), :], feats_peer,
        feat_sem.at[0], feat_sem.at[1], dp=twin,
    )
    feat_copy.start()
    part = jnp.zeros((BATCH, UNITS), F32)
    for k in range(ROWS):
        part = part + tn(feats[k], w_low[k])
    pre_part[:, 384:UPAD] = jnp.zeros((BATCH, UPAD - 384), LOW)
    pre_part[...] = pre.astype(LOW)
    pre_part[:, 0:UNITS] = (part + pre[:, 0:UNITS]).astype(LOW)

    rs_copies = []
    for n, peer in enumerate(peers):
        rows = pl.ds(pl.multiple_of(64 * peer, 64), 64)
        rs_copies.append(remote(pre_part.at[rows], rs_in.at[n], rsz_send.at[n], rsz_recv.at[n], mp=peer))
        rs_copies[n].start()

    for copy in hid_copies:
        copy.wait()
    placed = [nn(hid_own[layer], place_own) for layer in range(2)]
    vec = nn(vec_own[...], place_own.astype(F32), HIGHEST)
    for n in range(3):
        owner = (me + 3 - n) % 4
        place = place_ref[pl.ds(pl.multiple_of(128 * owner, 128), 128), :]
        for layer in range(2):
            placed[layer] = placed[layer] + nn(hid_all[n, layer], place)
        vec = vec + nn(vec_all[n], place.astype(F32), HIGHEST)
    for layer in range(2):
        hid_full[layer] = placed[layer].astype(LOW)
    vec_full[...] = vec

    for copy in rs_copies:
        copy.wait()
    own_rows = pl.ds(pl.multiple_of(64 * me, 64), 64)
    total = pre_part[own_rows, :].astype(F32)
    for n in range(3):
        total = total + rs_in[n].astype(F32)
    pre_full[own_rows, :] = total.astype(LOW)
    ag_copies = []
    for n, peer in enumerate(peers):
        ag_copies.append(remote(pre_full.at[own_rows], pre_full.at[own_rows], agz_send.at[n], agz_recv.at[n], mp=peer))
        ag_copies[n].start()
    for copy in ag_copies:
        copy.wait()

    pre_first = pre_full[...].astype(F32) + vec_full[0:1, :]
    act_first = (pre_first * jax.nn.sigmoid(pre_first)).astype(LOW)
    pre_second = nn(act_first, hid_full[0]) + vec_full[1:2, :]
    act_second = (pre_second * jax.nn.sigmoid(pre_second)).astype(LOW)
    pre_third = nn(act_second, hid_full[1]) + vec_full[2:3, :]
    act_third = (pre_third * jax.nn.sigmoid(pre_third)).astype(LOW)
    row_iota = lax.broadcasted_iota(jnp.int32, (8, UPAD), 0)
    readout = jnp.where(row_iota == 0, vec_full[3:4, :], 0.0).astype(LOW)
    upstream = jnp.where(
        lax.broadcasted_iota(jnp.int32, (8, BATCH), 0) == 0, grad_ref[...].astype(F32), 0.0
    )
    logit_ref[...] = nt(readout, act_third) + offset_ref[0]
    grad_third = (tn(upstream.astype(LOW), readout) * silu_slope(pre_third)).astype(LOW)
    grad_second = (nt(grad_third, hid_full[1]) * silu_slope(pre_second)).astype(LOW)
    grad_first = (nt(grad_second, hid_full[0]) * silu_slope(pre_first)).astype(LOW)
    gf[...] = grad_first
    gf_copy = remote(gf, gf_peer, gf_sem.at[0], gf_sem.at[1], dp=twin)
    gf_copy.start()

    first_mine = nt(grad_first, place_own).astype(LOW)
    second_mine = nt(grad_second, place_own).astype(LOW)
    third_mine = nt(grad_third, place_own).astype(LOW)
    aux[0:25] = nn(emb_low, first_mine).astype(LOW).reshape(25, 16, 128)
    aux[25:50] = tn(act_first, second_mine)[0:UNITS].astype(LOW).reshape(25, 16, 128)
    aux[50:75] = tn(act_second, third_mine)[0:UNITS].astype(LOW).reshape(25, 16, 128)
    aux[75:76] = jnp.zeros((1, 16, 128), LOW)
    aux_copy = remote(
        aux.at[pl.ds(AUX * (1 - core), AUX)], aux_in, aux_sem.at[0], aux_sem.at[1], dp=twin
    )
    aux_copy.start()
    ones = jnp.ones((8, BATCH), LOW)
    vec_grads = jnp.where(row_iota == 0, nn(ones, grad_first), 0.0)
    vec_grads = vec_grads + jnp.where(row_iota == 1, nn(ones, grad_second), 0.0)
    vec_grads = vec_grads + jnp.where(row_iota == 2, nn(ones, grad_third), 0.0)
    vec_grads = vec_grads + jnp.where(row_iota == 3, nn(jnp.broadcast_to(upstream[0:1], (8, BATCH)).astype(LOW), act_third), 0.0)
    vec_grads = vec_grads + jnp.where(row_iota == 4, jnp.sum(upstream), 0.0)
    vec_grads = vec_grads * 0.25
    for j in range(4):
        smalls[0, 72 + 8 * j:80 + 8 * j, :] = vec_grads[:, 128 * j:128 * (j + 1)]

    feat_copy.wait()
    own_half = pl.ds(pl.multiple_of(HALF * core, HALF), HALF)
    gf_copy.wait()
    main_own = gf[:, 0:384]
    main_peer = gf_peer[:, 0:384]
    tail_own = jnp.transpose(gf[:, 384:UPAD].astype(F32))[0:16].astype(LOW)
    tail_peer = jnp.transpose(gf_peer[:, 384:UPAD].astype(F32))[0:16].astype(LOW)
    for k in range(ROWS):
        own = feats[k, own_half, :]
        peer = feats_peer[k]
        grad_main = (nn(own, main_own) + nn(peer, main_peer)).astype(LOW)
        grad_tail = (nt(tail_own, own) + nt(tail_peer, peer)).astype(LOW)
        for j in range(3):
            at = KTILES * k + 24 * j
            acc[at:at + 24] = grad_main[:, 128 * j:128 * (j + 1)].reshape(24, 16, 128)
            acc[KTILES * k + 72 + j] = grad_tail[:, 128 * j:128 * (j + 1)]
    aux_copy.wait()
    aux_mine = aux[pl.ds(AUX * core, AUX)].astype(F32) + aux_in[...].astype(F32)
    acc[KTILES * ROWS:KTILES * ROWS + AUX] = aux_mine.astype(LOW)
    acc[KTILES * ROWS + AUX:TILES] = jnp.zeros((TILES - KTILES * ROWS - AUX, 16, 128), LOW)

    starts = [QUART * q for q in range(4)]
    boxes = [rs0, rs1, rs2, rs3]

    def reduce_send(t):
        n = QUART >> (t + 1)
        copies = []
        for q in range(4):
            d = (q + t) % 4
            away = starts[q] + (1 - bits[d]) * n
            copies.append(remote(acc.at[pl.ds(away, n)], boxes[t].at[q], red_send.at[t, q], red_recv.at[t, q], dp=partner[d]))
            copies[q].start()
            starts[q] = starts[q] + bits[d] * n
        return copies

    def reduce_add(t, copies):
        n = QUART >> (t + 1)
        for q in range(4):
            copies[q].wait()
            keep = pl.ds(starts[q], n)
            acc[keep] = (acc[keep].astype(F32) + boxes[t][q].astype(F32)).astype(LOW)

    moving = reduce_send(0)

    grad_first = gf[...]
    gf_units = grad_first[:, 0:UNITS]
    dprojected = []
    dchosen = []
    for k in range(ROWS):
        dfeat = nt(w_low[k], gf_units)
        dprojected.append(nn(first_t_ref[...], (dfeat * right[k]).astype(LOW)))
        dchosen.append(nn(second_t_ref[...], (dfeat * left[k]).astype(LOW)))
    reduce_add(0, moving)
    moving = reduce_send(1)
    bil_rows = jnp.zeros((16, 128), F32)
    lane_iota = lax.broadcasted_iota(jnp.int32, (16, 128), 1)
    for k in range(ROWS):
        sums = []
        for l in range(EMB):
            product = source[l] * dprojected[k]
            product = product[:, 0:128] + product[:, 128:256]
            sums.append(jnp.sum(product, axis=0, keepdims=True))
        sums.append(jnp.zeros((6, 128), F32))
        row_sum = jnp.sum(jnp.concatenate(sums, axis=0), axis=1, keepdims=True)
        bil_rows = bil_rows + jnp.where(lane_iota == columns + k, row_sum, 0.0)
    smalls[0, 0:16, :] = bil_rows
    for l in range(EMB):
        total = dprojected[0] * bil_ref[l, columns]
        for k in range(1, ROWS):
            total = total + dprojected[k] * bil_ref[l, columns + k]
        dsrc[l] = total
    for k in range(ROWS):
        dsrc[columns + k] = dsrc[columns + k] + dchosen[k]
    eterm[...] = nt(fplaced[...], grad_first).reshape(EMB, FPAD, BATCH)
    lanes_away = pl.ds(pl.multiple_of(128 * (1 - half), 128), 128)
    lanes_own = pl.ds(pl.multiple_of(128 * half, 128), 128)
    zsend[0] = dsrc[:, :, lanes_away].reshape(EMB * FPAD, 128).astype(LOW)
    zsend[1] = eterm[:, :, lanes_away].reshape(EMB * FPAD, 128).astype(LOW)
    z_copy = remote(zsend, zrecv, zs_send.at[0], zs_recv.at[0], mp=near)
    z_copy.start()
    reduce_add(1, moving)
    moving = reduce_send(2)

    z_copy.wait()
    back = dsrc[:, :, lanes_own] + zrecv[0].astype(F32).reshape(EMB, FPAD, 128)
    term = eterm[:, :, lanes_own] + zrecv[1].astype(F32).reshape(EMB, FPAD, 128)
    emb_half = emb_ref[:, :, lanes_own]
    z1 = z1_s[:, lanes_own]
    z2 = z2_s[:, lanes_own]
    dscale = jnp.sum(back * emb_half, axis=0)
    dz2 = dscale * jax.nn.sigmoid(z2)
    excited = z1 * jax.nn.sigmoid(z1)
    dexciter = nt(excited, dz2, HIGHEST)
    dz1 = nn(exciter, dz2, HIGHEST) * silu_slope(z1)
    dsqueezer = nt(sq_s[:, lanes_own], dz1, HIGHEST)
    dsqueezed = nn(squeezer, dz1, HIGHEST) * (1.0 / EMB)
    weighted = jnp.where(stream == 0, jnp.zeros((1, 1), F32), jnp.ones((1, 1), F32))
    through = back * scale_s[:, lanes_own][None] + dsqueezed[None]
    mine = term + jnp.where(stream == 0, back, through)
    zsend2[...] = mine.reshape(EMB * FPAD, 128).astype(LOW)
    z_copy = remote(zsend2, zrecv2, zs_send.at[1], zs_recv.at[1], mp=cross)
    z_copy.start()
    smalls[0, 16:72, :] = jnp.zeros((56, 128), F32)
    smalls[0, 16:56, 0:16] = dsqueezer * weighted
    smalls[0, 56:72, 0:FPAD] = dexciter * weighted
    reduce_add(2, moving)
    moving = reduce_send(3)

    hops = [("mp", near), ("mp", cross), ("dp", twin)] + [("dp", dev) for dev in partner]

    def small_send(t):
        axis, dev = hops[t]
        copy = remote(smalls.at[t], small_in.at[t], sm_send.at[t], sm_recv.at[t], **{axis: dev})
        copy.start()
        return copy

    def small_add(t, copy):
        copy.wait()
        smalls[t + 1] = smalls[t] + small_in[t]

    small = small_send(0)
    z_copy.wait()
    whole = (zsend2[...].astype(F32) + zrecv2[...].astype(F32)).astype(LOW)
    zsend3[...] = whole
    z_copy = remote(zsend3, zrecv3, zs_send.at[2], zs_recv.at[2], mp=near)
    z_copy.start()
    small_add(0, small)
    small = small_send(1)
    reduce_add(3, moving)

    n = QUART >> 4
    own_copies = []
    core_copies = []

    def pass_on(t, q, src, start, count):
        copy = remote(src, gout_ref.at[core, pl.ds(start, count)], core_send.at[t, q], core_recv.at[t, q], dp=twin)
        copy.start()
        core_copies.append(copy)

    moving = []
    for q in range(4):
        piece = acc.at[pl.ds(starts[q], n)]
        where = gout_ref.at[core, pl.ds(starts[q], n)]
        moving.append(remote(piece, where, gat_send.at[3, q], gat_recv.at[3, q], dp=partner[(q + 3) % 4]))
        moving[q].start()
        own_copies.append(pltpu.make_async_copy(piece, where, own_sem.at[q]))
        own_copies[q].start()
        pass_on(4, q, piece, starts[q], n)
    small_add(1, small)
    small = small_send(2)
    for t in (3, 2, 1, 0):
        n = QUART >> (t + 1)
        later = []
        for q in range(4):
            bit = bits[(q + t) % 4]
            moving[q].wait()
            if t == 3:
                own_copies[q].wait()
            came = starts[q] + (1 - 2 * bit) * n
            pass_on(t, q, gout_ref.at[core, pl.ds(came, n)], came, n)
            starts[q] = starts[q] - bit * n
            if t > 0:
                where = gout_ref.at[core, pl.ds(starts[q], 2 * n)]
                later.append(remote(where, where, gat_send.at[t - 1, q], gat_recv.at[t - 1, q], dp=partner[(q + t - 1) % 4]))
                later[q].start()
        moving = later
        small_add(5 - t, small)
        if t > 0:
            small = small_send(6 - t)
    small = small_send(6)
    z_copy.wait()
    egrad_ref[:, :, lanes_own] = zsend3[...].reshape(EMB, FPAD, 128)
    egrad_ref[:, :, lanes_away] = zrecv3[...].reshape(EMB, FPAD, 128)
    small_add(6, small)
    small_ref[0:72] = smalls[7, 0:72, :]
    vec_grads = jnp.concatenate([smalls[7, 72 + 8 * j:80 + 8 * j, :] for j in range(4)], axis=1)
    small_ref[72:80] = nt(vec_grads, place_own.astype(F32), HIGHEST)
    for copy in core_copies:
        copy.wait()


def step(emb, pairwise, fieldwise, hidden, biases, readout, offset, logit_grad, bilinear, squeezer, exciter):
    first_index, second_index = np.triu_indices(FIELDS, 1)
    first = np.zeros((PPAD, FPAD), np.float32)
    second = np.zeros((PPAD, FPAD), np.float32)
    first[np.arange(PAIRS), first_index] = 1.0
    second[np.arange(PAIRS), second_index] = 1.0
    place = np.zeros((UPAD, UPAD), np.float32)
    unit = np.arange(UNITS)
    place[128 * (unit // UDEV) + unit % UDEV, unit] = 1.0
    constants = (
        np.concatenate([first, first], axis=1), np.concatenate([second, second], axis=1), first.T, second.T, place
    )
    constants = [jnp.asarray(value, LOW) for value in constants]
    vmem = pl.BlockSpec(memory_space=pltpu.VMEM)
    smem = pl.BlockSpec(memory_space=pltpu.SMEM)
    hbm = pl.BlockSpec(memory_space=pl.ANY)
    low = lambda *shape: pltpu.VMEM(shape, LOW)
    full = lambda *shape: pltpu.VMEM(shape, F32)
    dma = lambda *shape: pltpu.SemaphoreType.DMA(shape)
    return pl.pallas_call(
        step_kernel,
        out_shape=(
            jax.ShapeDtypeStruct((2, TILES, 16, 128), LOW),
            jax.ShapeDtypeStruct((80, 128), F32),
            jax.ShapeDtypeStruct((EMB, FPAD, BATCH), LOW),
            jax.ShapeDtypeStruct((8, BATCH), F32),
        ),
        in_specs=[vmem, hbm, vmem, vmem, vmem, vmem, smem, vmem, smem, vmem, vmem] + [vmem] * 5,
        out_specs=(hbm, vmem, vmem, vmem),
        scratch_shapes=[
            full(ROWS, PAIRS, UNITS), low(ROWS, PPAD, UNITS),
            full(ROWS, PPAD, BATCH), full(ROWS, PPAD, BATCH), low(ROWS, PPAD, BATCH), low(ROWS, HALF, BATCH),
            full(EMB, FPAD, BATCH), full(FPAD, BATCH), full(FPAD, BATCH), full(16, BATCH), full(FPAD, BATCH),
            full(FPAD, 128), full(16, 128), full(EMB * FPAD, 128), low(EMB * FPAD, UPAD),
            low(2, UPAD, 128), low(3, 2, UPAD, 128), full(8, 128), full(3, 8, 128), low(2, UPAD, UPAD), full(8, UPAD),
            low(BATCH, UPAD), low(3, 64, UPAD), low(BATCH, UPAD), low(BATCH, UPAD), low(BATCH, UPAD),
            low(TILES, 16, 128), low(4, QUART // 2, 16, 128), low(4, QUART // 4, 16, 128),
            low(4, QUART // 8, 16, 128), low(4, QUART // 16, 16, 128), low(2 * AUX, 16, 128), low(AUX, 16, 128),
            full(EMB, FPAD, BATCH), full(EMB, FPAD, BATCH),
            low(2, EMB * FPAD, 128), low(2, EMB * FPAD, 128), low(EMB * FPAD, 128), low(EMB * FPAD, 128),
            low(EMB * FPAD, 128), low(EMB * FPAD, 128), full(8, SMALL, 128), full(7, SMALL, 128),
            dma(ROWS), dma(3), dma(3), dma(3), dma(3), dma(2), dma(3), dma(3), dma(3), dma(3),
            dma(2), dma(2), dma(4, 4), dma(4, 4), dma(4), dma(4, 4), dma(4, 4), dma(5, 4), dma(5, 4),
            dma(3), dma(3), dma(7), dma(7),
        ],
        compiler_params=pltpu.CompilerParams(
            collective_id=0, has_side_effects=True, vmem_limit_bytes=48 * MIB
        ),
        name="step",
    )(
        emb, pairwise, fieldwise, hidden, biases, readout.reshape(1, UDEV), offset, logit_grad.reshape(1, BATCH),
        bilinear, squeezer, exciter, *constants,
    )


def update_kernel(*refs):
    grads, aux, small, egrad, logit = refs[:5]
    sets = [refs[5 + 3 * i:8 + 3 * i] for i in range(9)]
    logits_out, egrad_out = refs[32:34]
    outs = [refs[34 + 3 * i:37 + 3 * i] for i in range(9)]

    def put(which, at, grad, rate):
        weight, momentum, average = (ref[at] for ref in sets[which])
        for ref, value in zip(outs[which], nesterov(weight, momentum, average, grad, rate)):
            ref[at] = value

    for j in range(3):
        grad = grads[0, 24 * j:24 * (j + 1)].astype(F32).reshape(HALF, 128)
        put(0, (0, slice(None), slice(128 * j, 128 * (j + 1))), grad, RATE)
    tail = jnp.concatenate(
        [jnp.transpose(jnp.pad(grads[0, 72 + j].astype(F32), ((0, 112), (0, 0)))) for j in range(3)], axis=0
    )
    put(0, (0, slice(None), slice(384, UNITS)), tail[:, 0:16], RATE)

    @pl.when((pl.program_id(0) == 0) & (pl.program_id(1) == 0))
    def small_ones():
        whole = jnp.concatenate([aux[0, 0:AUX], aux[1, 0:AUX]], axis=0).astype(F32).reshape(2 * AUX * 16, 128)
        for k in range(EMB):
            put(1, (k,), whole[FPAD * k:FPAD * k + FIELDS, 0:UDEV], RATE)
        for layer in range(2):
            put(2, (layer,), whole[UNITS * (layer + 1):UNITS * (layer + 2), 0:UDEV], RATE)
        everything = (slice(None), slice(None))
        put(3, everything, small[72:75, 0:UDEV], FAST_RATE)
        put(4, everything, small[75:76, 0:UDEV], RATE)
        put(5, everything, small[76:77, 0:1], RATE)
        put(6, everything, small[0:EMB, 0:EMB], RATE)
        put(7, everything, small[16:16 + FIELDS, 0:REDUCED], FAST_RATE)
        put(8, everything, small[56:56 + REDUCED, 0:FIELDS], FAST_RATE)
        logits_out[...] = logit[0:1, :]
        for k in range(EMB):
            egrad_out[k] = egrad[k, :, :].astype(F32)[0:FIELDS]


def update(grads, small, egrad, logit, sets):
    whole = lambda array: pl.BlockSpec(array.shape, lambda k, c: (0,) * array.ndim)
    rows = pl.BlockSpec((1, HALF, UNITS), lambda k, c: (k, c, 0))
    in_specs = [
        pl.BlockSpec((1, KTILES, 16, 128), lambda k, c: (c, k, 0, 0)),
        pl.BlockSpec((2, KTILES, 16, 128), lambda k, c: (0, ROWS, 0, 0)),
        whole(small), whole(egrad), whole(logit),
    ]
    out_shapes = [jax.ShapeDtypeStruct((1, BATCH), F32), jax.ShapeDtypeStruct((EMB, FIELDS, BATCH), F32)]
    out_specs = [whole(shape) for shape in out_shapes]
    operands = [grads, grads, small, egrad, logit]
    for index, arrays in enumerate(sets):
        for array in arrays:
            spec = rows if index == 0 else whole(array)
            operands.append(array)
            in_specs.append(spec)
            out_specs.append(spec)
            out_shapes.append(jax.ShapeDtypeStruct(array.shape, F32))
    return pl.pallas_call(
        update_kernel,
        grid=(ROWS, 2),
        in_specs=in_specs,
        out_specs=out_specs,
        out_shape=out_shapes,
        compiler_params=pltpu.CompilerParams(vmem_limit_bytes=48 * MIB),
        name="update",
    )(*operands)


def per_device(
    id_lists, id_counts, embed_rows, logit_grad,
    bilinear, bilinear_momentum, bilinear_average,
    squeezer, squeezer_momentum, squeezer_average,
    exciter, exciter_momentum, exciter_average,
    pairwise, pairwise_momentum, pairwise_average,
    fieldwise, fieldwise_momentum, fieldwise_average,
    hidden, hidden_momentum, hidden_average,
    biases, biases_momentum, biases_average,
    readout, readout_momentum, readout_average,
    offset, offset_momentum, offset_average,
):
    emb = pool(id_lists, id_counts, embed_rows)
    grads, small, egrad, logit = step(
        emb, pairwise, fieldwise, hidden, biases, readout, offset, logit_grad, bilinear, squeezer, exciter
    )
    row = lambda *arrays: tuple(array.reshape(1, -1) for array in arrays)
    outs = update(
        grads, small, egrad, logit,
        [
            (pairwise, pairwise_momentum, pairwise_average),
            (fieldwise, fieldwise_momentum, fieldwise_average),
            (hidden, hidden_momentum, hidden_average),
            (biases, biases_momentum, biases_average),
            row(readout, readout_momentum, readout_average),
            row(offset, offset_momentum, offset_average),
            (bilinear, bilinear_momentum, bilinear_average),
            (squeezer, squeezer_momentum, squeezer_average),
            (exciter, exciter_momentum, exciter_average),
        ],
    )
    logits, egrad_full = outs[0].reshape(-1), outs[1]
    pair, field, hid, bias, read, off, bil, squ, exc = (tuple(outs[2 + 3 * i:5 + 3 * i]) for i in range(9))
    flat = lambda arrays: tuple(array.reshape(-1) for array in arrays)
    return (logits, egrad_full) + bil + squ + exc + pair + field + hid + bias + flat(read) + flat(off)


def solution(mesh):
    whole = (P(),) * 3
    rows = (P("mp", None, None),) * 3
    units = (P(None, None, "mp"),) * 3
    vectors = (P(None, "mp"),) * 3
    line = (P("mp"),) * 3
    weights = whole + whole + whole + rows + units + units + vectors + line + whole
    return jax.shard_map(
        per_device,
        mesh=mesh,
        in_specs=(P(None, None, "dp"), P(None, "dp"), P("dp", None), P("dp")) + weights,
        out_specs=(P("dp"), P(None, None, "dp")) + weights,
        check_vma=False,
    )
```

```python
import jax
import jax.numpy as jnp
import numpy as np
from jax import lax
from jax.experimental import pallas as pl
from jax.experimental.pallas import tpu as pltpu
from jax.sharding import PartitionSpec as P

MOMENTUM = 0.9
RATE = 0.01
FAST_RATE = 0.05
DECAY = 0.8
HIGHEST = lax.Precision.HIGHEST
F32 = jnp.float32
LOW = jnp.bfloat16
MESH = pl.DeviceIdType.MESH
MIB = 1024 * 1024

EMB = 10
FIELDS = 39
FPAD = 40
REDUCED = 13
UNITS = 400
ZROWS = 112
UDEV = 100
SLOTS = 8
BATCH = 256
FETCH = 1024
PAIRS = 741
PPAD = 768
HALF = 384
ROWS = 5
TILES = 448
QUART = TILES // 4
KTILES = 75
BLOCK = 80
AUX = 38
SMALL = 80


def dot(left, right, contract, precision=None):
    return lax.dot_general(
        left, right, ((contract[0], contract[1]), ((), ())),
        precision=precision, preferred_element_type=F32,
    )


def nn(left, right, precision=None):
    return dot(left, right, ((1,), (0,)), precision)


def nt(left, right, precision=None):
    return dot(left, right, ((1,), (1,)), precision)


def tn(left, right, precision=None):
    return dot(left, right, ((0,), (0,)), precision)


def in_hbm(arrays):
    return tuple(pltpu.with_memory_space_constraint(array, pltpu.HBM) for array in arrays)


def nesterov(weight, momentum, average, grad, step_rate):
    velocity = MOMENTUM * momentum + grad
    updated = weight - step_rate * (grad + MOMENTUM * velocity)
    smoothed = DECAY * average + (1.0 - DECAY) * updated
    return (velocity, smoothed, updated)


def pool(ids_ref, count_ref, rows_ref, counts, table, out_ref):
    for chunk in range(8):
        part = rows_ref[:, 128 * chunk:128 * (chunk + 1)].astype(F32)
        for k in range(EMB):
            table[k, chunk:chunk + 1, :] = part[k:k + 1, :]
    counts[0:FIELDS, :] = count_ref[...]
    counts[FIELDS:FPAD, :] = jnp.ones((1, BATCH), jnp.int32)
    ids_ref[FIELDS] = jnp.full((SLOTS, BATCH), 8 * FETCH, jnp.int32)
    sublane = lax.broadcasted_iota(jnp.int32, (8, 128), 0)

    def group(g, carry):
        fields = pl.ds(pl.multiple_of(8 * g, 8), 8)
        for h in range(2):
            lanes = slice(128 * h, 128 * (h + 1))
            live = counts[fields, lanes]
            found = [[] for _ in range(EMB)]
            for row in range(8):
                ids = jnp.where(live[row:row + 1, :] > sublane, ids_ref[8 * g + row, :, lanes], 8 * FETCH)
                totals = [None] * EMB
                for slot in range(SLOTS):
                    wide = jnp.broadcast_to(ids[slot:slot + 1, :], (8, 128))
                    lane = wide & 127
                    hit = (wide >> 7) == sublane
                    for k in range(EMB):
                        value = jnp.take_along_axis(table[k], lane, axis=1, mode="promise_in_bounds")
                        value = jnp.where(hit, value, 0.0)
                        totals[k] = value if totals[k] is None else totals[k] + value
                for k in range(EMB):
                    found[k].append(jnp.sum(totals[k], axis=0, keepdims=True))
            divisor = live.astype(F32)
            for k in range(EMB):
                pooled = jnp.concatenate(found[k], axis=0) / divisor
                out_ref[k, fields, lanes] = pooled.astype(LOW).astype(F32)
        return carry

    lax.fori_loop(0, FPAD // 8, group, 0)


def silu_slope(before):
    gate = jax.nn.sigmoid(before)
    return gate * (1.0 + before * (1.0 - gate))


def softplus(value):
    return jnp.maximum(value, 0.0) + jnp.log1p(jnp.exp(-jnp.abs(value)))


def split(value):
    high = value.astype(LOW).astype(F32)
    return jnp.concatenate([high, value - high], axis=0).astype(LOW)


def step_kernel(
    *rest,
):
    hbm, pairs_in, rest = rest[:17], rest[17:20], rest[20:]
    gout_ref, small_ref, egrad_ref, logit_ref, *pairs_out = rest[:7]
    loaded, rest = rest[7:24], rest[24:]
    pair_ref = pairs_out[0]
    (
        ids_ref, count_ref, rows_ref,
        field_ref, hidden_ref, bias_ref, readout_ref, grad_ref, squ_ref, exc_ref,
        first_ref, second_ref, first_t_ref, second_t_ref, place_ref, place_t_ref, bil_ref,
    ) = loaded
    (
    emb_ref, counts, table, w_low, w_turned, left, right, feats, feats_peer, source, scale_s, sq_s, z1_s, z2_s, squ_pad, exc_pad,
    fpad, fplaced, fplaced_t, hid_all, vec_all, hid_full, hid_turned,
    pre_part, rs_in, pre_full, gf, gf_peer,
    acc, rs0, rs1, rs2, rs3, aux, aux_in,
    dsrc, eterm, zsend, zrecv, zsend2, zrecv2, zsend3, zrecv3, smalls, small_in,
    load_sem, pair_sem, hid_send, hid_recv, vec_send, vec_recv, feat_sem, rsz_send, rsz_recv, agz_send, agz_recv,
    gf_sem, aux_sem, red_send, red_recv, own_sem, gat_send, gat_recv, core_send, core_recv,
    zs_send, zs_recv, sm_send, sm_recv,
    ) = rest
    dp = lax.axis_index("dp")
    me = lax.axis_index("mp")
    core = dp % 2
    yy = (dp // 2) % 4
    xx = dp // 8

    def at_dp(x, y, c):
        return (x * 4 + y) * 2 + c

    def low_bit(pos):
        return ((pos + 1) // 2) % 2

    def flip(pos):
        return pos + 1 - 2 * (pos % 2)

    partner = [
        at_dp(flip(xx), yy, core),
        at_dp(xx, flip(yy), core),
        at_dp(3 - xx, yy, core),
        at_dp(xx, 3 - yy, core),
    ]
    bits = [low_bit(xx), low_bit(yy), xx // 2, yy // 2]
    twin = at_dp(xx, yy, 1 - core)
    peers = [(me + off) % 4 for off in (1, 2, 3)]
    stream = me // 2
    columns = (me % 2) * ROWS
    half = ((me + 1) // 2) % 2
    near = flip(me)
    cross = 3 - me

    def remote(src, dst, send, recv, **where):
        return pltpu.make_async_remote_copy(
            src_ref=src, dst_ref=dst, send_sem=send, recv_sem=recv, device_id=where, device_id_type=MESH
        )

    targets = (ids_ref.at[pl.ds(0, FIELDS)],) + tuple(loaded[1:])
    loads = [pltpu.make_async_copy(src, dst, load_sem.at[n]) for n, (src, dst) in enumerate(zip(hbm, targets))]
    for copy in loads:
        copy.start()
    pair_loads = [
        pltpu.make_async_copy(src, dst, pair_sem.at[n]) for n, (src, dst) in enumerate(zip(pairs_in, pairs_out))
    ]
    for copy in pair_loads:
        copy.start()
    barrier = pltpu.get_barrier_semaphore()
    for peer in peers:
        pl.semaphore_signal(barrier, inc=1, device_id={"mp": peer}, device_id_type=MESH)
    for dev in partner + [twin]:
        pl.semaphore_signal(barrier, inc=1, device_id={"dp": dev}, device_id_type=MESH)

    lanes_me = pl.ds(pl.multiple_of(128 * me, 128), 128)
    for copy in loads:
        copy.wait()
    fpad[...] = jnp.zeros_like(fpad)
    for layer in range(2):
        fpad[:, 0:UDEV] = hidden_ref[layer]
        hid_all[layer, :, lanes_me] = fpad[...].astype(LOW)
    fpad[0:8, :] = jnp.zeros((8, 128), F32)
    fpad[0:3, 0:UDEV] = bias_ref[...]
    fpad[3:4, 0:UDEV] = readout_ref[...].astype(LOW).astype(F32)
    vec_all[:, lanes_me] = fpad[0:8, :]
    pl.semaphore_wait(barrier, 8)

    hid_copies = []
    for n, peer in enumerate(peers):
        mine = hid_all.at[:, :, lanes_me]
        hid_copies.append(remote(mine, mine, hid_send.at[n], hid_recv.at[n], mp=peer))
        mine = vec_all.at[:, lanes_me]
        hid_copies.append(remote(mine, mine, vec_send.at[n], vec_recv.at[n], mp=peer))
    for copy in hid_copies:
        copy.start()

    pool(ids_ref, count_ref, rows_ref, counts, table, emb_ref)

    squ_pad[...] = jnp.zeros_like(squ_pad)
    squ_pad[0:REDUCED, 0:FIELDS] = squ_ref[...]
    exc_pad[...] = jnp.zeros_like(exc_pad)
    exc_pad[0:REDUCED, 0:FIELDS] = exc_ref[...]
    squeezer = squ_pad[:, 0:FPAD]
    exciter = exc_pad[:, 0:FPAD]
    emb = emb_ref[...]
    squeezed = jnp.sum(emb, axis=0) * (1.0 / EMB)
    z1 = nn(squeezer, squeezed, HIGHEST)
    excited = z1 * jax.nn.sigmoid(z1)
    z2 = tn(exciter, excited, HIGHEST)
    scales = softplus(z2)
    sq_s[...] = squeezed
    z1_s[...] = z1
    z2_s[...] = z2
    scale_s[...] = scales
    factor = jnp.where(stream == 0, jnp.ones_like(scales), scales)
    for k in range(EMB):
        source[k] = emb_ref[k] * factor

    fpad[...] = jnp.zeros_like(fpad)
    for k in range(EMB):
        fpad[FPAD * k:FPAD * k + FIELDS, 0:UDEV] = field_ref[k]
    field_low = fpad[...].astype(LOW)
    place_own = place_ref[lanes_me, :]
    fplaced[...] = nn(field_low, place_own).astype(LOW)
    fplaced_t[...] = nt(place_t_ref[:, lanes_me], field_low).astype(LOW)
    emb_low = emb.reshape(EMB * FPAD, BATCH).astype(LOW)
    pre = nn(fplaced_t[...], emb_low)
    for k in range(ROWS):
        projected = source[0] * bil_ref[0, columns + k]
        for l in range(1, EMB):
            projected = projected + source[l] * bil_ref[l, columns + k]
        left_k = nn(first_ref[...], split(projected))
        right_k = nn(second_ref[...], split(source[columns + k]))
        left[k] = left_k.astype(LOW)
        right[k] = right_k.astype(LOW)
        feats[k] = (left_k * right_k).astype(LOW)
    feat_copy = remote(
        feats.at[:, pl.ds(pl.multiple_of(HALF * (1 - core), HALF), HALF), :], feats_peer,
        feat_sem.at[0], feat_sem.at[1], dp=twin,
    )
    feat_copy.start()
    pair_loads[0].wait()
    for k in range(ROWS):
        w_low[k, :, 640:PPAD] = jnp.zeros((UNITS, PPAD - 640), LOW)
        w_low[k, :, 0:PAIRS] = pair_ref[k].astype(LOW)
        pre = pre + nn(w_low[k], feats[k])
    pre_part[0:UNITS, :] = pre.astype(LOW)
    pre_part[UNITS:4 * ZROWS, :] = jnp.zeros((4 * ZROWS - UNITS, BATCH), LOW)

    rs_copies = []
    for n, peer in enumerate(peers):
        rows = pl.ds(pl.multiple_of(ZROWS * peer, ZROWS), ZROWS)
        rs_copies.append(remote(pre_part.at[rows], rs_in.at[n], rsz_send.at[n], rsz_recv.at[n], mp=peer))
        rs_copies[n].start()

    for k in range(ROWS):
        w_turned[k] = jnp.transpose(w_low[k])
    for copy in rs_copies:
        copy.wait()
    own_rows = pl.ds(pl.multiple_of(ZROWS * me, ZROWS), ZROWS)
    total = pre_part[own_rows, :].astype(F32)
    for n in range(3):
        total = total + rs_in[n].astype(F32)
    pre_full[own_rows, :] = total.astype(LOW)
    ag_copies = []
    for n, peer in enumerate(peers):
        ag_copies.append(remote(pre_full.at[own_rows], pre_full.at[own_rows], agz_send.at[n], agz_recv.at[n], mp=peer))
        ag_copies[n].start()
    for copy in hid_copies:
        copy.wait()
    for layer in range(2):
        hid_full[layer] = nn(hid_all[layer], place_ref[...]).astype(LOW)
        hid_turned[layer] = nt(place_t_ref[...], hid_all[layer]).astype(LOW)
    vec_rows = nn(vec_all[...], place_ref[...].astype(F32), HIGHEST)
    vec_cols = nt(place_t_ref[...].astype(F32), vec_all[...], HIGHEST)
    for copy in ag_copies:
        copy.wait()

    pre_first = pre_full[0:UNITS, :].astype(F32) + vec_cols[:, 0:1]
    act_first = (pre_first * jax.nn.sigmoid(pre_first)).astype(LOW)
    pre_second = nn(hid_turned[0], act_first) + vec_cols[:, 1:2]
    act_second = (pre_second * jax.nn.sigmoid(pre_second)).astype(LOW)
    pre_third = nn(hid_turned[1], act_second) + vec_cols[:, 2:3]
    act_third = (pre_third * jax.nn.sigmoid(pre_third)).astype(LOW)
    upstream = grad_ref[...].astype(F32)
    logit_ref[...] = nn(vec_rows.astype(LOW), act_third)
    grad_third = ((vec_cols[:, 3:4] * upstream) * silu_slope(pre_third)).astype(LOW)
    grad_second = (nn(hid_full[1], grad_third) * silu_slope(pre_second)).astype(LOW)
    grad_first = (nn(hid_full[0], grad_second) * silu_slope(pre_first)).astype(LOW)
    gf[...] = grad_first
    gf_copy = remote(gf, gf_peer, gf_sem.at[0], gf_sem.at[1], dp=twin)
    gf_copy.start()

    first_mine = nn(place_own, grad_first).astype(LOW)
    second_mine = nn(place_own, grad_second).astype(LOW)
    third_mine = nn(place_own, grad_third).astype(LOW)
    aux[0:25] = nt(emb_low, first_mine).astype(LOW).reshape(25, 16, 128)
    aux[25:50] = nt(act_first, second_mine).astype(LOW).reshape(25, 16, 128)
    aux[50:75] = nt(act_second, third_mine).astype(LOW).reshape(25, 16, 128)
    aux[75:76] = jnp.zeros((1, 16, 128), LOW)
    aux_copy = remote(
        aux.at[pl.ds(AUX * (1 - core), AUX)], aux_in, aux_sem.at[0], aux_sem.at[1], dp=twin
    )
    aux_copy.start()
    ones = jnp.ones((8, BATCH), LOW)
    row_iota = lax.broadcasted_iota(jnp.int32, (8, UNITS), 0)
    vec_grads = jnp.where(row_iota == 0, nt(ones, grad_first), 0.0)
    vec_grads = vec_grads + jnp.where(row_iota == 1, nt(ones, grad_second), 0.0)
    vec_grads = vec_grads + jnp.where(row_iota == 2, nt(ones, grad_third), 0.0)
    upstream_rows = jnp.broadcast_to(upstream, (8, BATCH)).astype(LOW)
    vec_grads = vec_grads + jnp.where(row_iota == 3, nt(upstream_rows, act_third), 0.0)
    vec_grads = vec_grads + jnp.where(row_iota == 4, jnp.sum(upstream), 0.0)
    vec_grads = vec_grads * 0.25
    for j in range(3):
        smalls[0, 48 + 8 * j:56 + 8 * j, :] = vec_grads[:, 128 * j:128 * (j + 1)]
    smalls[0, 72:80, :] = jnp.zeros((8, 128), F32)
    smalls[0, 72:80, 0:16] = vec_grads[:, 384:UNITS]

    feat_copy.wait()
    own_half = pl.ds(pl.multiple_of(HALF * core, HALF), HALF)
    gf_copy.wait()
    for k in range(ROWS):
        grad = (nt(gf[...], feats[k, own_half, :]) + nt(gf_peer[...], feats_peer[k])).astype(LOW)
        tiles = [grad[:, 128 * j:128 * (j + 1)].reshape(25, 16, 128) for j in range(3)]
        acc[KTILES * k:KTILES * (k + 1)] = jnp.stack(tiles, axis=1).reshape(KTILES, 16, 128)
    aux_copy.wait()
    aux_mine = aux[pl.ds(AUX * core, AUX)].astype(F32) + aux_in[...].astype(F32)
    acc[KTILES * ROWS:KTILES * ROWS + AUX] = aux_mine.astype(LOW)
    acc[KTILES * ROWS + AUX:TILES] = jnp.zeros((TILES - KTILES * ROWS - AUX, 16, 128), LOW)

    starts = [QUART * q for q in range(4)]
    boxes = [rs0, rs1, rs2, rs3]

    def reduce_send(t):
        n = QUART >> (t + 1)
        copies = []
        for q in range(4):
            d = (q + t) % 4
            away = starts[q] + (1 - bits[d]) * n
            copies.append(remote(acc.at[pl.ds(away, n)], boxes[t].at[q], red_send.at[t, q], red_recv.at[t, q], dp=partner[d]))
            copies[q].start()
            starts[q] = starts[q] + bits[d] * n
        return copies

    def reduce_add(t, copies):
        n = QUART >> (t + 1)
        for q in range(4):
            copies[q].wait()
            keep = pl.ds(starts[q], n)
            acc[keep] = (acc[keep].astype(F32) + boxes[t][q].astype(F32)).astype(LOW)

    moving = reduce_send(0)

    grad_first = gf[...]
    dprojected = []
    dchosen = []
    for k in range(ROWS):
        dfeat = nn(w_turned[k], grad_first)
        dprojected.append(nn(first_t_ref[...], (dfeat * right[k].astype(F32)).astype(LOW)))
        dchosen.append(nn(second_t_ref[...], (dfeat * left[k].astype(F32)).astype(LOW)))
    reduce_add(0, moving)
    moving = reduce_send(1)
    bil_rows = jnp.zeros((16, 128), F32)
    lane_iota = lax.broadcasted_iota(jnp.int32, (16, 128), 1)
    for k in range(ROWS):
        sums = []
        for l in range(EMB):
            product = source[l] * dprojected[k]
            product = product[:, 0:128] + product[:, 128:256]
            sums.append(jnp.sum(product, axis=0, keepdims=True))
        sums.append(jnp.zeros((6, 128), F32))
        row_sum = jnp.sum(jnp.concatenate(sums, axis=0), axis=1, keepdims=True)
        bil_rows = bil_rows + jnp.where(lane_iota == columns + k, row_sum, 0.0)
    smalls[0, 0:16, :] = bil_rows
    for l in range(EMB):
        total = dprojected[0] * bil_ref[l, columns]
        for k in range(1, ROWS):
            total = total + dprojected[k] * bil_ref[l, columns + k]
        dsrc[l] = total
    for k in range(ROWS):
        dsrc[columns + k] = dsrc[columns + k] + dchosen[k]
    eterm[...] = nn(fplaced[...], grad_first).reshape(EMB, FPAD, BATCH)
    lanes_away = pl.ds(pl.multiple_of(128 * (1 - half), 128), 128)
    lanes_own = pl.ds(pl.multiple_of(128 * half, 128), 128)
    zsend[0] = dsrc[:, :, lanes_away].reshape(EMB * FPAD, 128).astype(LOW)
    zsend[1] = eterm[:, :, lanes_away].reshape(EMB * FPAD, 128).astype(LOW)
    z_copy = remote(zsend, zrecv, zs_send.at[0], zs_recv.at[0], mp=near)
    z_copy.start()
    reduce_add(1, moving)
    moving = reduce_send(2)

    z_copy.wait()
    back = dsrc[:, :, lanes_own] + zrecv[0].astype(F32).reshape(EMB, FPAD, 128)
    term = eterm[:, :, lanes_own] + zrecv[1].astype(F32).reshape(EMB, FPAD, 128)
    emb_half = emb_ref[:, :, lanes_own]
    z1 = z1_s[:, lanes_own]
    z2 = z2_s[:, lanes_own]
    dscale = jnp.sum(back * emb_half, axis=0)
    dz2 = dscale * jax.nn.sigmoid(z2)
    excited = z1 * jax.nn.sigmoid(z1)
    dexciter = nt(excited, dz2, HIGHEST)
    dz1 = nn(exciter, dz2, HIGHEST) * silu_slope(z1)
    dsqueezer = nt(dz1, sq_s[:, lanes_own], HIGHEST)
    dsqueezed = tn(squeezer, dz1, HIGHEST) * (1.0 / EMB)
    weighted = jnp.where(stream == 0, jnp.zeros((1, 1), F32), jnp.ones((1, 1), F32))
    through = back * scale_s[:, lanes_own][None] + dsqueezed[None]
    mine = term + jnp.where(stream == 0, back, through)
    zsend2[...] = mine.reshape(EMB * FPAD, 128).astype(LOW)
    z_copy = remote(zsend2, zrecv2, zs_send.at[1], zs_recv.at[1], mp=cross)
    z_copy.start()
    smalls[0, 16:48, :] = jnp.zeros((32, 128), F32)
    smalls[0, 16:32, 0:FPAD] = dsqueezer * weighted
    smalls[0, 32:48, 0:FPAD] = dexciter * weighted
    reduce_add(2, moving)
    moving = reduce_send(3)

    hops = [("mp", near), ("mp", cross), ("dp", twin)] + [("dp", dev) for dev in partner]

    def small_send(t):
        axis, dev = hops[t]
        copy = remote(smalls.at[t], small_in.at[t], sm_send.at[t], sm_recv.at[t], **{axis: dev})
        copy.start()
        return copy

    def small_add(t, copy):
        copy.wait()
        smalls[t + 1] = smalls[t] + small_in[t]

    small = small_send(0)
    z_copy.wait()
    whole = (zsend2[...].astype(F32) + zrecv2[...].astype(F32)).astype(LOW)
    zsend3[...] = whole
    z_copy = remote(zsend3, zrecv3, zs_send.at[2], zs_recv.at[2], mp=near)
    z_copy.start()
    small_add(0, small)
    small = small_send(1)
    reduce_add(3, moving)

    n = QUART >> 4
    own_copies = []
    core_copies = []

    def pass_on(t, q, src, start, count):
        copy = remote(src, gout_ref.at[core, pl.ds(start, count)], core_send.at[t, q], core_recv.at[t, q], dp=twin)
        copy.start()
        core_copies.append(copy)

    moving = []
    for q in range(4):
        piece = acc.at[pl.ds(starts[q], n)]
        where = gout_ref.at[core, pl.ds(starts[q], n)]
        moving.append(remote(piece, where, gat_send.at[3, q], gat_recv.at[3, q], dp=partner[(q + 3) % 4]))
        moving[q].start()
        own_copies.append(pltpu.make_async_copy(piece, where, own_sem.at[q]))
        own_copies[q].start()
        pass_on(4, q, piece, starts[q], n)
    small_add(1, small)
    small = small_send(2)
    for t in (3, 2, 1, 0):
        n = QUART >> (t + 1)
        later = []
        for q in range(4):
            bit = bits[(q + t) % 4]
            moving[q].wait()
            if t == 3:
                own_copies[q].wait()
            came = starts[q] + (1 - 2 * bit) * n
            pass_on(t, q, gout_ref.at[core, pl.ds(came, n)], came, n)
            starts[q] = starts[q] - bit * n
            if t > 0:
                where = gout_ref.at[core, pl.ds(starts[q], 2 * n)]
                later.append(remote(where, where, gat_send.at[t - 1, q], gat_recv.at[t - 1, q], dp=partner[(q + t - 1) % 4]))
                later[q].start()
        moving = later
        small_add(5 - t, small)
        if t > 0:
            small = small_send(6 - t)
    small = small_send(6)
    z_copy.wait()
    egrad_ref[:, :, lanes_own] = zsend3[...].reshape(EMB, FPAD, 128)
    egrad_ref[:, :, lanes_away] = zrecv3[...].reshape(EMB, FPAD, 128)
    small_add(6, small)
    small_ref[0:48] = smalls[7, 0:48, :]
    vec_grads = jnp.concatenate([smalls[7, 48 + 8 * j:56 + 8 * j, :] for j in range(4)], axis=1)[:, 0:UNITS]
    small_ref[48:56] = nt(vec_grads, place_ref[lanes_me, :].astype(F32), HIGHEST)
    for copy in core_copies + pair_loads[1:]:
        copy.wait()


def step(id_lists, id_counts, embed_rows, pair_set, fieldwise, hidden, biases, readout, logit_grad, bilinear, squeezer, exciter):
    first_index, second_index = np.triu_indices(FIELDS, 1)
    first = np.zeros((PPAD, FPAD), np.float32)
    second = np.zeros((PPAD, FPAD), np.float32)
    first[np.arange(PAIRS), first_index] = 1.0
    second[np.arange(PAIRS), second_index] = 1.0
    place = np.zeros((512, UNITS), np.float32)
    unit = np.arange(UNITS)
    place[128 * (unit // UDEV) + unit % UDEV, unit] = 1.0
    constants = (
        np.concatenate([first, first], axis=1), np.concatenate([second, second], axis=1), first.T, second.T, place, place.T
    )
    constants = [jnp.asarray(value, LOW) for value in constants]
    small_operands = (
        id_lists.transpose(1, 0, 2), id_counts, embed_rows.T,
        fieldwise, hidden, biases, readout.reshape(1, UDEV), logit_grad.reshape(1, BATCH), squeezer.T, exciter,
        *constants, bilinear,
    )
    vmem = pl.BlockSpec(memory_space=pltpu.VMEM)
    hbm = pl.BlockSpec(memory_space=pltpu.HBM)
    anywhere = pl.BlockSpec(memory_space=pl.ANY)
    low = lambda *shape: pltpu.VMEM(shape, LOW)
    full = lambda *shape: pltpu.VMEM(shape, F32)
    dma = lambda *shape: pltpu.SemaphoreType.DMA(shape)
    return pl.pallas_call(
        step_kernel,
        out_shape=(
            jax.ShapeDtypeStruct((2, TILES, 16, 128), LOW),
            jax.ShapeDtypeStruct((56, 128), F32),
            jax.ShapeDtypeStruct((EMB, FPAD, BATCH), LOW),
            jax.ShapeDtypeStruct((8, BATCH), F32),
        ) + (pltpu.VMEM(pair_set[0].shape, F32),) * 3,
        in_specs=[hbm] * 20,
        out_specs=(anywhere, vmem, vmem, vmem) + (vmem,) * 3,
        scratch_shapes=[
            pltpu.VMEM((FPAD, SLOTS, BATCH), jnp.int32),
            *(pltpu.VMEM(array.shape, array.dtype) for array in small_operands[1:-1]),
            pltpu.SMEM((EMB, EMB), F32),
            full(EMB, FPAD, BATCH), pltpu.VMEM((FPAD, BATCH), jnp.int32), full(EMB, 8, 128),
            low(ROWS, UNITS, PPAD), low(ROWS, PPAD, UNITS),
            low(ROWS, PPAD, BATCH), low(ROWS, PPAD, BATCH), low(ROWS, PPAD, BATCH), low(ROWS, HALF, BATCH),
            full(EMB, FPAD, BATCH), full(FPAD, BATCH), full(FPAD, BATCH), full(16, BATCH), full(FPAD, BATCH),
            full(16, 128), full(16, 128), full(EMB * FPAD, 128), low(EMB * FPAD, UNITS), low(UNITS, EMB * FPAD),
            low(2, UNITS, 512), full(8, 512), low(2, UNITS, UNITS), low(2, UNITS, UNITS),
            low(4 * ZROWS, BATCH), low(3, ZROWS, BATCH), low(4 * ZROWS, BATCH), low(UNITS, BATCH), low(UNITS, BATCH),
            low(TILES, 16, 128), low(4, QUART // 2, 16, 128), low(4, QUART // 4, 16, 128),
            low(4, QUART // 8, 16, 128), low(4, QUART // 16, 16, 128), low(2 * AUX, 16, 128), low(AUX, 16, 128),
            full(EMB, FPAD, BATCH), full(EMB, FPAD, BATCH),
            low(2, EMB * FPAD, 128), low(2, EMB * FPAD, 128), low(EMB * FPAD, 128), low(EMB * FPAD, 128),
            low(EMB * FPAD, 128), low(EMB * FPAD, 128), full(8, SMALL, 128), full(7, SMALL, 128),
            dma(17), dma(3), dma(3), dma(3), dma(3), dma(3), dma(2), dma(3), dma(3), dma(3), dma(3),
            dma(2), dma(2), dma(4, 4), dma(4, 4), dma(4), dma(4, 4), dma(4, 4), dma(5, 4), dma(5, 4),
            dma(3), dma(3), dma(7), dma(7),
        ],
        compiler_params=pltpu.CompilerParams(
            collective_id=0, has_side_effects=True, vmem_limit_bytes=30 * MIB
        ),
        name="step",
    )(*in_hbm(small_operands), *in_hbm(pair_set))


def update_kernel(grads, small, egrad, logit, weight, momentum, average, *refs):
    inputs, refs = refs[:24], refs[24:]
    logits_out, egrad_out = refs[:2]
    pair_outs, outputs, refs = refs[2:5], refs[5:29], refs[29:]
    held, refs = refs[:24], refs[24:]
    logits_held, egrad_held, pair_held, in_sem, out_sem, pair_sem = refs

    loads = [pltpu.make_async_copy(src, dst, in_sem.at[n]) for n, (src, dst) in enumerate(zip(inputs, held))]
    for copy in loads:
        copy.start()

    stores = []
    for k in range(ROWS):
        slot = k % 2
        if k >= 2:
            for copy in stores[3 * (k - 2):3 * (k - 1)]:
                copy.wait()
        for c in range(2):
            for j in range(3):
                first = HALF * c + 128 * j
                last = min(first + 128, PAIRS)
                tiles = [grads[c, KTILES * k + 3 * r + j] for r in range(UNITS // 16)]
                grad = jnp.concatenate(tiles, axis=0).astype(F32)[:, 0:last - first]
                at = (k, slice(None), slice(first, last))
                values = nesterov(weight[at], momentum[at], average[at], grad, RATE)
                for n, value in enumerate(values):
                    pair_held[slot, n, :, first:last] = value
        for n in range(3):
            stores.append(pltpu.make_async_copy(pair_held.at[slot, n], pair_outs[n].at[k], pair_sem.at[slot, n]))
            stores[-1].start()

    for copy in loads:
        copy.wait()

    def put(which, at, grad, rate):
        weight, momentum, average = held[3 * which:3 * which + 3]
        values = nesterov(weight[at], momentum[at], average[at], grad, rate)
        for ref, value in zip((weight, momentum, average), values):
            ref[at] = value

    whole = jnp.concatenate([grads[0, KTILES * ROWS:KTILES * ROWS + AUX], grads[1, KTILES * ROWS:KTILES * ROWS + AUX]], axis=0)
    whole = whole.astype(F32).reshape(2 * AUX * 16, 128)
    for k in range(EMB):
        put(0, (k,), whole[FPAD * k:FPAD * k + FIELDS, 0:UDEV], RATE)
    for layer in range(2):
        put(1, (layer,), whole[UNITS * (layer + 1):UNITS * (layer + 2), 0:UDEV], RATE)
    everything = (slice(None), slice(None))
    offset_weight = held[12][...]
    put(2, everything, small[48:51, 0:UDEV], FAST_RATE)
    put(3, everything, small[51:52, 0:UDEV], RATE)
    put(4, everything, small[52:53, 0:1], RATE)
    put(5, everything, small[0:EMB, 0:EMB], RATE)
    put(6, everything, small[16:16 + REDUCED, 0:FIELDS], FAST_RATE)
    put(7, everything, small[32:32 + REDUCED, 0:FIELDS], FAST_RATE)
    logits_held[...] = logit[3:4, :] + offset_weight
    for k in range(EMB):
        egrad_held[k] = egrad[k, :, :].astype(F32)[0:FIELDS]
    lasts = zip((logits_held, egrad_held) + tuple(held), (logits_out, egrad_out) + tuple(outputs))
    lasts = [pltpu.make_async_copy(src, dst, out_sem.at[n]) for n, (src, dst) in enumerate(lasts)]
    for copy in lasts:
        copy.start()
    for copy in lasts + stores[3 * (ROWS - 2):]:
        copy.wait()


def update(grads, small, egrad, logit, sets):
    vmem = pl.BlockSpec(memory_space=pltpu.VMEM)
    hbm = pl.BlockSpec(memory_space=pltpu.HBM)
    pair, others = sets[0], [array for arrays in sets[1:] for array in arrays]
    shapes = [(1, BATCH), (EMB, FIELDS, BATCH)] + [array.shape for array in pair] + [array.shape for array in others]
    return pl.pallas_call(
        update_kernel,
        in_specs=[vmem] * 7 + [hbm] * 24,
        out_specs=[hbm] * 29,
        out_shape=[jax.ShapeDtypeStruct(shape, F32) for shape in shapes],
        scratch_shapes=[
            *(pltpu.VMEM(array.shape, F32) for array in others),
            pltpu.VMEM((1, BATCH), F32), pltpu.VMEM((EMB, FIELDS, BATCH), F32),
            pltpu.VMEM((2, 3, UNITS, PAIRS), F32),
            pltpu.SemaphoreType.DMA((24,)), pltpu.SemaphoreType.DMA((26,)), pltpu.SemaphoreType.DMA((2, 3)),
        ],
        compiler_params=pltpu.CompilerParams(vmem_limit_bytes=16 * MIB),
        name="update",
    )(grads, small, egrad, logit, *pair, *in_hbm(others[:12]), *others[12:15], *in_hbm(others[15:]))


def per_device(
    id_lists, id_counts, embed_rows, logit_grad,
    bilinear, bilinear_momentum, bilinear_average,
    squeezer, squeezer_momentum, squeezer_average,
    exciter, exciter_momentum, exciter_average,
    pairwise, pairwise_momentum, pairwise_average,
    fieldwise, fieldwise_momentum, fieldwise_average,
    hidden, hidden_momentum, hidden_average,
    biases, biases_momentum, biases_average,
    readout, readout_momentum, readout_average,
    offset, offset_momentum, offset_average,
):
    turn = lambda *arrays: tuple(array.swapaxes(-1, -2) for array in arrays)
    pair_set = turn(pairwise, pairwise_momentum, pairwise_average)
    grads, small, egrad, logit, *held = step(
        id_lists, id_counts, embed_rows, pair_set, fieldwise, hidden, biases, readout, logit_grad, bilinear, squeezer, exciter
    )
    row = lambda *arrays: tuple(array.reshape(1, -1) for array in arrays)
    outs = update(
        grads, small, egrad, logit,
        [
            held,
            (fieldwise, fieldwise_momentum, fieldwise_average),
            (hidden, hidden_momentum, hidden_average),
            (biases, biases_momentum, biases_average),
            row(readout, readout_momentum, readout_average),
            row(offset, offset_momentum, offset_average),
            (bilinear, bilinear_momentum, bilinear_average),
            turn(squeezer, squeezer_momentum, squeezer_average),
            (exciter, exciter_momentum, exciter_average),
        ],
    )
    logits, egrad_full = outs[0].reshape(-1), outs[1]
    pair, field, hid, bias, read, off, bil, squ, exc = (tuple(outs[2 + 3 * i:5 + 3 * i]) for i in range(9))
    flat = lambda arrays: tuple(array.reshape(-1) for array in arrays)
    return (logits, egrad_full) + bil + turn(*squ) + exc + turn(*pair) + field + hid + bias + flat(read) + flat(off)


def solution(mesh):
    whole = (P(),) * 3
    rows = (P("mp", None, None),) * 3
    units = (P(None, None, "mp"),) * 3
    vectors = (P(None, "mp"),) * 3
    line = (P("mp"),) * 3
    weights = whole + whole + whole + rows + units + units + vectors + line + whole
    return jax.shard_map(
        per_device,
        mesh=mesh,
        in_specs=(P(None, None, "dp"), P(None, "dp"), P("dp", None), P("dp")) + weights,
        out_specs=(P("dp"), P(None, None, "dp")) + weights,
        check_vma=False,
    )
```

```python
import jax
import jax.numpy as jnp
import numpy as np
from jax import lax
from jax.experimental import pallas as pl
from jax.experimental.pallas import tpu as pltpu
from jax.sharding import PartitionSpec as P

MOMENTUM = 0.9
RATE = 0.01
FAST_RATE = 0.05
DECAY = 0.8
HIGHEST = lax.Precision.HIGHEST
F32 = jnp.float32
LOW = jnp.bfloat16
MESH = pl.DeviceIdType.MESH
MIB = 1024 * 1024

EMB = 10
FIELDS = 39
FPAD = 40
REDUCED = 13
UNITS = 400
ZROWS = 112
UDEV = 100
SLOTS = 8
BATCH = 256
FETCH = 1024
PAIRS = 741
PPAD = 768
HALF = 384
ROWS = 5
TILES = 416
HALVES = TILES // 2
CHUNKS = (112, 96)
KTILES = 75
AUX = 38
SMALL = 48
STEPS = 4095


def dot(left, right, contract, precision=None):
    return lax.dot_general(
        left, right, ((contract[0], contract[1]), ((), ())),
        precision=precision, preferred_element_type=F32,
    )


def nn(left, right, precision=None):
    return dot(left, right, ((1,), (0,)), precision)


def nt(left, right, precision=None):
    return dot(left, right, ((1,), (1,)), precision)


def tn(left, right, precision=None):
    return dot(left, right, ((0,), (0,)), precision)


def in_hbm(arrays):
    return tuple(pltpu.with_memory_space_constraint(array, pltpu.HBM) for array in arrays)


def nesterov(weight, momentum, average, grad, step_rate):
    velocity = MOMENTUM * momentum + grad
    updated = weight - step_rate * (grad + MOMENTUM * velocity)
    smoothed = DECAY * average + (1.0 - DECAY) * updated
    return (velocity, smoothed, updated)


def pool(ids_ref, count_ref, rows_ref, counts, table, out_ref):
    rows = rows_ref[...].astype(F32)
    largest = jnp.maximum(jnp.max(jnp.abs(rows), keepdims=True), 1e-30)
    fixed = jnp.round(rows * (STEPS / largest)).astype(jnp.int32) + (STEPS + 1)
    for chunk in range(8):
        part = fixed[:, 128 * chunk:128 * (chunk + 1)]
        for k in range(EMB // 2):
            table[k, chunk:chunk + 1, :] = part[2 * k:2 * k + 1, :] * 65536 + part[2 * k + 1:2 * k + 2, :]
    counts[0:FIELDS, :] = count_ref[...]
    counts[FIELDS:FPAD, :] = jnp.ones((1, BATCH), jnp.int32)
    ids_ref[FIELDS] = jnp.full((SLOTS, BATCH), 8 * FETCH, jnp.int32)
    sublane = lax.broadcasted_iota(jnp.int32, (8, 128), 0)
    unit = largest * (1.0 / STEPS)

    def group(g, carry):
        fields = pl.ds(pl.multiple_of(8 * g, 8), 8)
        for h in range(2):
            lanes = slice(128 * h, 128 * (h + 1))
            live = counts[fields, lanes]
            found = [[] for _ in range(EMB // 2)]
            for row in range(8):
                ids = jnp.where(live[row:row + 1, :] > sublane, ids_ref[8 * g + row, :, lanes], 8 * FETCH)
                totals = [None] * (EMB // 2)
                for slot in range(SLOTS):
                    wide = jnp.broadcast_to(ids[slot:slot + 1, :], (8, 128))
                    lane = wide & 127
                    hit = (wide >> 7) == sublane
                    for k in range(EMB // 2):
                        value = jnp.take_along_axis(table[k], lane, axis=1, mode="promise_in_bounds")
                        value = jnp.where(hit, value, 0)
                        totals[k] = value if totals[k] is None else totals[k] + value
                for k in range(EMB // 2):
                    found[k].append(jnp.sum(totals[k], axis=0, keepdims=True))
            factor = unit / live.astype(F32)
            for k in range(EMB // 2):
                both = jnp.concatenate(found[k], axis=0)
                for part, word in enumerate(((both >> 16) & 65535, both & 65535)):
                    total = (word - (STEPS + 1) * live).astype(F32)
                    out_ref[2 * k + part, fields, lanes] = (total * factor).astype(LOW).astype(F32)
        return carry

    lax.fori_loop(0, FPAD // 8, group, 0)
    out_ref[:, FPAD - 8:FPAD, :] = jnp.where(
        lax.broadcasted_iota(jnp.int32, (EMB, 8, BATCH), 1) == 7, 0.0, out_ref[:, FPAD - 8:FPAD, :]
    )


def gate_of(before):
    return 0.5 + 0.5 * jnp.tanh(0.5 * before)


def silu_slope(before, gate):
    return gate * (1.0 + before * (1.0 - gate))


def softplus(value):
    return jnp.maximum(value, 0.0) + jnp.log1p(jnp.exp(-jnp.abs(value)))


def split(value):
    high = value.astype(LOW).astype(F32)
    return jnp.concatenate([high, value - high], axis=0).astype(LOW)


def step_kernel(*refs):
    hbm, pairs_in, refs = refs[:20], refs[20:23], refs[23:]
    gout_ref, small_ref, egrad_ref, logit_ref, *pairs_out = refs[:7]
    loaded, refs = refs[7:27], refs[27:]
    pair_ref = pairs_out[0]
    (
        hidden_ref, ids_ref, count_ref, rows_ref,
        field_ref, bias_ref, readout_ref, grad_ref, squ_ref, exc_ref,
        first_ref, second_ref, first_t_ref, second_t_ref, place_ref, place_t_ref, same_ref, rows_of_ref, cols_of_ref, bil_ref,
    ) = loaded
    (
        emb_ref, counts, table, w_low, w_turned, left, right, feats, feats_peer, source, scale_s, sq_s, z1_s, z2_s,
        squ_pad, exc_pad, fpad, fplaced, fplaced_t, hid_all, vec_all, hid_full, hid_turned,
        pre_part, rs_in, pre_full, gf, gf_peer,
        acc, box1, box2, aux, aux_in,
        dsrc, eterm, zsend, zrecv, zsend2, zrecv2, zsend3, zrecv3, small_z, small_x, small_y, small_c,
        load_sem, pair_sem, hid_send, hid_recv, vec_send, vec_recv, twin_sem, feat_sem,
        rsz_send, rsz_recv, agz_send, agz_recv,
        gf_sem, aux_sem, red_send, red_recv, own_sem, gat_send, gat_recv, core_send, core_recv,
        zs_send, zs_recv, smz_send, smz_recv, smx_send, smx_recv, smy_send, smy_recv, smc_sem,
    ) = refs
    dp = lax.axis_index("dp")
    me = lax.axis_index("mp")
    core = dp % 2
    yy = (dp // 2) % 4
    xx = dp // 8

    def at_dp(x, y, c):
        return (x * 4 + y) * 2 + c

    rings = (
        [((xx + off) % 4, at_dp((xx + off) % 4, yy, core)) for off in (1, 3, 2)],
        [((yy + off) % 4, at_dp(xx, (yy + off) % 4, core)) for off in (1, 3, 2)],
    )
    places = (xx, yy)
    twin = at_dp(xx, yy, 1 - core)
    peers = [(me + off) % 4 for off in (1, 3, 2)]
    stream = me // 2
    columns = (me % 2) * ROWS
    half = ((me + 1) // 2) % 2
    near = me + 1 - 2 * (me % 2)
    cross = 3 - me

    def remote(src, dst, send, recv, **where):
        return pltpu.make_async_remote_copy(
            src_ref=src, dst_ref=dst, send_sem=send, recv_sem=recv, device_id=where, device_id_type=MESH
        )

    targets = loaded[:1] + (ids_ref.at[pl.ds(0, FIELDS)],) + loaded[2:]
    loads = [pltpu.make_async_copy(src, dst, load_sem.at[n]) for n, (src, dst) in enumerate(zip(hbm, targets))]
    for copy in loads:
        copy.start()
    pair_loads = [
        pltpu.make_async_copy(src, dst, pair_sem.at[n]) for n, (src, dst) in enumerate(zip(pairs_in, pairs_out))
    ]
    for copy in pair_loads:
        copy.start()
    barrier = pltpu.get_barrier_semaphore()
    for peer in peers:
        pl.semaphore_signal(barrier, inc=1, device_id={"mp": peer}, device_id_type=MESH)
    for dev in [dev for ring in rings for _, dev in ring] + [twin]:
        pl.semaphore_signal(barrier, inc=1, device_id={"dp": dev}, device_id_type=MESH)

    lanes_me = pl.ds(pl.multiple_of(128 * me, 128), 128)
    fpad[...] = jnp.zeros_like(fpad)
    loads[0].wait()
    fpad[:, 0:UDEV] = hidden_ref[core]
    hid_all[core, :, lanes_me] = fpad[...].astype(LOW)
    for copy in loads[1:]:
        copy.wait()
    fpad[0:8, :] = jnp.zeros((8, 128), F32)
    fpad[0:3, 0:UDEV] = bias_ref[...]
    fpad[3:4, 0:UDEV] = readout_ref[...].astype(LOW).astype(F32)
    vec_all[:, lanes_me] = fpad[0:8, :]
    pl.semaphore_wait(barrier, 10)

    hid_copies = []
    for n, peer in enumerate(peers):
        mine = hid_all.at[core, :, lanes_me]
        hid_copies.append(remote(mine, mine, hid_send.at[n], hid_recv.at[n], mp=peer))
        mine = vec_all.at[:, lanes_me]
        hid_copies.append(remote(mine, mine, vec_send.at[n], vec_recv.at[n], mp=peer))
    for copy in hid_copies:
        copy.start()

    pool(ids_ref, count_ref, rows_ref, counts, table, emb_ref)

    squ_pad[...] = jnp.zeros_like(squ_pad)
    squ_pad[0:REDUCED, 0:FIELDS] = squ_ref[...]
    exc_pad[...] = jnp.zeros_like(exc_pad)
    exc_pad[0:REDUCED, 0:FIELDS] = exc_ref[...]
    squeezer = squ_pad[:, 0:FPAD]
    exciter = exc_pad[:, 0:FPAD]
    emb = emb_ref[...]
    squeezed = jnp.sum(emb, axis=0) * (1.0 / EMB)
    z1 = nn(squeezer, squeezed, HIGHEST)
    z2 = tn(exciter, z1 * gate_of(z1), HIGHEST)
    scales = softplus(z2)
    sq_s[...] = squeezed
    z1_s[...] = z1
    z2_s[...] = z2
    scale_s[...] = scales
    factor = jnp.where(stream == 0, jnp.ones_like(scales), scales)
    for k in range(EMB):
        source[k] = emb_ref[k] * factor

    for k in range(ROWS):
        projected = source[0] * bil_ref[0, columns + k]
        for l in range(1, EMB):
            projected = projected + source[l] * bil_ref[l, columns + k]
        left_k = nn(first_ref[...], split(projected))
        right_k = nn(second_ref[...], split(source[columns + k]))
        left[k] = left_k.astype(LOW)
        right[k] = right_k.astype(LOW)
        feats[k] = (left_k * right_k).astype(LOW)
    feat_copy = remote(
        feats.at[:, pl.ds(pl.multiple_of(HALF * (1 - core), HALF), HALF), :], feats_peer,
        feat_sem.at[0], feat_sem.at[1], dp=twin,
    )
    feat_copy.start()
    fpad[0:8, :] = jnp.zeros((8, 128), F32)
    for k in range(EMB):
        fpad[FPAD * k:FPAD * k + FIELDS, 0:UDEV] = field_ref[k]
        fpad[FPAD * k + FIELDS:FPAD * (k + 1), :] = jnp.zeros((1, 128), F32)
    field_low = fpad[...].astype(LOW)
    place_own = place_ref[lanes_me, :]
    fplaced_t[...] = nt(place_t_ref[:, lanes_me], field_low).astype(LOW)
    emb_low = emb.reshape(EMB * FPAD, BATCH).astype(LOW)
    pre = nn(fplaced_t[...], emb_low)
    pair_loads[0].wait()
    for k in range(ROWS):
        w_low[k, :, 640:PPAD] = jnp.zeros((UNITS, PPAD - 640), LOW)
        w_low[k, :, 0:PAIRS] = pair_ref[k].astype(LOW)
        pre = pre + nn(w_low[k], feats[k])
    pre_part[0:UNITS, :] = pre.astype(LOW)
    pre_part[UNITS:4 * ZROWS, :] = jnp.zeros((4 * ZROWS - UNITS, BATCH), LOW)

    rs_copies = []
    for n, peer in enumerate(peers):
        rows = pl.ds(pl.multiple_of(ZROWS * peer, ZROWS), ZROWS)
        rs_copies.append(remote(pre_part.at[rows], rs_in.at[n], rsz_send.at[n], rsz_recv.at[n], mp=peer))
        rs_copies[n].start()
    for copy in hid_copies:
        copy.wait()
    layer = hid_all.at[core]
    hid_twin = remote(layer, layer, twin_sem.at[0], twin_sem.at[1], dp=twin)
    hid_twin.start()
    fplaced[...] = nn(field_low, place_own).astype(LOW)
    for k in range(ROWS):
        w_turned[k] = jnp.transpose(w_low[k])
    for copy in rs_copies:
        copy.wait()
    own_rows = pl.ds(pl.multiple_of(ZROWS * me, ZROWS), ZROWS)
    total = pre_part[own_rows, :].astype(F32)
    for n in range(3):
        total = total + rs_in[n].astype(F32)
    pre_full[own_rows, :] = total.astype(LOW)
    ag_copies = []
    for n, peer in enumerate(peers):
        ag_copies.append(remote(pre_full.at[own_rows], pre_full.at[own_rows], agz_send.at[n], agz_recv.at[n], mp=peer))
        ag_copies[n].start()

    hid_twin.wait()
    for layer in range(2):
        hid_full[layer] = nn(hid_all[layer], place_ref[...]).astype(LOW)
        hid_turned[layer] = nt(place_t_ref[...], hid_all[layer]).astype(LOW)
    vec_rows = nn(vec_all[...], place_ref[...].astype(F32), HIGHEST)
    vec_cols = nt(place_t_ref[...].astype(F32), vec_all[...], HIGHEST)
    for copy in ag_copies:
        copy.wait()

    pre_first = pre_full[0:UNITS, :].astype(F32) + vec_cols[:, 0:1]
    gate_first = gate_of(pre_first)
    act_first = (pre_first * gate_first).astype(LOW)
    pre_second = nn(hid_turned[0], act_first) + vec_cols[:, 1:2]
    gate_second = gate_of(pre_second)
    act_second = (pre_second * gate_second).astype(LOW)
    pre_third = nn(hid_turned[1], act_second) + vec_cols[:, 2:3]
    gate_third = gate_of(pre_third)
    act_third = (pre_third * gate_third).astype(LOW)
    upstream = grad_ref[...].astype(F32)
    grad_third = ((vec_cols[:, 3:4] * upstream) * silu_slope(pre_third, gate_third)).astype(LOW)
    grad_second = (nn(hid_full[1], grad_third) * silu_slope(pre_second, gate_second)).astype(LOW)
    grad_first = (nn(hid_full[0], grad_second) * silu_slope(pre_first, gate_first)).astype(LOW)
    gf[...] = grad_first
    gf_copy = remote(gf, gf_peer, gf_sem.at[0], gf_sem.at[1], dp=twin)
    gf_copy.start()

    first_mine = nn(place_own, grad_first).astype(LOW)
    second_mine = nn(place_own, grad_second).astype(LOW)
    third_mine = nn(place_own, grad_third).astype(LOW)
    act_mine = nn(place_own, act_third).astype(LOW)
    aux[0:25] = nt(emb_low, first_mine).astype(LOW).reshape(25, 16, 128)
    aux[25:50] = nt(act_first, second_mine).astype(LOW).reshape(25, 16, 128)
    aux[50:75] = nt(act_second, third_mine).astype(LOW).reshape(25, 16, 128)
    ones = jnp.ones((16, BATCH), LOW)
    upstream_rows = jnp.broadcast_to(upstream, (16, BATCH)).astype(LOW)
    row_iota = lax.broadcasted_iota(jnp.int32, (16, 128), 0)
    vec_grads = jnp.where(row_iota == 0, nt(ones, first_mine), 0.0)
    vec_grads = vec_grads + jnp.where(row_iota == 1, nt(ones, second_mine), 0.0)
    vec_grads = vec_grads + jnp.where(row_iota == 2, nt(ones, third_mine), 0.0)
    vec_grads = vec_grads + jnp.where(row_iota == 3, nt(upstream_rows, act_mine), 0.0)
    aux[75] = vec_grads.astype(LOW)
    aux_copy = remote(
        aux.at[pl.ds(AUX * (1 - core), AUX)], aux_in, aux_sem.at[0], aux_sem.at[1], dp=twin
    )
    aux_copy.start()

    feat_copy.wait()
    own_half = pl.ds(pl.multiple_of(HALF * core, HALF), HALF)
    gf_copy.wait()
    for k in range(ROWS):
        grad = (nt(gf[...], feats[k, own_half, :]) + nt(gf_peer[...], feats_peer[k])).astype(LOW)
        tiles = [grad[:, 128 * j:128 * (j + 1)].reshape(25, 16, 128) for j in range(3)]
        acc[KTILES * k:KTILES * (k + 1)] = jnp.stack(tiles, axis=1).reshape(KTILES, 16, 128)
    acc[KTILES * ROWS + AUX:TILES] = jnp.zeros((TILES - KTILES * ROWS - AUX, 16, 128), LOW)
    aux_copy.wait()
    aux_mine = aux[pl.ds(AUX * core, AUX)].astype(F32) + aux_in[...].astype(F32)
    acc[KTILES * ROWS:KTILES * ROWS + AUX] = aux_mine.astype(LOW)

    offsets = (0, CHUNKS[0])
    starts = [[HALVES * h + offsets[c] for c in range(2)] for h in range(2)]

    def size_of(t, c):
        return CHUNKS[c] // (4, 16)[t]

    def box_of(t, h, n, c):
        return (box1, box2)[t].at[h, n, pl.ds(offsets[c] // (4, 16)[t], size_of(t, c))]

    def reduce_send(t, c):
        size = size_of(t, c)
        copies = []
        for n in range(3):
            for h in range(2):
                place, dev = rings[(h + t) % 2][n]
                src = acc.at[pl.ds(starts[h][c] + place * size, size)]
                copies.append(
                    remote(src, box_of(t, h, n, c), red_send.at[t, h, c, n], red_recv.at[t, h, c, n], dp=dev)
                )
                copies[-1].start()
        for h in range(2):
            starts[h][c] = starts[h][c] + places[(h + t) % 2] * size
        return copies

    def reduce_add(t, c, copies):
        for copy in copies:
            copy.wait()
        for h in range(2):
            keep = pl.ds(starts[h][c], size_of(t, c))
            total = acc[keep].astype(F32)
            for n in range(3):
                total = total + box_of(t, h, n, c)[...].astype(F32)
            acc[keep] = total.astype(LOW)

    own_copies = []
    core_copies = []

    def pass_on(h, c, slot, start, count):
        where = gout_ref.at[core, pl.ds(start, count)]
        copy = remote(where, where, core_send.at[h, c, slot], core_recv.at[h, c, slot], dp=twin)
        copy.start()
        core_copies.append(copy)

    def gather_send(t, c):
        size = size_of(t, c)
        copies = []
        for n in range(3):
            for h in range(2):
                _, dev = rings[(h + t) % 2][n]
                where = gout_ref.at[core, pl.ds(starts[h][c], size)]
                src = acc.at[pl.ds(starts[h][c], size)] if t == 1 else where
                copy = remote(src, where, gat_send.at[t, h, c, n], gat_recv.at[t, h, c, n], dp=dev)
                copy.start()
                sender = rings[(h + t) % 2][(1, 0, 2)[n]][0]
                came = starts[h][c] + (sender - places[(h + t) % 2]) * size
                copies.append((copy, h, n, came))
        for h in range(2):
            if t == 1:
                where = pl.ds(starts[h][c], size)
                own = pltpu.make_async_copy(acc.at[where], gout_ref.at[core, where], own_sem.at[h, c])
                own.start()
                own_copies.append(own)
            starts[h][c] = starts[h][c] - places[(h + t) % 2] * size
        return copies

    def gather_wide(c, copies):
        for copy, _, _, _ in copies:
            copy.wait()
        for own in own_copies[2 * c:2 * c + 2]:
            own.wait()
        wide = gather_send(0, c)
        for h in range(2):
            pass_on(h, c, 3, starts[h][c] + places[h] * size_of(0, c), size_of(0, c))
        return wide

    def gather_end(c, copies):
        for copy, h, n, came in copies:
            copy.wait()
            pass_on(h, c, n, came, size_of(0, c))

    moving = [reduce_send(0, c) for c in range(2)]

    dprojected = []
    dchosen = []
    for k in range(ROWS):
        dfeat = nn(w_turned[k], gf[...])
        dprojected.append(nn(first_t_ref[...], (dfeat * right[k].astype(F32)).astype(LOW)))
        dchosen.append(nn(second_t_ref[...], (dfeat * left[k].astype(F32)).astype(LOW)))
    for l in range(EMB):
        total = dprojected[0] * bil_ref[l, columns]
        for k in range(1, ROWS):
            total = total + dprojected[k] * bil_ref[l, columns + k]
        dsrc[l] = total
    for k in range(ROWS):
        dsrc[columns + k] = dsrc[columns + k] + dchosen[k]
    eterm[...] = nn(fplaced[...], gf[...]).reshape(EMB, FPAD, BATCH)
    lanes_away = pl.ds(pl.multiple_of(128 * (1 - half), 128), 128)
    lanes_own = pl.ds(pl.multiple_of(128 * half, 128), 128)
    zsend[0] = dsrc[:, :, lanes_away].reshape(EMB * FPAD, 128).astype(LOW)
    zsend[1] = eterm[:, :, lanes_away].reshape(EMB * FPAD, 128).astype(LOW)
    z_copies = [remote(zsend.at[n], zrecv.at[n], zs_send.at[n], zs_recv.at[n], mp=near) for n in range(2)]
    for copy in z_copies:
        copy.start()
    products = nt(
        source[...].reshape(EMB * FPAD, BATCH).astype(LOW), jnp.concatenate(dprojected, axis=0).astype(LOW)
    )
    products = products * same_ref[...].astype(F32)
    bil_rows = nn(nn(rows_of_ref[...].astype(F32), products, HIGHEST), cols_of_ref[me % 2].astype(F32), HIGHEST)
    bil_rows = jnp.where(row_iota == 15, jnp.sum(upstream) * 0.25, bil_rows)
    reduce_add(0, 0, moving[0])
    moving[0] = reduce_send(1, 0)

    z_copies[0].wait()
    back = dsrc[:, :, lanes_own] + zrecv[0].astype(F32).reshape(EMB, FPAD, 128)
    emb_half = emb_ref[:, :, lanes_own]
    z1 = z1_s[:, lanes_own]
    z2 = z2_s[:, lanes_own]
    dscale = jnp.sum(back * emb_half, axis=0)
    dz2 = dscale * gate_of(z2)
    gate = gate_of(z1)
    dexciter = nt(z1 * gate, dz2, HIGHEST)
    dz1 = nn(exciter, dz2, HIGHEST) * silu_slope(z1, gate)
    dsqueezer = nt(dz1, sq_s[:, lanes_own], HIGHEST)
    weighted = jnp.where(stream == 0, jnp.zeros((1, 1), F32), jnp.ones((1, 1), F32))

    small_z[me, 0:16, :] = bil_rows
    small_z[me, 16:SMALL, :] = jnp.zeros((32, 128), F32)
    small_z[me, 16:32, 0:FPAD] = dsqueezer * weighted
    small_z[me, 32:48, 0:FPAD] = dexciter * weighted
    small = []
    for n, peer in enumerate(peers):
        small.append(remote(small_z.at[me], small_z.at[me], smz_send.at[n], smz_recv.at[n], mp=peer))
        small[n].start()
    dsqueezed = tn(squeezer, dz1, HIGHEST) * (1.0 / EMB)
    through = back * scale_s[:, lanes_own][None] + dsqueezed[None]
    z_copies[1].wait()
    term = eterm[:, :, lanes_own] + zrecv[1].astype(F32).reshape(EMB, FPAD, 128)
    mine = term + jnp.where(stream == 0, back, through)
    zsend2[...] = mine.reshape(EMB * FPAD, 128).astype(LOW)
    z_copy = remote(zsend2, zrecv2, zs_send.at[2], zs_recv.at[2], mp=cross)
    z_copy.start()

    reduce_add(0, 1, moving[1])
    moving[1] = reduce_send(1, 1)
    reduce_add(1, 0, moving[0])
    moving[0] = gather_send(1, 0)
    for copy in small:
        copy.wait()
    small_x[xx] = small_z[0] + small_z[1] + small_z[2] + small_z[3]
    small = []
    for n, (_, dev) in enumerate(rings[0]):
        small.append(remote(small_x.at[xx], small_x.at[xx], smx_send.at[n], smx_recv.at[n], dp=dev))
        small[n].start()
    reduce_add(1, 1, moving[1])
    moving[1] = gather_send(1, 1)
    moving[0] = gather_wide(0, moving[0])
    for copy in small:
        copy.wait()
    small_y[yy] = small_x[0] + small_x[1] + small_x[2] + small_x[3]
    small = []
    for n, (_, dev) in enumerate(rings[1]):
        small.append(remote(small_y.at[yy], small_y.at[yy], smy_send.at[n], smy_recv.at[n], dp=dev))
        small[n].start()
    moving[1] = gather_wide(1, moving[1])
    logit_ref[...] = nn(vec_rows.astype(LOW), act_third)
    z_copy.wait()
    whole = (zsend2[...].astype(F32) + zrecv2[...].astype(F32)).astype(LOW)
    zsend3[...] = whole
    z_copy = remote(zsend3, zrecv3, zs_send.at[3], zs_recv.at[3], mp=near)
    z_copy.start()
    egrad_ref[:, :, lanes_own] = whole.reshape(EMB, FPAD, 128)
    gather_end(0, moving[0])
    for copy in small:
        copy.wait()
    small_c[core] = small_y[0] + small_y[1] + small_y[2] + small_y[3]
    small = remote(small_c.at[core], small_c.at[core], smc_sem.at[0], smc_sem.at[1], dp=twin)
    small.start()
    z_copy.wait()
    egrad_ref[:, :, lanes_away] = zrecv3[...].reshape(EMB, FPAD, 128)
    gather_end(1, moving[1])
    small.wait()
    small_ref[...] = small_c[0] + small_c[1]
    for copy in core_copies + pair_loads[1:]:
        copy.wait()


def step(id_lists, id_counts, embed_rows, pair_set, fieldwise, hidden, biases, readout, logit_grad, bilinear, squeezer, exciter):
    first_index, second_index = np.triu_indices(FIELDS, 1)
    first = np.zeros((PPAD, FPAD), np.float32)
    second = np.zeros((PPAD, FPAD), np.float32)
    first[np.arange(PAIRS), first_index] = 1.0
    second[np.arange(PAIRS), second_index] = 1.0
    place = np.zeros((512, UNITS), np.float32)
    unit = np.arange(UNITS)
    place[128 * (unit // UDEV) + unit % UDEV, unit] = 1.0
    pair_field = np.arange(EMB * FPAD)
    same = (pair_field[:, None] % FPAD == pair_field[None, :ROWS * FPAD] % FPAD).astype(np.float32)
    rows_of = (np.arange(16)[:, None] == pair_field[None, :] // FPAD).astype(np.float32)
    cols_of = np.stack([
        (pair_field[:ROWS * FPAD, None] // FPAD + ROWS * part == np.arange(128)[None, :]).astype(np.float32) for part in range(2)
    ])
    constants = (
        np.concatenate([first, first], axis=1), np.concatenate([second, second], axis=1), first.T, second.T, place, place.T,
        same, rows_of, cols_of,
    )
    constants = [jnp.asarray(value, LOW) for value in constants]
    small_operands = (
        hidden, id_lists.transpose(1, 0, 2), id_counts, embed_rows.T,
        fieldwise, biases, readout.reshape(1, UDEV), logit_grad.reshape(1, BATCH), squeezer.T, exciter,
        *constants, bilinear,
    )
    vmem = pl.BlockSpec(memory_space=pltpu.VMEM)
    hbm = pl.BlockSpec(memory_space=pltpu.HBM)
    anywhere = pl.BlockSpec(memory_space=pl.ANY)
    low = lambda *shape: pltpu.VMEM(shape, LOW)
    full = lambda *shape: pltpu.VMEM(shape, F32)
    dma = lambda *shape: pltpu.SemaphoreType.DMA(shape)
    return pl.pallas_call(
        step_kernel,
        out_shape=(
            pltpu.VMEM((2, TILES, 16, 128), LOW),
            jax.ShapeDtypeStruct((SMALL, 128), F32),
            jax.ShapeDtypeStruct((EMB, FPAD, BATCH), LOW),
            jax.ShapeDtypeStruct((8, BATCH), F32),
        ) + (pltpu.VMEM(pair_set[0].shape, F32),) * 3,
        in_specs=[hbm] * 23,
        out_specs=(anywhere, vmem, vmem, vmem) + (vmem,) * 3,
        scratch_shapes=[
            pltpu.VMEM(hidden.shape, F32), pltpu.VMEM((FPAD, SLOTS, BATCH), jnp.int32),
            *(pltpu.VMEM(array.shape, array.dtype) for array in small_operands[2:-1]),
            pltpu.SMEM((EMB, EMB), F32),
            full(EMB, FPAD, BATCH), pltpu.VMEM((FPAD, BATCH), jnp.int32), pltpu.VMEM((EMB // 2, 8, 128), jnp.int32),
            low(ROWS, UNITS, PPAD), low(ROWS, PPAD, UNITS),
            low(ROWS, PPAD, BATCH), low(ROWS, PPAD, BATCH), low(ROWS, PPAD, BATCH), low(ROWS, HALF, BATCH),
            full(EMB, FPAD, BATCH), full(FPAD, BATCH), full(FPAD, BATCH), full(16, BATCH), full(FPAD, BATCH),
            full(16, 128), full(16, 128), full(EMB * FPAD, 128), low(EMB * FPAD, UNITS), low(UNITS, EMB * FPAD),
            low(2, UNITS, 512), full(8, 512), low(2, UNITS, UNITS), low(2, UNITS, UNITS),
            low(4 * ZROWS, BATCH), low(3, ZROWS, BATCH), low(4 * ZROWS, BATCH), low(UNITS, BATCH), low(UNITS, BATCH),
            low(TILES, 16, 128), low(2, 3, HALVES // 4, 16, 128), low(2, 3, HALVES // 16, 16, 128),
            low(2 * AUX, 16, 128), low(AUX, 16, 128),
            full(EMB, FPAD, BATCH), full(EMB, FPAD, BATCH),
            low(2, EMB * FPAD, 128), low(2, EMB * FPAD, 128), low(EMB * FPAD, 128), low(EMB * FPAD, 128),
            low(EMB * FPAD, 128), low(EMB * FPAD, 128),
            full(4, SMALL, 128), full(4, SMALL, 128), full(4, SMALL, 128), full(2, SMALL, 128),
            dma(20), dma(3), dma(3), dma(3), dma(3), dma(3), dma(2), dma(2),
            dma(3), dma(3), dma(3), dma(3),
            dma(2), dma(2), dma(2, 2, 2, 3), dma(2, 2, 2, 3), dma(2, 2), dma(2, 2, 2, 3), dma(2, 2, 2, 3),
            dma(2, 2, 4), dma(2, 2, 4),
            dma(4), dma(4), dma(3), dma(3), dma(3), dma(3), dma(3), dma(3), dma(2),
        ],
        compiler_params=pltpu.CompilerParams(
            collective_id=0, has_side_effects=True, vmem_limit_bytes=32 * MIB
        ),
        name="step",
    )(*in_hbm(small_operands), *in_hbm(pair_set))


def update_kernel(grads, small, egrad, logit, weight, momentum, average, *refs):
    inputs, refs = refs[:24], refs[24:]
    logits_out, egrad_out = refs[:2]
    pair_outs, outputs, refs = refs[2:5], refs[5:29], refs[29:]
    held, refs = refs[:24], refs[24:]
    logits_held, egrad_held, pair_held, in_sem, out_sem, pair_sem = refs

    loads = [pltpu.make_async_copy(src, dst, in_sem.at[n]) for n, (src, dst) in enumerate(zip(inputs, held))]
    for copy in loads:
        copy.start()

    stores = []
    for k in range(ROWS):
        slot = k % 2
        if k >= 2:
            for copy in stores[3 * (k - 2):3 * (k - 1)]:
                copy.wait()
        for c in range(2):
            for j in range(3):
                first = HALF * c + 128 * j
                last = min(first + 128, PAIRS)
                tiles = [grads[c, KTILES * k + 3 * r + j] for r in range(UNITS // 16)]
                grad = jnp.concatenate(tiles, axis=0).astype(F32)[:, 0:last - first]
                at = (k, slice(None), slice(first, last))
                values = nesterov(weight[at], momentum[at], average[at], grad, RATE)
                for n, value in enumerate(values):
                    pair_held[slot, n, :, first:last] = value
        for n in range(3):
            stores.append(pltpu.make_async_copy(pair_held.at[slot, n], pair_outs[n].at[k], pair_sem.at[slot, n]))
            stores[-1].start()

    for copy in loads:
        copy.wait()

    def put(which, at, grad, rate):
        weight, momentum, average = held[3 * which:3 * which + 3]
        values = nesterov(weight[at], momentum[at], average[at], grad, rate)
        for ref, value in zip((weight, momentum, average), values):
            ref[at] = value

    whole = jnp.concatenate([grads[0, KTILES * ROWS:KTILES * ROWS + AUX], grads[1, KTILES * ROWS:KTILES * ROWS + AUX]], axis=0)
    whole = whole.astype(F32).reshape(2 * AUX * 16, 128)
    for k in range(EMB):
        put(0, (k,), whole[FPAD * k:FPAD * k + FIELDS, 0:UDEV], RATE)
    for layer in range(2):
        put(1, (layer,), whole[UNITS * (layer + 1):UNITS * (layer + 2), 0:UDEV], RATE)
    everything = (slice(None), slice(None))
    offset_weight = held[12][...]
    put(2, everything, whole[75 * 16:75 * 16 + 3, 0:UDEV], FAST_RATE)
    put(3, everything, whole[75 * 16 + 3:75 * 16 + 4, 0:UDEV], RATE)
    put(4, everything, small[15:16, 0:1], RATE)
    put(5, everything, small[0:EMB, 0:EMB], RATE)
    put(6, everything, small[16:16 + REDUCED, 0:FIELDS], FAST_RATE)
    put(7, everything, small[32:32 + REDUCED, 0:FIELDS], FAST_RATE)
    logits_held[...] = logit[3:4, :] + offset_weight
    for k in range(EMB):
        egrad_held[k] = egrad[k, :, :].astype(F32)[0:FIELDS]
    lasts = zip((logits_held, egrad_held) + tuple(held), (logits_out, egrad_out) + tuple(outputs))
    lasts = [pltpu.make_async_copy(src, dst, out_sem.at[n]) for n, (src, dst) in enumerate(lasts)]
    for copy in lasts:
        copy.start()
    for copy in lasts + stores[3 * (ROWS - 2):]:
        copy.wait()


def update(grads, small, egrad, logit, sets):
    vmem = pl.BlockSpec(memory_space=pltpu.VMEM)
    hbm = pl.BlockSpec(memory_space=pltpu.HBM)
    pair, others = sets[0], [array for arrays in sets[1:] for array in arrays]
    shapes = [(1, BATCH), (EMB, FIELDS, BATCH)] + [array.shape for array in pair] + [array.shape for array in others]
    return pl.pallas_call(
        update_kernel,
        in_specs=[vmem] * 7 + [hbm] * 24,
        out_specs=[hbm] * 29,
        out_shape=[jax.ShapeDtypeStruct(shape, F32) for shape in shapes],
        scratch_shapes=[
            *(pltpu.VMEM(array.shape, F32) for array in others),
            pltpu.VMEM((1, BATCH), F32), pltpu.VMEM((EMB, FIELDS, BATCH), F32),
            pltpu.VMEM((2, 3, UNITS, PAIRS), F32),
            pltpu.SemaphoreType.DMA((24,)), pltpu.SemaphoreType.DMA((26,)), pltpu.SemaphoreType.DMA((2, 3)),
        ],
        compiler_params=pltpu.CompilerParams(vmem_limit_bytes=16 * MIB),
        name="update",
    )(grads, small, egrad, logit, *pair, *in_hbm(others[:12]), *others[12:15], *in_hbm(others[15:]))


def per_device(
    id_lists, id_counts, embed_rows, logit_grad,
    bilinear, bilinear_momentum, bilinear_average,
    squeezer, squeezer_momentum, squeezer_average,
    exciter, exciter_momentum, exciter_average,
    pairwise, pairwise_momentum, pairwise_average,
    fieldwise, fieldwise_momentum, fieldwise_average,
    hidden, hidden_momentum, hidden_average,
    biases, biases_momentum, biases_average,
    readout, readout_momentum, readout_average,
    offset, offset_momentum, offset_average,
):
    turn = lambda *arrays: tuple(array.swapaxes(-1, -2) for array in arrays)
    pair_set = turn(pairwise, pairwise_momentum, pairwise_average)
    grads, small, egrad, logit, *held = step(
        id_lists, id_counts, embed_rows, pair_set, fieldwise, hidden, biases, readout, logit_grad, bilinear, squeezer, exciter
    )
    row = lambda *arrays: tuple(array.reshape(1, -1) for array in arrays)
    outs = update(
        grads, small, egrad, logit,
        [
            held,
            (fieldwise, fieldwise_momentum, fieldwise_average),
            (hidden, hidden_momentum, hidden_average),
            (biases, biases_momentum, biases_average),
            row(readout, readout_momentum, readout_average),
            row(offset, offset_momentum, offset_average),
            (bilinear, bilinear_momentum, bilinear_average),
            turn(squeezer, squeezer_momentum, squeezer_average),
            (exciter, exciter_momentum, exciter_average),
        ],
    )
    logits, egrad_full = outs[0].reshape(-1), outs[1]
    pair, field, hid, bias, read, off, bil, squ, exc = (tuple(outs[2 + 3 * i:5 + 3 * i]) for i in range(9))
    flat = lambda arrays: tuple(array.reshape(-1) for array in arrays)
    return (logits, egrad_full) + bil + turn(*squ) + exc + turn(*pair) + field + hid + bias + flat(read) + flat(off)


def solution(mesh):
    whole = (P(),) * 3
    rows = (P("mp", None, None),) * 3
    units = (P(None, None, "mp"),) * 3
    vectors = (P(None, "mp"),) * 3
    line = (P("mp"),) * 3
    weights = whole + whole + whole + rows + units + units + vectors + line + whole
    return jax.shard_map(
        per_device,
        mesh=mesh,
        in_specs=(P(None, None, "dp"), P(None, "dp"), P("dp", None), P("dp")) + weights,
        out_specs=(P("dp"), P(None, None, "dp")) + weights,
        check_vma=False,
    )
```

```python
import jax
import jax.numpy as jnp
import numpy as np
from jax import lax
from jax.experimental import pallas as pl
from jax.experimental.pallas import tpu as pltpu
from jax.sharding import PartitionSpec as P

MOMENTUM = 0.9
RATE = 0.01
FAST_RATE = 0.05
DECAY = 0.8
HIGHEST = lax.Precision.HIGHEST
F32 = jnp.float32
LOW = jnp.bfloat16
MESH = pl.DeviceIdType.MESH
MIB = 1024 * 1024

EMB = 10
FIELDS = 39
FPAD = 40
REDUCED = 13
UNITS = 400
ZROWS = 112
ZPARTS = ((0, 64), (64, 48))
UDEV = 100
SLOTS = 8
BATCH = 256
FETCH = 1024
PAIRS = 741
PPAD = 768
HALF = 384
ROWS = 5
TILES = 416
HALVES = TILES // 2
CHUNKS = (112, 96)
KTILES = 75
BUFFERS = 3
AUX = 38
SMALL = 48
STEPS = 4095


def dot(left, right, contract, precision=None):
    return lax.dot_general(
        left, right, ((contract[0], contract[1]), ((), ())),
        precision=precision, preferred_element_type=F32,
    )


def nn(left, right, precision=None):
    return dot(left, right, ((1,), (0,)), precision)


def nt(left, right, precision=None):
    return dot(left, right, ((1,), (1,)), precision)


def tn(left, right, precision=None):
    return dot(left, right, ((0,), (0,)), precision)


def in_hbm(arrays):
    return tuple(pltpu.with_memory_space_constraint(array, pltpu.HBM) for array in arrays)


def nesterov(weight, momentum, average, grad, step_rate):
    velocity = MOMENTUM * momentum + grad
    updated = weight - step_rate * (grad + MOMENTUM * velocity)
    smoothed = DECAY * average + (1.0 - DECAY) * updated
    return (velocity, smoothed, updated)


def pool(ids_ref, count_ref, rows_ref, counts, table, out_ref, between):
    rows = rows_ref[...].astype(F32)
    largest = jnp.maximum(jnp.max(jnp.abs(rows), keepdims=True), 1e-30)
    fixed = jnp.round(rows * (STEPS / largest)).astype(jnp.int32) + (STEPS + 1)
    for chunk in range(8):
        part = fixed[:, 128 * chunk:128 * (chunk + 1)]
        for k in range(EMB // 2):
            table[k, chunk:chunk + 1, :] = part[2 * k:2 * k + 1, :] * 65536 + part[2 * k + 1:2 * k + 2, :]
    counts[0:FIELDS, :] = count_ref[...]
    counts[FIELDS:FPAD, :] = jnp.ones((1, BATCH), jnp.int32)
    ids_ref[FIELDS] = jnp.full((SLOTS, BATCH), 8 * FETCH, jnp.int32)
    sublane = lax.broadcasted_iota(jnp.int32, (8, 128), 0)
    unit = largest * (1.0 / STEPS)

    def group(g, carry):
        fields = pl.ds(pl.multiple_of(8 * g, 8), 8)
        for h in range(2):
            lanes = slice(128 * h, 128 * (h + 1))
            live = counts[fields, lanes]
            found = [[] for _ in range(EMB // 2)]
            for row in range(8):
                ids = jnp.where(live[row:row + 1, :] > sublane, ids_ref[8 * g + row, :, lanes], 8 * FETCH)
                totals = [None] * (EMB // 2)
                for slot in range(SLOTS):
                    wide = jnp.broadcast_to(ids[slot:slot + 1, :], (8, 128))
                    lane = wide & 127
                    hit = (wide >> 7) == sublane
                    for k in range(EMB // 2):
                        value = jnp.take_along_axis(table[k], lane, axis=1, mode="promise_in_bounds")
                        value = jnp.where(hit, value, 0)
                        totals[k] = value if totals[k] is None else totals[k] + value
                for k in range(EMB // 2):
                    found[k].append(jnp.sum(totals[k], axis=0, keepdims=True))
            factor = unit / live.astype(F32)
            for k in range(EMB // 2):
                both = jnp.concatenate(found[k], axis=0)
                for part, word in enumerate(((both >> 16) & 65535, both & 65535)):
                    total = (word - (STEPS + 1) * live).astype(F32)
                    out_ref[2 * k + part, fields, lanes] = (total * factor).astype(LOW).astype(F32)
        return carry

    lax.fori_loop(0, 2, group, 0)
    between()
    lax.fori_loop(2, FPAD // 8, group, 0)
    out_ref[:, FPAD - 8:FPAD, :] = jnp.where(
        lax.broadcasted_iota(jnp.int32, (EMB, 8, BATCH), 1) == 7, 0.0, out_ref[:, FPAD - 8:FPAD, :]
    )


def gate_of(before):
    return 0.5 + 0.5 * jnp.tanh(0.5 * before)


def silu_slope(before, gate):
    return gate * (1.0 + before * (1.0 - gate))


def softplus(value):
    return jnp.maximum(value, 0.0) + jnp.log1p(jnp.exp(-jnp.abs(value)))


def two_terms(value):
    high = value.astype(LOW)
    return high, (value - high.astype(F32)).astype(LOW)


def split(value):
    high = value.astype(LOW).astype(F32)
    return jnp.concatenate([high, value - high], axis=0).astype(LOW)


def step_kernel(*refs):
    hbm, pairs_in, refs = refs[:20], refs[20:23], refs[23:]
    gout_ref, small_ref, egrad_ref, logit_ref, *pairs_out = refs[:7]
    loaded, refs = refs[7:27], refs[27:]
    pair_ref = pairs_out[0]
    (
        ids_ref, count_ref, rows_ref, hidden_ref,
        field_ref, bias_ref, readout_ref, grad_ref, squ_ref, exc_ref,
        first_ref, second_ref, first_t_ref, second_t_ref, place_ref, place_t_ref, same_ref, rows_of_ref, cols_of_ref, bil_ref,
    ) = loaded
    (
        emb_ref, counts, table, w_low, w_turned, left, right, feats, feats_peer, source, scale_s, sq_s, z1_s, z2_s,
        squ_pad, exc_pad, fpad, fplaced, fplaced_t, hid_all, vec_all, hid_full, hid_turned,
        pre_part, rs_in, pre_full, gf, gf_peer,
        acc, box1, box2, aux, aux_in,
        dsrc, eterm, zsend, zrecv, zsend2, zrecv2, zsend3, zrecv3, small_z, small_x, small_y, small_c,
        load_sem, pair_sem, hid_send, hid_recv, vec_send, vec_recv, twin_sem, feat_sem,
        rsz_send, rsz_recv, agz_send, agz_recv,
        gf_sem, aux_sem, red_send, red_recv, own_sem, gat_send, gat_recv, core_send, core_recv,
        zs_send, zs_recv, smz_send, smz_recv, smx_send, smx_recv, smy_send, smy_recv, smc_sem,
    ) = refs
    dp = lax.axis_index("dp")
    me = lax.axis_index("mp")
    core = dp % 2
    yy = (dp // 2) % 4
    xx = dp // 8

    def at_dp(x, y, c):
        return (x * 4 + y) * 2 + c

    rings = (
        [((xx + off) % 4, at_dp((xx + off) % 4, yy, core)) for off in (1, 3, 2)],
        [((yy + off) % 4, at_dp(xx, (yy + off) % 4, core)) for off in (1, 3, 2)],
    )
    places = (xx, yy)
    twin = at_dp(xx, yy, 1 - core)
    peers = [(me + off) % 4 for off in (1, 3, 2)]
    stream = me // 2
    columns = (me % 2) * ROWS
    half = ((me + 1) // 2) % 2
    near = me + 1 - 2 * (me % 2)
    cross = 3 - me

    def remote(src, dst, send, recv, **where):
        return pltpu.make_async_remote_copy(
            src_ref=src, dst_ref=dst, send_sem=send, recv_sem=recv, device_id=where, device_id_type=MESH
        )

    targets = (ids_ref.at[pl.ds(0, FIELDS)],) + loaded[1:]
    loads = [pltpu.make_async_copy(src, dst, load_sem.at[n]) for n, (src, dst) in enumerate(zip(hbm, targets))]
    for copy in loads:
        copy.start()
    pair_loads = [
        pltpu.make_async_copy(src, dst, pair_sem.at[n]) for n, (src, dst) in enumerate(zip(pairs_in, pairs_out))
    ]
    for copy in pair_loads:
        copy.start()
    barrier = pltpu.get_barrier_semaphore()
    for peer in peers:
        pl.semaphore_signal(barrier, inc=1, device_id={"mp": peer}, device_id_type=MESH)
    for dev in [dev for ring in rings for _, dev in ring] + [twin]:
        pl.semaphore_signal(barrier, inc=1, device_id={"dp": dev}, device_id_type=MESH)

    lanes_me = pl.ds(pl.multiple_of(128 * me, 128), 128)
    hid_copies = []
    for n, peer in enumerate(peers):
        mine = hid_all.at[core, :, lanes_me]
        hid_copies.append(remote(mine, mine, hid_send.at[n], hid_recv.at[n], mp=peer))
        mine = vec_all.at[:, lanes_me]
        hid_copies.append(remote(mine, mine, vec_send.at[n], vec_recv.at[n], mp=peer))

    def share_hidden():
        for copy in loads[3:]:
            copy.wait()
        fpad[...] = jnp.zeros_like(fpad)
        fpad[:, 0:UDEV] = hidden_ref[core]
        hid_all[core, :, lanes_me] = fpad[...].astype(LOW)
        fpad[0:8, :] = jnp.zeros((8, 128), F32)
        fpad[0:3, 0:UDEV] = bias_ref[...]
        fpad[3:4, 0:UDEV] = readout_ref[...].astype(LOW).astype(F32)
        vec_all[:, lanes_me] = fpad[0:8, :]
        pl.semaphore_wait(barrier, 10)
        for copy in hid_copies:
            copy.start()

    for copy in loads[:3]:
        copy.wait()
    pool(ids_ref, count_ref, rows_ref, counts, table, emb_ref, share_hidden)

    squ_pad[...] = jnp.zeros_like(squ_pad)
    squ_pad[0:REDUCED, 0:FIELDS] = squ_ref[...]
    exc_pad[...] = jnp.zeros_like(exc_pad)
    exc_pad[0:REDUCED, 0:FIELDS] = exc_ref[...]
    squeezer = squ_pad[:, 0:FPAD]
    exciter = exc_pad[:, 0:FPAD]
    emb = emb_ref[...]
    squeezed = jnp.sum(emb, axis=0) * (1.0 / EMB)
    z1 = nn(squeezer, squeezed, HIGHEST)
    z2 = tn(exciter, z1 * gate_of(z1), HIGHEST)
    scales = softplus(z2)
    sq_s[...] = squeezed
    z1_s[...] = z1
    z2_s[...] = z2
    scale_s[...] = scales
    factor = jnp.where(stream == 0, jnp.ones_like(scales), scales)
    for k in range(EMB):
        source[k] = emb_ref[k] * factor

    for k in range(ROWS):
        projected = source[0] * bil_ref[0, columns + k]
        for l in range(1, EMB):
            projected = projected + source[l] * bil_ref[l, columns + k]
        left_k = nn(first_ref[...], split(projected))
        right_k = nn(second_ref[...], split(source[columns + k]))
        left[k] = left_k.astype(LOW)
        right[k] = right_k.astype(LOW)
        feats[k] = (left_k * right_k).astype(LOW)
    feat_copy = remote(
        feats.at[:, pl.ds(pl.multiple_of(HALF * (1 - core), HALF), HALF), :], feats_peer,
        feat_sem.at[0], feat_sem.at[1], dp=twin,
    )
    feat_copy.start()
    fpad[0:8, :] = jnp.zeros((8, 128), F32)
    for k in range(EMB):
        fpad[FPAD * k:FPAD * k + FIELDS, 0:UDEV] = field_ref[k]
        fpad[FPAD * k + FIELDS:FPAD * (k + 1), :] = jnp.zeros((1, 128), F32)
    field_low = fpad[...].astype(LOW)
    place_own = place_ref[lanes_me, :]
    fplaced_t[...] = nt(place_t_ref[:, lanes_me], field_low).astype(LOW)
    emb_low = emb.reshape(EMB * FPAD, BATCH).astype(LOW)
    pre = nn(fplaced_t[...], emb_low)
    pair_loads[0].wait()
    for k in range(ROWS):
        w_low[k, :, 640:PPAD] = jnp.zeros((UNITS, PPAD - 640), LOW)
        w_low[k, :, 0:PAIRS] = pair_ref[k].astype(LOW)
        pre = pre + nn(w_low[k], feats[k])
    pre_part[0:UNITS, :] = pre.astype(LOW)
    pre_part[UNITS:4 * ZROWS, :] = jnp.zeros((4 * ZROWS - UNITS, BATCH), LOW)

    rs_copies = []
    for part, (low_row, count) in enumerate(ZPARTS):
        for n, peer in enumerate(peers):
            rows = pl.ds(pl.multiple_of(ZROWS * peer + low_row, 16), count)
            box = rs_in.at[n, pl.ds(low_row, count)]
            rs_copies.append(remote(pre_part.at[rows], box, rsz_send.at[part, n], rsz_recv.at[part, n], mp=peer))
            rs_copies[-1].start()
    for copy in hid_copies:
        copy.wait()
    layer = hid_all.at[core]
    hid_twin = remote(layer, layer, twin_sem.at[0], twin_sem.at[1], dp=twin)
    hid_twin.start()
    fplaced[...] = nn(field_low, place_own).astype(LOW)
    ag_copies = []
    for part, (low_row, count) in enumerate(ZPARTS):
        for copy in rs_copies[3 * part:3 * part + 3]:
            copy.wait()
        own_rows = pl.ds(pl.multiple_of(ZROWS * me + low_row, 16), count)
        total = pre_part[own_rows, :].astype(F32)
        for n in range(3):
            total = total + rs_in[n, low_row:low_row + count].astype(F32)
        pre_full[own_rows, :] = total.astype(LOW)
        mine = pre_full.at[own_rows]
        for n, peer in enumerate(peers):
            ag_copies.append(remote(mine, mine, agz_send.at[part, n], agz_recv.at[part, n], mp=peer))
            ag_copies[-1].start()

    hid_twin.wait()
    for layer in range(2):
        hid_full[layer] = nn(hid_all[layer], place_ref[...]).astype(LOW)
        hid_turned[layer] = nt(place_t_ref[...], hid_all[layer]).astype(LOW)
    vec_rows = nn(vec_all[...], place_ref[...].astype(F32), HIGHEST)
    vec_cols = nt(place_t_ref[...].astype(F32), vec_all[...], HIGHEST)
    for copy in ag_copies:
        copy.wait()

    pre_first = pre_full[0:UNITS, :].astype(F32) + vec_cols[:, 0:1]
    gate_first = gate_of(pre_first)
    act_first = (pre_first * gate_first).astype(LOW)
    pre_second = nn(hid_turned[0], act_first) + vec_cols[:, 1:2]
    gate_second = gate_of(pre_second)
    act_second = (pre_second * gate_second).astype(LOW)
    pre_third = nn(hid_turned[1], act_second) + vec_cols[:, 2:3]
    gate_third = gate_of(pre_third)
    act_third = (pre_third * gate_third).astype(LOW)
    upstream = grad_ref[...].astype(F32).reshape(1, BATCH)
    grad_third = ((vec_cols[:, 3:4] * upstream) * silu_slope(pre_third, gate_third)).astype(LOW)
    grad_second = (nn(hid_full[1], grad_third) * silu_slope(pre_second, gate_second)).astype(LOW)
    grad_first = (nn(hid_full[0], grad_second) * silu_slope(pre_first, gate_first)).astype(LOW)
    gf[...] = grad_first
    gf_copy = remote(gf, gf_peer, gf_sem.at[0], gf_sem.at[1], dp=twin)
    gf_copy.start()

    first_mine = nn(place_own, grad_first).astype(LOW)
    second_mine = nn(place_own, grad_second).astype(LOW)
    third_mine = nn(place_own, grad_third).astype(LOW)
    act_mine = nn(place_own, act_third).astype(LOW)
    aux[0:25] = nt(emb_low, first_mine).astype(LOW).reshape(25, 16, 128)
    aux[25:50] = nt(act_first, second_mine).astype(LOW).reshape(25, 16, 128)
    aux[50:75] = nt(act_second, third_mine).astype(LOW).reshape(25, 16, 128)
    ones = jnp.ones((16, BATCH), LOW)
    upstream_rows = jnp.broadcast_to(upstream, (16, BATCH)).astype(LOW)
    row_iota = lax.broadcasted_iota(jnp.int32, (16, 128), 0)
    vec_grads = jnp.where(row_iota == 0, nt(ones, first_mine), 0.0)
    vec_grads = vec_grads + jnp.where(row_iota == 1, nt(ones, second_mine), 0.0)
    vec_grads = vec_grads + jnp.where(row_iota == 2, nt(ones, third_mine), 0.0)
    vec_grads = vec_grads + jnp.where(row_iota == 3, nt(upstream_rows, act_mine), 0.0)
    aux[75] = jnp.zeros((16, 128), LOW)
    aux_copy = remote(
        aux.at[pl.ds(AUX * (1 - core), AUX)], aux_in, aux_sem.at[0], aux_sem.at[1], dp=twin
    )
    aux_copy.start()

    feat_copy.wait()
    own_half = pl.ds(pl.multiple_of(HALF * core, HALF), HALF)
    gf_copy.wait()
    for k in range(ROWS):
        grad = (nt(gf[...], feats[k, own_half, :]) + nt(gf_peer[...], feats_peer[k])).astype(LOW)
        tiles = [grad[:, 128 * j:128 * (j + 1)].reshape(25, 16, 128) for j in range(3)]
        acc[KTILES * k:KTILES * (k + 1)] = jnp.stack(tiles, axis=1).reshape(KTILES, 16, 128)
    acc[KTILES * ROWS + AUX:TILES] = jnp.zeros((TILES - KTILES * ROWS - AUX, 16, 128), LOW)
    aux_copy.wait()
    aux_mine = aux[pl.ds(AUX * core, AUX)].astype(F32) + aux_in[...].astype(F32)
    acc[KTILES * ROWS:KTILES * ROWS + AUX] = aux_mine.astype(LOW)

    offsets = (0, CHUNKS[0])
    starts = [[HALVES * h + offsets[c] for c in range(2)] for h in range(2)]

    def size_of(t, c):
        return CHUNKS[c] // (4, 16)[t]

    def box_of(t, h, n, c):
        return (box1, box2)[t].at[h, n, pl.ds(offsets[c] // (4, 16)[t], size_of(t, c))]

    def reduce_send(t, c):
        size = size_of(t, c)
        copies = []
        for n in range(3):
            for h in range(2):
                place, dev = rings[(h + t) % 2][n]
                src = acc.at[pl.ds(starts[h][c] + place * size, size)]
                copies.append(
                    remote(src, box_of(t, h, n, c), red_send.at[t, h, c, n], red_recv.at[t, h, c, n], dp=dev)
                )
                copies[-1].start()
        for h in range(2):
            starts[h][c] = starts[h][c] + places[(h + t) % 2] * size
        return copies

    def reduce_add(t, c, copies):
        for copy in copies:
            copy.wait()
        for h in range(2):
            keep = pl.ds(starts[h][c], size_of(t, c))
            total = acc[keep].astype(F32)
            for n in range(3):
                total = total + box_of(t, h, n, c)[...].astype(F32)
            acc[keep] = total.astype(LOW)

    own_copies = []
    core_copies = []

    def pass_on(h, c, slot, start, count):
        where = gout_ref.at[core, pl.ds(start, count)]
        copy = remote(where, where, core_send.at[h, c, slot], core_recv.at[h, c, slot], dp=twin)
        copy.start()
        core_copies.append(copy)

    def gather_send(t, c):
        size = size_of(t, c)
        copies = []
        for n in range(3):
            for h in range(2):
                _, dev = rings[(h + t) % 2][n]
                where = gout_ref.at[core, pl.ds(starts[h][c], size)]
                src = acc.at[pl.ds(starts[h][c], size)] if t == 1 else where
                copy = remote(src, where, gat_send.at[t, h, c, n], gat_recv.at[t, h, c, n], dp=dev)
                copy.start()
                sender = rings[(h + t) % 2][(1, 0, 2)[n]][0]
                came = starts[h][c] + (sender - places[(h + t) % 2]) * size
                copies.append((copy, h, n, came))
        for h in range(2):
            if t == 1:
                where = pl.ds(starts[h][c], size)
                own = pltpu.make_async_copy(acc.at[where], gout_ref.at[core, where], own_sem.at[h, c])
                own.start()
                own_copies.append(own)
            starts[h][c] = starts[h][c] - places[(h + t) % 2] * size
        return copies

    def gather_wide(c, copies):
        for copy, _, _, _ in copies:
            copy.wait()
        for own in own_copies[2 * c:2 * c + 2]:
            own.wait()
        wide = gather_send(0, c)
        for h in range(2):
            pass_on(h, c, 3, starts[h][c] + places[h] * size_of(0, c), size_of(0, c))
        return wide

    def gather_end(c, copies):
        for copy, h, n, came in copies:
            copy.wait()
            pass_on(h, c, n, came, size_of(0, c))

    moving = [reduce_send(0, c) for c in range(2)]

    dprojected = []
    dchosen = []
    for k in range(ROWS):
        w_turned[k] = jnp.transpose(w_low[k])
        dfeat = nn(w_turned[k], gf[...])
        dprojected.append(nn(first_t_ref[...], (dfeat * right[k].astype(F32)).astype(LOW)))
        dchosen.append(nn(second_t_ref[...], (dfeat * left[k].astype(F32)).astype(LOW)))
    for l in range(EMB):
        total = dprojected[0] * bil_ref[l, columns]
        for k in range(1, ROWS):
            total = total + dprojected[k] * bil_ref[l, columns + k]
        dsrc[l] = total
    for k in range(ROWS):
        dsrc[columns + k] = dsrc[columns + k] + dchosen[k]
    eterm[...] = nn(fplaced[...], gf[...]).reshape(EMB, FPAD, BATCH)
    lanes_away = pl.ds(pl.multiple_of(128 * (1 - half), 128), 128)
    lanes_own = pl.ds(pl.multiple_of(128 * half, 128), 128)
    zsend[0] = dsrc[:, :, lanes_away].reshape(EMB * FPAD, 128).astype(LOW)
    zsend[1] = eterm[:, :, lanes_away].reshape(EMB * FPAD, 128).astype(LOW)
    z_copies = [remote(zsend.at[n], zrecv.at[n], zs_send.at[n], zs_recv.at[n], mp=near) for n in range(2)]
    for copy in z_copies:
        copy.start()
    source_high, source_rest = two_terms(source[...].reshape(EMB * FPAD, BATCH))
    dproj_high, dproj_rest = two_terms(jnp.concatenate(dprojected, axis=0))
    products = nt(source_high, dproj_high) + nt(source_high, dproj_rest) + nt(source_rest, dproj_high)
    products = products * same_ref[...].astype(F32)
    bil_rows = nn(nn(rows_of_ref[...].astype(F32), products, HIGHEST), cols_of_ref[me % 2].astype(F32), HIGHEST)
    bil_rows = jnp.where(row_iota == 15, jnp.sum(upstream) * 0.25, bil_rows)
    reduce_add(0, 0, moving[0])
    moving[0] = reduce_send(1, 0)

    z_copies[0].wait()
    back = dsrc[:, :, lanes_own] + zrecv[0].astype(F32).reshape(EMB, FPAD, 128)
    emb_half = emb_ref[:, :, lanes_own]
    z1 = z1_s[:, lanes_own]
    z2 = z2_s[:, lanes_own]
    dscale = jnp.sum(back * emb_half, axis=0)
    dz2 = dscale * gate_of(z2)
    gate = gate_of(z1)
    dexciter = nt(z1 * gate, dz2, HIGHEST)
    dz1 = nn(exciter, dz2, HIGHEST) * silu_slope(z1, gate)
    dsqueezer = nt(dz1, sq_s[:, lanes_own], HIGHEST)
    weighted = jnp.where(stream == 0, jnp.zeros((1, 1), F32), jnp.ones((1, 1), F32))

    small_z[me, 0:16, :] = bil_rows
    small_z[me, 16:SMALL, :] = jnp.zeros((32, 128), F32)
    small_z[me, 16:32, 0:FPAD] = dsqueezer * weighted
    small_z[me, 32:48, 0:FPAD] = dexciter * weighted
    small = []
    for n, peer in enumerate(peers):
        small.append(remote(small_z.at[me], small_z.at[me], smz_send.at[n], smz_recv.at[n], mp=peer))
        small[n].start()
    dsqueezed = tn(squeezer, dz1, HIGHEST) * (1.0 / EMB)
    through = back * scale_s[:, lanes_own][None] + dsqueezed[None]
    z_copies[1].wait()
    term = eterm[:, :, lanes_own] + zrecv[1].astype(F32).reshape(EMB, FPAD, 128)
    mine = term + jnp.where(stream == 0, back, through)
    zsend2[...] = mine.reshape(EMB * FPAD, 128).astype(LOW)
    z_copy = remote(zsend2, zrecv2, zs_send.at[2], zs_recv.at[2], mp=cross)
    z_copy.start()

    reduce_add(0, 1, moving[1])
    moving[1] = reduce_send(1, 1)
    reduce_add(1, 0, moving[0])
    moving[0] = gather_send(1, 0)
    for copy in small:
        copy.wait()
    small_x[xx, 0:SMALL] = small_z[0] + small_z[1] + small_z[2] + small_z[3]
    small_x[xx, SMALL:SMALL + 8] = vec_grads[0:8]
    small = []
    for n, (_, dev) in enumerate(rings[0]):
        small.append(remote(small_x.at[xx], small_x.at[xx], smx_send.at[n], smx_recv.at[n], dp=dev))
        small[n].start()
    reduce_add(1, 1, moving[1])
    moving[1] = gather_send(1, 1)
    moving[0] = gather_wide(0, moving[0])
    for copy in small:
        copy.wait()
    small_y[yy] = small_x[0] + small_x[1] + small_x[2] + small_x[3]
    small = []
    for n, (_, dev) in enumerate(rings[1]):
        small.append(remote(small_y.at[yy], small_y.at[yy], smy_send.at[n], smy_recv.at[n], dp=dev))
        small[n].start()
    moving[1] = gather_wide(1, moving[1])
    logit_ref[...] = nn(vec_rows.astype(LOW), act_third)
    z_copy.wait()
    whole = (zsend2[...].astype(F32) + zrecv2[...].astype(F32)).astype(LOW)
    zsend3[...] = whole
    z_copy = remote(zsend3, zrecv3, zs_send.at[3], zs_recv.at[3], mp=near)
    z_copy.start()
    egrad_ref[:, :, lanes_own] = whole.reshape(EMB, FPAD, 128)
    gather_end(0, moving[0])
    for copy in small:
        copy.wait()
    small_c[core] = small_y[0] + small_y[1] + small_y[2] + small_y[3]
    small = remote(small_c.at[core], small_c.at[core], smc_sem.at[0], smc_sem.at[1], dp=twin)
    small.start()
    z_copy.wait()
    egrad_ref[:, :, lanes_away] = zrecv3[...].reshape(EMB, FPAD, 128)
    gather_end(1, moving[1])
    small.wait()
    small_ref[...] = small_c[0] + small_c[1]
    for copy in core_copies + pair_loads[1:]:
        copy.wait()


def step(id_lists, id_counts, embed_rows, pair_set, fieldwise, hidden, biases, readout, logit_grad, bilinear, squeezer, exciter):
    first_index, second_index = np.triu_indices(FIELDS, 1)
    first = np.zeros((PPAD, FPAD), np.float32)
    second = np.zeros((PPAD, FPAD), np.float32)
    first[np.arange(PAIRS), first_index] = 1.0
    second[np.arange(PAIRS), second_index] = 1.0
    place = np.zeros((512, UNITS), np.float32)
    unit = np.arange(UNITS)
    place[128 * (unit // UDEV) + unit % UDEV, unit] = 1.0
    pair_field = np.arange(EMB * FPAD)
    same = (pair_field[:, None] % FPAD == pair_field[None, :ROWS * FPAD] % FPAD).astype(np.float32)
    rows_of = (np.arange(16)[:, None] == pair_field[None, :] // FPAD).astype(np.float32)
    cols_of = np.stack([
        (pair_field[:ROWS * FPAD, None] // FPAD + ROWS * part == np.arange(128)[None, :]).astype(np.float32) for part in range(2)
    ])
    constants = (
        np.concatenate([first, first], axis=1), np.concatenate([second, second], axis=1), first.T, second.T, place, place.T,
        same, rows_of, cols_of,
    )
    constants = [jnp.asarray(value, LOW) for value in constants]
    small_operands = (
        id_lists.transpose(1, 0, 2), id_counts, embed_rows.T, hidden,
        fieldwise, biases, readout.reshape(1, UDEV), logit_grad, squeezer.T, exciter,
        *constants, bilinear,
    )
    vmem = pl.BlockSpec(memory_space=pltpu.VMEM)
    hbm = pl.BlockSpec(memory_space=pltpu.HBM)
    anywhere = pl.BlockSpec(memory_space=pl.ANY)
    low = lambda *shape: pltpu.VMEM(shape, LOW)
    full = lambda *shape: pltpu.VMEM(shape, F32)
    dma = lambda *shape: pltpu.SemaphoreType.DMA(shape)
    return pl.pallas_call(
        step_kernel,
        out_shape=(
            pltpu.VMEM((2, TILES, 16, 128), LOW),
            jax.ShapeDtypeStruct((SMALL + 8, 128), F32),
            jax.ShapeDtypeStruct((EMB, FPAD, BATCH), LOW),
            jax.ShapeDtypeStruct((8, BATCH), F32),
        ) + (pltpu.VMEM(pair_set[0].shape, F32),) * 3,
        in_specs=[hbm] * 23,
        out_specs=(anywhere, vmem, vmem, vmem) + (vmem,) * 3,
        scratch_shapes=[
            pltpu.VMEM((FPAD, SLOTS, BATCH), jnp.int32),
            *(pltpu.VMEM(array.shape, array.dtype) for array in small_operands[1:-1]),
            pltpu.SMEM((EMB, EMB), F32),
            full(EMB, FPAD, BATCH), pltpu.VMEM((FPAD, BATCH), jnp.int32), pltpu.VMEM((EMB // 2, 8, 128), jnp.int32),
            low(ROWS, UNITS, PPAD), low(ROWS, PPAD, UNITS),
            low(ROWS, PPAD, BATCH), low(ROWS, PPAD, BATCH), low(ROWS, PPAD, BATCH), low(ROWS, HALF, BATCH),
            full(EMB, FPAD, BATCH), full(FPAD, BATCH), full(FPAD, BATCH), full(16, BATCH), full(FPAD, BATCH),
            full(16, 128), full(16, 128), full(EMB * FPAD, 128), low(EMB * FPAD, UNITS), low(UNITS, EMB * FPAD),
            low(2, UNITS, 512), full(8, 512), low(2, UNITS, UNITS), low(2, UNITS, UNITS),
            low(4 * ZROWS, BATCH), low(3, ZROWS, BATCH), low(4 * ZROWS, BATCH), low(UNITS, BATCH), low(UNITS, BATCH),
            low(TILES, 16, 128), low(2, 3, HALVES // 4, 16, 128), low(2, 3, HALVES // 16, 16, 128),
            low(2 * AUX, 16, 128), low(AUX, 16, 128),
            full(EMB, FPAD, BATCH), full(EMB, FPAD, BATCH),
            low(2, EMB * FPAD, 128), low(2, EMB * FPAD, 128), low(EMB * FPAD, 128), low(EMB * FPAD, 128),
            low(EMB * FPAD, 128), low(EMB * FPAD, 128),
            full(4, SMALL, 128), full(4, SMALL + 8, 128), full(4, SMALL + 8, 128), full(2, SMALL + 8, 128),
            dma(20), dma(3), dma(3), dma(3), dma(3), dma(3), dma(2), dma(2),
            dma(2, 3), dma(2, 3), dma(2, 3), dma(2, 3),
            dma(2), dma(2), dma(2, 2, 2, 3), dma(2, 2, 2, 3), dma(2, 2), dma(2, 2, 2, 3), dma(2, 2, 2, 3),
            dma(2, 2, 4), dma(2, 2, 4),
            dma(4), dma(4), dma(3), dma(3), dma(3), dma(3), dma(3), dma(3), dma(2),
        ],
        compiler_params=pltpu.CompilerParams(
            collective_id=0, has_side_effects=True, vmem_limit_bytes=32 * MIB
        ),
        name="step",
    )(*in_hbm(small_operands), *in_hbm(pair_set))


def update_kernel(grads, small, egrad, logit, weight, momentum, average, *refs):
    inputs, refs = refs[:24], refs[24:]
    logits_out, egrad_out = refs[:2]
    pair_outs, outputs, refs = refs[2:5], refs[5:29], refs[29:]
    held, refs = refs[:24], refs[24:]
    logits_held, egrad_held, pair_held, in_sem, out_sem, pair_sem = refs

    loads = [pltpu.make_async_copy(src, dst, in_sem.at[n]) for n, (src, dst) in enumerate(zip(inputs, held))]
    for copy in loads:
        copy.start()

    def put(which, at, grad, rate):
        weight, momentum, average = held[3 * which:3 * which + 3]
        values = nesterov(weight[at], momentum[at], average[at], grad, rate)
        for ref, value in zip((weight, momentum, average), values):
            ref[at] = value

    def small_ones():
        for copy in loads:
            copy.wait()
        tiles = slice(KTILES * ROWS, KTILES * ROWS + AUX)
        whole = jnp.concatenate([grads[0, tiles], grads[1, tiles]], axis=0).astype(F32).reshape(2 * AUX * 16, 128)
        for k in range(EMB):
            put(0, (k,), whole[FPAD * k:FPAD * k + FIELDS, 0:UDEV], RATE)
        for layer in range(2):
            put(1, (layer,), whole[UNITS * (layer + 1):UNITS * (layer + 2), 0:UDEV], RATE)
        everything = (slice(None), slice(None))
        offset_weight = held[12][...]
        put(2, everything, small[SMALL:SMALL + 3, 0:UDEV], FAST_RATE)
        put(3, everything, small[SMALL + 3:SMALL + 4, 0:UDEV], RATE)
        put(4, everything, small[15:16, 0:1], RATE)
        put(5, everything, small[0:EMB, 0:EMB], RATE)
        put(6, everything, small[16:16 + REDUCED, 0:FIELDS], FAST_RATE)
        put(7, everything, small[32:32 + REDUCED, 0:FIELDS], FAST_RATE)
        logits_held[...] = logit[3:4, :] + offset_weight
        for k in range(EMB):
            egrad_held[k] = egrad[k, :, :].astype(F32)[0:FIELDS]
        ends = zip((logits_held, egrad_held) + tuple(held), (logits_out, egrad_out) + tuple(outputs))
        ends = [pltpu.make_async_copy(src, dst, out_sem.at[n]) for n, (src, dst) in enumerate(ends)]
        for copy in ends:
            copy.start()
        return ends

    stores = []
    for k in range(ROWS):
        slot = k % BUFFERS
        if k >= BUFFERS:
            for copy in stores[3 * (k - BUFFERS):3 * (k - BUFFERS + 1)]:
                copy.wait()
        for c in range(2):
            for j in range(3):
                first = HALF * c + 128 * j
                last = min(first + 128, PAIRS)
                tiles = [grads[c, KTILES * k + 3 * r + j] for r in range(UNITS // 16)]
                grad = jnp.concatenate(tiles, axis=0).astype(F32)[:, 0:last - first]
                at = (k, slice(None), slice(first, last))
                values = nesterov(weight[at], momentum[at], average[at], grad, RATE)
                for n, value in enumerate(values):
                    pair_held[slot, n, :, first:last] = value
        for n in range(3):
            stores.append(pltpu.make_async_copy(pair_held.at[slot, n], pair_outs[n].at[k], pair_sem.at[slot, n]))
            stores[-1].start()
        if k == 1:
            lasts = small_ones()
    for copy in lasts + stores[3 * (ROWS - BUFFERS):]:
        copy.wait()


def update(grads, small, egrad, logit, sets):
    vmem = pl.BlockSpec(memory_space=pltpu.VMEM)
    hbm = pl.BlockSpec(memory_space=pltpu.HBM)
    pair, others = sets[0], [array for arrays in sets[1:] for array in arrays]
    shapes = [(1, BATCH), (EMB, FIELDS, BATCH)] + [array.shape for array in pair] + [array.shape for array in others]
    return pl.pallas_call(
        update_kernel,
        in_specs=[vmem] * 7 + [hbm] * 24,
        out_specs=[hbm] * 29,
        out_shape=[jax.ShapeDtypeStruct(shape, F32) for shape in shapes],
        scratch_shapes=[
            *(pltpu.VMEM(array.shape, F32) for array in others),
            pltpu.VMEM((1, BATCH), F32), pltpu.VMEM((EMB, FIELDS, BATCH), F32),
            pltpu.VMEM((BUFFERS, 3, UNITS, PAIRS), F32),
            pltpu.SemaphoreType.DMA((24,)), pltpu.SemaphoreType.DMA((26,)), pltpu.SemaphoreType.DMA((BUFFERS, 3)),
        ],
        compiler_params=pltpu.CompilerParams(vmem_limit_bytes=18 * MIB),
        name="update",
    )(grads, small, egrad, logit, *pair, *in_hbm(others[:12]), *others[12:15], *in_hbm(others[15:]))


def per_device(
    id_lists, id_counts, embed_rows, logit_grad,
    bilinear, bilinear_momentum, bilinear_average,
    squeezer, squeezer_momentum, squeezer_average,
    exciter, exciter_momentum, exciter_average,
    pairwise, pairwise_momentum, pairwise_average,
    fieldwise, fieldwise_momentum, fieldwise_average,
    hidden, hidden_momentum, hidden_average,
    biases, biases_momentum, biases_average,
    readout, readout_momentum, readout_average,
    offset, offset_momentum, offset_average,
):
    turn = lambda *arrays: tuple(array.swapaxes(-1, -2) for array in arrays)
    pair_set = turn(pairwise, pairwise_momentum, pairwise_average)
    grads, small, egrad, logit, *held = step(
        id_lists, id_counts, embed_rows, pair_set, fieldwise, hidden, biases, readout, logit_grad, bilinear, squeezer, exciter
    )
    row = lambda *arrays: tuple(array.reshape(1, -1) for array in arrays)
    outs = update(
        grads, small, egrad, logit,
        [
            held,
            (fieldwise, fieldwise_momentum, fieldwise_average),
            (hidden, hidden_momentum, hidden_average),
            (biases, biases_momentum, biases_average),
            row(readout, readout_momentum, readout_average),
            row(offset, offset_momentum, offset_average),
            (bilinear, bilinear_momentum, bilinear_average),
            turn(squeezer, squeezer_momentum, squeezer_average),
            (exciter, exciter_momentum, exciter_average),
        ],
    )
    logits, egrad_full = outs[0].reshape(-1), outs[1]
    pair, field, hid, bias, read, off, bil, squ, exc = (tuple(outs[2 + 3 * i:5 + 3 * i]) for i in range(9))
    flat = lambda arrays: tuple(array.reshape(-1) for array in arrays)
    return (logits, egrad_full) + bil + turn(*squ) + exc + turn(*pair) + field + hid + bias + flat(read) + flat(off)


def solution(mesh):
    whole = (P(),) * 3
    rows = (P("mp", None, None),) * 3
    units = (P(None, None, "mp"),) * 3
    vectors = (P(None, "mp"),) * 3
    line = (P("mp"),) * 3
    weights = whole + whole + whole + rows + units + units + vectors + line + whole
    return jax.shard_map(
        per_device,
        mesh=mesh,
        in_specs=(P(None, None, "dp"), P(None, "dp"), P("dp", None), P("dp")) + weights,
        out_specs=(P("dp"), P(None, None, "dp")) + weights,
        check_vma=False,
    )
```

```python
import jax
import jax.numpy as jnp
import numpy as np
from jax import lax
from jax.experimental import pallas as pl
from jax.experimental.pallas import tpu as pltpu
from jax.sharding import PartitionSpec as P

MOMENTUM = 0.9
RATE = 0.01
FAST_RATE = 0.05
DECAY = 0.8
HIGHEST = lax.Precision.HIGHEST
F32 = jnp.float32
LOW = jnp.bfloat16
MESH = pl.DeviceIdType.MESH
MIB = 1024 * 1024

EMB = 10
FIELDS = 39
FPAD = 40
REDUCED = 13
UNITS = 400
ZROWS = 112
ZPARTS = ((0, 64), (64, 48))
UDEV = 100
SLOTS = 8
BATCH = 256
FETCH = 1024
PAIRS = 741
PPAD = 768
HALF = 384
ROWS = 5
TILES = 416
HALVES = TILES // 2
CHUNKS = (112, 96)
KTILES = 75
BUFFERS = 3
AUX = 38
SMALL = 16
STEPS = 4095


def dot(left, right, contract, precision=None):
    return lax.dot_general(
        left, right, ((contract[0], contract[1]), ((), ())),
        precision=precision, preferred_element_type=F32,
    )


def nn(left, right, precision=None):
    return dot(left, right, ((1,), (0,)), precision)


def nt(left, right, precision=None):
    return dot(left, right, ((1,), (1,)), precision)


def tn(left, right, precision=None):
    return dot(left, right, ((0,), (0,)), precision)


def in_hbm(arrays):
    return tuple(pltpu.with_memory_space_constraint(array, pltpu.HBM) for array in arrays)


def nesterov(weight, momentum, average, grad, step_rate):
    velocity = MOMENTUM * momentum + grad
    updated = weight - step_rate * (grad + MOMENTUM * velocity)
    smoothed = DECAY * average + (1.0 - DECAY) * updated
    return (velocity, smoothed, updated)


def pool(ids_ref, count_ref, rows_ref, counts, table, out_ref, between):
    rows = rows_ref[...].astype(F32)
    largest = jnp.maximum(jnp.max(jnp.abs(rows), keepdims=True), 1e-30)
    fixed = jnp.round(rows * (STEPS / largest)).astype(jnp.int32) + (STEPS + 1)
    for chunk in range(8):
        part = fixed[:, 128 * chunk:128 * (chunk + 1)]
        for k in range(EMB // 2):
            table[k, chunk:chunk + 1, :] = part[2 * k:2 * k + 1, :] * 65536 + part[2 * k + 1:2 * k + 2, :]
    counts[0:FIELDS, :] = count_ref[...]
    counts[FIELDS:FPAD, :] = jnp.ones((1, BATCH), jnp.int32)
    ids_ref[FIELDS] = jnp.full((SLOTS, BATCH), 8 * FETCH, jnp.int32)
    sublane = lax.broadcasted_iota(jnp.int32, (8, 128), 0)
    unit = largest * (1.0 / STEPS)

    def group(g, carry):
        fields = pl.ds(pl.multiple_of(8 * g, 8), 8)
        for h in range(2):
            lanes = slice(128 * h, 128 * (h + 1))
            live = counts[fields, lanes]
            found = [[] for _ in range(EMB // 2)]
            for row in range(8):
                ids = jnp.where(live[row:row + 1, :] > sublane, ids_ref[8 * g + row, :, lanes], 8 * FETCH)
                totals = [None] * (EMB // 2)
                for slot in range(SLOTS):
                    wide = jnp.broadcast_to(ids[slot:slot + 1, :], (8, 128))
                    lane = wide & 127
                    hit = (wide >> 7) == sublane
                    for k in range(EMB // 2):
                        value = jnp.take_along_axis(table[k], lane, axis=1, mode="promise_in_bounds")
                        value = jnp.where(hit, value, 0)
                        totals[k] = value if totals[k] is None else totals[k] + value
                for k in range(EMB // 2):
                    found[k].append(jnp.sum(totals[k], axis=0, keepdims=True))
            factor = unit / live.astype(F32)
            for k in range(EMB // 2):
                both = jnp.concatenate(found[k], axis=0)
                for part, word in enumerate(((both >> 16) & 65535, both & 65535)):
                    total = (word - (STEPS + 1) * live).astype(F32)
                    out_ref[2 * k + part, fields, lanes] = (total * factor).astype(LOW).astype(F32)
        return carry

    lax.fori_loop(0, 2, group, 0)
    between()
    lax.fori_loop(2, FPAD // 8, group, 0)
    out_ref[:, FPAD - 8:FPAD, :] = jnp.where(
        lax.broadcasted_iota(jnp.int32, (EMB, 8, BATCH), 1) == 7, 0.0, out_ref[:, FPAD - 8:FPAD, :]
    )


def gate_of(before):
    return 0.5 + 0.5 * jnp.tanh(0.5 * before)


def silu_slope(before, gate):
    return gate * (1.0 + before * (1.0 - gate))


def softplus(value):
    return jnp.maximum(value, 0.0) + jnp.log1p(jnp.exp(-jnp.abs(value)))


def two_terms(value):
    high = value.astype(LOW)
    return high, (value - high.astype(F32)).astype(LOW)


def split(value):
    high = value.astype(LOW).astype(F32)
    return jnp.concatenate([high, value - high], axis=0).astype(LOW)


def step_kernel(*refs):
    hbm, pairs_in, refs = refs[:20], refs[20:23], refs[23:]
    gout_ref, small_ref, egrad_ref, logit_ref, *pairs_out = refs[:7]
    loaded, refs = refs[7:27], refs[27:]
    pair_ref = pairs_out[0]
    (
        ids_ref, count_ref, rows_ref, hidden_ref,
        field_ref, bias_ref, readout_ref, grad_ref, squ_ref, exc_ref,
        first_ref, second_ref, first_t_ref, second_t_ref, place_ref, place_t_ref, same_ref, rows_of_ref, cols_of_ref, bil_ref,
    ) = loaded
    (
        emb_ref, counts, table, w_low, w_turned, left, right, feats, feats_peer, source, scale_s, sq_s, z1_s, z2_s,
        squ_pad, exc_pad, fpad, fplaced, fplaced_t, hid_all, vec_all, hid_full, hid_turned,
        pre_part, rs_in, pre_full, gf, gf_peer,
        acc, box1, box2, aux, aux_in,
        dsrc, eterm, zsend, zrecv, zsend2, zrecv2, zsend3, zrecv3, small_z, small_x, small_y, small_c,
        load_sem, pair_sem, hid_send, hid_recv, vec_send, vec_recv, twin_sem, feat_sem,
        rsz_send, rsz_recv, agz_send, agz_recv,
        gf_sem, aux_sem, red_send, red_recv, own_sem, gat_send, gat_recv, core_send, core_recv,
        zs_send, zs_recv, smz_send, smz_recv, smx_send, smx_recv, smy_send, smy_recv, smc_sem,
    ) = refs
    dp = lax.axis_index("dp")
    me = lax.axis_index("mp")
    core = dp % 2
    yy = (dp // 2) % 4
    xx = dp // 8

    def at_dp(x, y, c):
        return (x * 4 + y) * 2 + c

    rings = (
        [((xx + off) % 4, at_dp((xx + off) % 4, yy, core)) for off in (1, 3, 2)],
        [((yy + off) % 4, at_dp(xx, (yy + off) % 4, core)) for off in (1, 3, 2)],
    )
    places = (xx, yy)
    twin = at_dp(xx, yy, 1 - core)
    peers = [(me + off) % 4 for off in (1, 3, 2)]
    stream = me // 2
    columns = (me % 2) * ROWS
    half = ((me + 1) // 2) % 2
    near = me + 1 - 2 * (me % 2)
    cross = 3 - me

    def remote(src, dst, send, recv, **where):
        return pltpu.make_async_remote_copy(
            src_ref=src, dst_ref=dst, send_sem=send, recv_sem=recv, device_id=where, device_id_type=MESH
        )

    targets = (ids_ref.at[pl.ds(0, FIELDS)],) + loaded[1:]
    loads = [pltpu.make_async_copy(src, dst, load_sem.at[n]) for n, (src, dst) in enumerate(zip(hbm, targets))]
    for copy in loads:
        copy.start()
    pair_loads = [
        pltpu.make_async_copy(src, dst, pair_sem.at[n]) for n, (src, dst) in enumerate(zip(pairs_in, pairs_out))
    ]
    for copy in pair_loads:
        copy.start()
    barrier = pltpu.get_barrier_semaphore()
    for peer in peers:
        pl.semaphore_signal(barrier, inc=1, device_id={"mp": peer}, device_id_type=MESH)
    for dev in [dev for ring in rings for _, dev in ring] + [twin]:
        pl.semaphore_signal(barrier, inc=1, device_id={"dp": dev}, device_id_type=MESH)

    lanes_me = pl.ds(pl.multiple_of(128 * me, 128), 128)
    hid_copies = []
    for n, peer in enumerate(peers):
        mine = hid_all.at[core, :, lanes_me]
        hid_copies.append(remote(mine, mine, hid_send.at[n], hid_recv.at[n], mp=peer))
        mine = vec_all.at[:, lanes_me]
        hid_copies.append(remote(mine, mine, vec_send.at[n], vec_recv.at[n], mp=peer))

    def share_hidden():
        for copy in loads[3:]:
            copy.wait()
        fpad[...] = jnp.zeros_like(fpad)
        fpad[:, 0:UDEV] = hidden_ref[core]
        hid_all[core, :, lanes_me] = fpad[...].astype(LOW)
        fpad[0:8, :] = jnp.zeros((8, 128), F32)
        fpad[0:3, 0:UDEV] = bias_ref[...]
        fpad[3:4, 0:UDEV] = readout_ref[...].astype(LOW).astype(F32)
        vec_all[:, lanes_me] = fpad[0:8, :]
        pl.semaphore_wait(barrier, 10)
        for copy in hid_copies:
            copy.start()

    for copy in loads[:3]:
        copy.wait()
    pool(ids_ref, count_ref, rows_ref, counts, table, emb_ref, share_hidden)

    squ_pad[...] = jnp.zeros_like(squ_pad)
    squ_pad[0:REDUCED, 0:FIELDS] = squ_ref[...]
    exc_pad[...] = jnp.zeros_like(exc_pad)
    exc_pad[0:REDUCED, 0:FIELDS] = exc_ref[...]
    squeezer = squ_pad[:, 0:FPAD]
    exciter = exc_pad[:, 0:FPAD]
    emb = emb_ref[...]
    squeezed = jnp.sum(emb, axis=0) * (1.0 / EMB)
    z1 = nn(squeezer, squeezed, HIGHEST)
    z2 = tn(exciter, z1 * gate_of(z1), HIGHEST)
    scales = softplus(z2)
    sq_s[...] = squeezed
    z1_s[...] = z1
    z2_s[...] = z2
    scale_s[...] = scales
    factor = jnp.where(stream == 0, jnp.ones_like(scales), scales)
    for k in range(EMB):
        source[k] = emb_ref[k] * factor

    for k in range(ROWS):
        projected = source[0] * bil_ref[0, columns + k]
        for l in range(1, EMB):
            projected = projected + source[l] * bil_ref[l, columns + k]
        left_k = nn(first_ref[...], split(projected))
        right_k = nn(second_ref[...], split(source[columns + k]))
        left[k] = left_k.astype(LOW)
        right[k] = right_k.astype(LOW)
        feats[k] = (left_k * right_k).astype(LOW)
    feat_copy = remote(
        feats.at[:, pl.ds(pl.multiple_of(HALF * (1 - core), HALF), HALF), :], feats_peer,
        feat_sem.at[0], feat_sem.at[1], dp=twin,
    )
    feat_copy.start()
    fpad[0:8, :] = jnp.zeros((8, 128), F32)
    for k in range(EMB):
        fpad[FPAD * k:FPAD * k + FIELDS, 0:UDEV] = field_ref[k]
        fpad[FPAD * k + FIELDS:FPAD * (k + 1), :] = jnp.zeros((1, 128), F32)
    field_low = fpad[...].astype(LOW)
    place_own = place_ref[lanes_me, :]
    fplaced_t[...] = nt(place_t_ref[:, lanes_me], field_low).astype(LOW)
    emb_low = emb.reshape(EMB * FPAD, BATCH).astype(LOW)
    pre = nn(fplaced_t[...], emb_low)
    pair_loads[0].wait()
    for k in range(ROWS):
        w_low[k, :, 640:PPAD] = jnp.zeros((UNITS, PPAD - 640), LOW)
        w_low[k, :, 0:PAIRS] = pair_ref[k].astype(LOW)
        pre = pre + nn(w_low[k], feats[k])
    pre_part[0:UNITS, :] = pre.astype(LOW)
    pre_part[UNITS:4 * ZROWS, :] = jnp.zeros((4 * ZROWS - UNITS, BATCH), LOW)

    rs_copies = []
    for part, (low_row, count) in enumerate(ZPARTS):
        for n, peer in enumerate(peers):
            rows = pl.ds(pl.multiple_of(ZROWS * peer + low_row, 16), count)
            box = rs_in.at[n, pl.ds(low_row, count)]
            rs_copies.append(remote(pre_part.at[rows], box, rsz_send.at[part, n], rsz_recv.at[part, n], mp=peer))
            rs_copies[-1].start()
    for copy in hid_copies:
        copy.wait()
    layer = hid_all.at[core]
    hid_twin = remote(layer, layer, twin_sem.at[0], twin_sem.at[1], dp=twin)
    hid_twin.start()
    fplaced[...] = nn(field_low, place_own).astype(LOW)
    ag_copies = []
    for part, (low_row, count) in enumerate(ZPARTS):
        for copy in rs_copies[3 * part:3 * part + 3]:
            copy.wait()
        own_rows = pl.ds(pl.multiple_of(ZROWS * me + low_row, 16), count)
        total = pre_part[own_rows, :].astype(F32)
        for n in range(3):
            total = total + rs_in[n, low_row:low_row + count].astype(F32)
        pre_full[own_rows, :] = total.astype(LOW)
        mine = pre_full.at[own_rows]
        for n, peer in enumerate(peers):
            ag_copies.append(remote(mine, mine, agz_send.at[part, n], agz_recv.at[part, n], mp=peer))
            ag_copies[-1].start()

    hid_twin.wait()
    for layer in range(2):
        hid_full[layer] = nn(hid_all[layer], place_ref[...]).astype(LOW)
        hid_turned[layer] = nt(place_t_ref[...], hid_all[layer]).astype(LOW)
    vec_rows = nn(vec_all[...], place_ref[...].astype(F32), HIGHEST)
    vec_cols = nt(place_t_ref[...].astype(F32), vec_all[...], HIGHEST)
    for copy in ag_copies:
        copy.wait()

    pre_first = pre_full[0:UNITS, :].astype(F32) + vec_cols[:, 0:1]
    gate_first = gate_of(pre_first)
    act_first = (pre_first * gate_first).astype(LOW)
    pre_second = nn(hid_turned[0], act_first) + vec_cols[:, 1:2]
    gate_second = gate_of(pre_second)
    act_second = (pre_second * gate_second).astype(LOW)
    pre_third = nn(hid_turned[1], act_second) + vec_cols[:, 2:3]
    gate_third = gate_of(pre_third)
    act_third = (pre_third * gate_third).astype(LOW)
    upstream = grad_ref[...].astype(F32).reshape(1, BATCH)
    grad_third = ((vec_cols[:, 3:4] * upstream) * silu_slope(pre_third, gate_third)).astype(LOW)
    grad_second = (nn(hid_full[1], grad_third) * silu_slope(pre_second, gate_second)).astype(LOW)
    grad_first = (nn(hid_full[0], grad_second) * silu_slope(pre_first, gate_first)).astype(LOW)
    gf[...] = grad_first
    gf_copy = remote(gf, gf_peer, gf_sem.at[0], gf_sem.at[1], dp=twin)
    gf_copy.start()

    first_mine = nn(place_own, grad_first).astype(LOW)
    second_mine = nn(place_own, grad_second).astype(LOW)
    third_mine = nn(place_own, grad_third).astype(LOW)
    aux[0:25] = nt(emb_low, first_mine).astype(LOW).reshape(25, 16, 128)
    aux[25:50] = nt(act_first, second_mine).astype(LOW).reshape(25, 16, 128)
    aux[50:75] = nt(act_second, third_mine).astype(LOW).reshape(25, 16, 128)
    aux[75] = jnp.zeros((16, 128), LOW)
    aux_copy = remote(
        aux.at[pl.ds(AUX * (1 - core), AUX)], aux_in, aux_sem.at[0], aux_sem.at[1], dp=twin
    )
    aux_copy.start()

    feat_copy.wait()
    own_half = pl.ds(pl.multiple_of(HALF * core, HALF), HALF)
    gf_copy.wait()
    for k in range(ROWS):
        grad = (nt(gf[...], feats[k, own_half, :]) + nt(gf_peer[...], feats_peer[k])).astype(LOW)
        tiles = [grad[:, 128 * j:128 * (j + 1)].reshape(25, 16, 128) for j in range(3)]
        acc[KTILES * k:KTILES * (k + 1)] = jnp.stack(tiles, axis=1).reshape(KTILES, 16, 128)
    acc[KTILES * ROWS + AUX:TILES] = jnp.zeros((TILES - KTILES * ROWS - AUX, 16, 128), LOW)

    offsets = (0, CHUNKS[0])
    starts = [[HALVES * h + offsets[c] for c in range(2)] for h in range(2)]

    def size_of(t, c):
        return CHUNKS[c] // (4, 16)[t]

    def box_of(t, h, n, c):
        return (box1, box2)[t].at[h, n, pl.ds(offsets[c] // (4, 16)[t], size_of(t, c))]

    def reduce_send(t, c):
        size = size_of(t, c)
        copies = []
        for n in range(3):
            for h in range(2):
                place, dev = rings[(h + t) % 2][n]
                src = acc.at[pl.ds(starts[h][c] + place * size, size)]
                copies.append(
                    remote(src, box_of(t, h, n, c), red_send.at[t, h, c, n], red_recv.at[t, h, c, n], dp=dev)
                )
                copies[-1].start()
        for h in range(2):
            starts[h][c] = starts[h][c] + places[(h + t) % 2] * size
        return copies

    def reduce_add(t, c, copies):
        for copy in copies:
            copy.wait()
        for h in range(2):
            keep = pl.ds(starts[h][c], size_of(t, c))
            total = acc[keep].astype(F32)
            for n in range(3):
                total = total + box_of(t, h, n, c)[...].astype(F32)
            acc[keep] = total.astype(LOW)

    own_copies = []
    core_copies = []

    def pass_on(h, c, slot, start, count):
        where = gout_ref.at[core, pl.ds(start, count)]
        copy = remote(where, where, core_send.at[h, c, slot], core_recv.at[h, c, slot], dp=twin)
        copy.start()
        core_copies.append(copy)

    def gather_send(t, c):
        size = size_of(t, c)
        copies = []
        for n in range(3):
            for h in range(2):
                _, dev = rings[(h + t) % 2][n]
                where = gout_ref.at[core, pl.ds(starts[h][c], size)]
                src = acc.at[pl.ds(starts[h][c], size)] if t == 1 else where
                copy = remote(src, where, gat_send.at[t, h, c, n], gat_recv.at[t, h, c, n], dp=dev)
                copy.start()
                sender = rings[(h + t) % 2][(1, 0, 2)[n]][0]
                came = starts[h][c] + (sender - places[(h + t) % 2]) * size
                copies.append((copy, h, n, came))
        for h in range(2):
            if t == 1:
                where = pl.ds(starts[h][c], size)
                own = pltpu.make_async_copy(acc.at[where], gout_ref.at[core, where], own_sem.at[h, c])
                own.start()
                own_copies.append(own)
            starts[h][c] = starts[h][c] - places[(h + t) % 2] * size
        return copies

    def gather_wide(c, copies):
        for copy, _, _, _ in copies:
            copy.wait()
        for own in own_copies[2 * c:2 * c + 2]:
            own.wait()
        wide = gather_send(0, c)
        for h in range(2):
            pass_on(h, c, 3, starts[h][c] + places[h] * size_of(0, c), size_of(0, c))
        return wide

    def gather_end(c, copies):
        for copy, h, n, came in copies:
            copy.wait()
            pass_on(h, c, n, came, size_of(0, c))

    moving = [reduce_send(0, 0)]
    aux_copy.wait()
    aux_mine = aux[pl.ds(AUX * core, AUX)].astype(F32) + aux_in[...].astype(F32)
    acc[KTILES * ROWS:KTILES * ROWS + AUX] = aux_mine.astype(LOW)
    moving.append(reduce_send(0, 1))
    act_mine = nn(place_own, act_third).astype(LOW)
    ones = jnp.ones((16, BATCH), LOW)
    upstream_rows = jnp.broadcast_to(upstream, (16, BATCH)).astype(LOW)
    row_iota = lax.broadcasted_iota(jnp.int32, (16, 128), 0)
    vec_grads = jnp.where(row_iota == 0, nt(ones, first_mine), 0.0)
    vec_grads = vec_grads + jnp.where(row_iota == 1, nt(ones, second_mine), 0.0)
    vec_grads = vec_grads + jnp.where(row_iota == 2, nt(ones, third_mine), 0.0)
    vec_grads = vec_grads + jnp.where(row_iota == 3, nt(upstream_rows, act_mine), 0.0)

    dprojected = []
    dchosen = []
    for k in range(ROWS):
        w_turned[k] = jnp.transpose(w_low[k])
        dfeat = nn(w_turned[k], gf[...])
        dprojected.append(nn(first_t_ref[...], (dfeat * right[k].astype(F32)).astype(LOW)))
        dchosen.append(nn(second_t_ref[...], (dfeat * left[k].astype(F32)).astype(LOW)))
    for l in range(EMB):
        total = dprojected[0] * bil_ref[l, columns]
        for k in range(1, ROWS):
            total = total + dprojected[k] * bil_ref[l, columns + k]
        dsrc[l] = total
    for k in range(ROWS):
        dsrc[columns + k] = dsrc[columns + k] + dchosen[k]
    eterm[...] = nn(fplaced[...], gf[...]).reshape(EMB, FPAD, BATCH)
    lanes_away = pl.ds(pl.multiple_of(128 * (1 - half), 128), 128)
    lanes_own = pl.ds(pl.multiple_of(128 * half, 128), 128)
    zsend[0] = dsrc[:, :, lanes_away].reshape(EMB * FPAD, 128).astype(LOW)
    zsend[1] = eterm[:, :, lanes_away].reshape(EMB * FPAD, 128).astype(LOW)
    z_copies = [remote(zsend.at[n], zrecv.at[n], zs_send.at[n], zs_recv.at[n], mp=near) for n in range(2)]
    for copy in z_copies:
        copy.start()
    source_high, source_rest = two_terms(source[...].reshape(EMB * FPAD, BATCH))
    dproj_high, dproj_rest = two_terms(jnp.concatenate(dprojected, axis=0))
    products = nt(source_high, dproj_high) + nt(source_high, dproj_rest) + nt(source_rest, dproj_high)
    products = products * same_ref[...].astype(F32)
    bil_rows = nn(nn(rows_of_ref[...].astype(F32), products, HIGHEST), cols_of_ref[me % 2].astype(F32), HIGHEST)
    bil_rows = jnp.where(row_iota == 15, jnp.sum(upstream) * 0.25, bil_rows)
    reduce_add(0, 0, moving[0])
    moving[0] = reduce_send(1, 0)

    z_copies[0].wait()
    back = dsrc[:, :, lanes_own] + zrecv[0].astype(F32).reshape(EMB, FPAD, 128)
    emb_half = emb_ref[:, :, lanes_own]
    z1 = z1_s[:, lanes_own]
    z2 = z2_s[:, lanes_own]
    dscale = jnp.sum(back * emb_half, axis=0)
    dz2 = dscale * gate_of(z2)
    gate = gate_of(z1)
    dexciter = nt(z1 * gate, dz2, HIGHEST)
    dz1 = nn(exciter, dz2, HIGHEST) * silu_slope(z1, gate)
    dsqueezer = nt(dz1, sq_s[:, lanes_own], HIGHEST)
    weighted = jnp.where(stream == 0, jnp.zeros((1, 1), F32), jnp.ones((1, 1), F32))

    small_z[me] = jnp.concatenate([dsqueezer * weighted, dexciter * weighted, bil_rows[:, 0:128 - 2 * FPAD]], axis=1)
    small = []
    for n, peer in enumerate(peers):
        small.append(remote(small_z.at[me], small_z.at[me], smz_send.at[n], smz_recv.at[n], mp=peer))
        small[n].start()
    dsqueezed = tn(squeezer, dz1, HIGHEST) * (1.0 / EMB)
    through = back * scale_s[:, lanes_own][None] + dsqueezed[None]
    z_copies[1].wait()
    term = eterm[:, :, lanes_own] + zrecv[1].astype(F32).reshape(EMB, FPAD, 128)
    mine = term + jnp.where(stream == 0, back, through)
    zsend2[...] = mine.reshape(EMB * FPAD, 128).astype(LOW)
    z_copy = remote(zsend2, zrecv2, zs_send.at[2], zs_recv.at[2], mp=cross)
    z_copy.start()

    reduce_add(0, 1, moving[1])
    moving[1] = reduce_send(1, 1)
    for copy in small:
        copy.wait()
    small_x[xx, 0:SMALL] = small_z[0] + small_z[1] + small_z[2] + small_z[3]
    small_x[xx, SMALL:SMALL + 8] = vec_grads[0:8]
    small = []
    for n, (_, dev) in enumerate(rings[0]):
        small.append(remote(small_x.at[xx], small_x.at[xx], smx_send.at[n], smx_recv.at[n], dp=dev))
        small[n].start()
    reduce_add(1, 0, moving[0])
    moving[0] = gather_send(1, 0)
    reduce_add(1, 1, moving[1])
    moving[1] = gather_send(1, 1)
    for copy in small:
        copy.wait()
    small_y[yy] = small_x[0] + small_x[1] + small_x[2] + small_x[3]
    small = []
    for n, (_, dev) in enumerate(rings[1]):
        small.append(remote(small_y.at[yy], small_y.at[yy], smy_send.at[n], smy_recv.at[n], dp=dev))
        small[n].start()
    moving[0] = gather_wide(0, moving[0])
    moving[1] = gather_wide(1, moving[1])
    logit_ref[...] = nn(vec_rows.astype(LOW), act_third)
    z_copy.wait()
    whole = (zsend2[...].astype(F32) + zrecv2[...].astype(F32)).astype(LOW)
    zsend3[...] = whole
    z_copy = remote(zsend3, zrecv3, zs_send.at[3], zs_recv.at[3], mp=near)
    z_copy.start()
    egrad_ref[:, :, lanes_own] = whole.reshape(EMB, FPAD, 128)
    gather_end(0, moving[0])
    for copy in small:
        copy.wait()
    small_c[core] = small_y[0] + small_y[1] + small_y[2] + small_y[3]
    small = remote(small_c.at[core], small_c.at[core], smc_sem.at[0], smc_sem.at[1], dp=twin)
    small.start()
    z_copy.wait()
    egrad_ref[:, :, lanes_away] = zrecv3[...].reshape(EMB, FPAD, 128)
    gather_end(1, moving[1])
    small.wait()
    small_ref[...] = small_c[0] + small_c[1]
    for copy in core_copies + pair_loads[1:]:
        copy.wait()


def step(id_lists, id_counts, embed_rows, pair_set, fieldwise, hidden, biases, readout, logit_grad, bilinear, squeezer, exciter):
    first_index, second_index = np.triu_indices(FIELDS, 1)
    first = np.zeros((PPAD, FPAD), np.float32)
    second = np.zeros((PPAD, FPAD), np.float32)
    first[np.arange(PAIRS), first_index] = 1.0
    second[np.arange(PAIRS), second_index] = 1.0
    place = np.zeros((512, UNITS), np.float32)
    unit = np.arange(UNITS)
    place[128 * (unit // UDEV) + unit % UDEV, unit] = 1.0
    pair_field = np.arange(EMB * FPAD)
    same = (pair_field[:, None] % FPAD == pair_field[None, :ROWS * FPAD] % FPAD).astype(np.float32)
    rows_of = (np.arange(16)[:, None] == pair_field[None, :] // FPAD).astype(np.float32)
    cols_of = np.stack([
        (pair_field[:ROWS * FPAD, None] // FPAD + ROWS * part == np.arange(128)[None, :]).astype(np.float32) for part in range(2)
    ])
    constants = (
        np.concatenate([first, first], axis=1), np.concatenate([second, second], axis=1), first.T, second.T, place, place.T,
        same, rows_of, cols_of,
    )
    constants = [jnp.asarray(value, LOW) for value in constants]
    small_operands = (
        id_lists.transpose(1, 0, 2), id_counts, embed_rows.T, hidden,
        fieldwise, biases, readout.reshape(1, UDEV), logit_grad, squeezer.T, exciter,
        *constants, bilinear,
    )
    vmem = pl.BlockSpec(memory_space=pltpu.VMEM)
    hbm = pl.BlockSpec(memory_space=pltpu.HBM)
    anywhere = pl.BlockSpec(memory_space=pl.ANY)
    low = lambda *shape: pltpu.VMEM(shape, LOW)
    full = lambda *shape: pltpu.VMEM(shape, F32)
    dma = lambda *shape: pltpu.SemaphoreType.DMA(shape)
    return pl.pallas_call(
        step_kernel,
        out_shape=(
            pltpu.VMEM((2, TILES, 16, 128), LOW),
            jax.ShapeDtypeStruct((SMALL + 8, 128), F32),
            jax.ShapeDtypeStruct((EMB, FPAD, BATCH), LOW),
            jax.ShapeDtypeStruct((8, BATCH), F32),
        ) + (pltpu.VMEM(pair_set[0].shape, F32),) * 3,
        in_specs=[hbm] * 23,
        out_specs=(anywhere, vmem, vmem, vmem) + (vmem,) * 3,
        scratch_shapes=[
            pltpu.VMEM((FPAD, SLOTS, BATCH), jnp.int32),
            *(pltpu.VMEM(array.shape, array.dtype) for array in small_operands[1:-1]),
            pltpu.SMEM((EMB, EMB), F32),
            full(EMB, FPAD, BATCH), pltpu.VMEM((FPAD, BATCH), jnp.int32), pltpu.VMEM((EMB // 2, 8, 128), jnp.int32),
            low(ROWS, UNITS, PPAD), low(ROWS, PPAD, UNITS),
            low(ROWS, PPAD, BATCH), low(ROWS, PPAD, BATCH), low(ROWS, PPAD, BATCH), low(ROWS, HALF, BATCH),
            full(EMB, FPAD, BATCH), full(FPAD, BATCH), full(FPAD, BATCH), full(16, BATCH), full(FPAD, BATCH),
            full(16, 128), full(16, 128), full(EMB * FPAD, 128), low(EMB * FPAD, UNITS), low(UNITS, EMB * FPAD),
            low(2, UNITS, 512), full(8, 512), low(2, UNITS, UNITS), low(2, UNITS, UNITS),
            low(4 * ZROWS, BATCH), low(3, ZROWS, BATCH), low(4 * ZROWS, BATCH), low(UNITS, BATCH), low(UNITS, BATCH),
            low(TILES, 16, 128), low(2, 3, HALVES // 4, 16, 128), low(2, 3, HALVES // 16, 16, 128),
            low(2 * AUX, 16, 128), low(AUX, 16, 128),
            full(EMB, FPAD, BATCH), full(EMB, FPAD, BATCH),
            low(2, EMB * FPAD, 128), low(2, EMB * FPAD, 128), low(EMB * FPAD, 128), low(EMB * FPAD, 128),
            low(EMB * FPAD, 128), low(EMB * FPAD, 128),
            full(4, SMALL, 128), full(4, SMALL + 8, 128), full(4, SMALL + 8, 128), full(2, SMALL + 8, 128),
            dma(20), dma(3), dma(3), dma(3), dma(3), dma(3), dma(2), dma(2),
            dma(2, 3), dma(2, 3), dma(2, 3), dma(2, 3),
            dma(2), dma(2), dma(2, 2, 2, 3), dma(2, 2, 2, 3), dma(2, 2), dma(2, 2, 2, 3), dma(2, 2, 2, 3),
            dma(2, 2, 4), dma(2, 2, 4),
            dma(4), dma(4), dma(3), dma(3), dma(3), dma(3), dma(3), dma(3), dma(2),
        ],
        compiler_params=pltpu.CompilerParams(
            collective_id=0, has_side_effects=True, vmem_limit_bytes=32 * MIB
        ),
        name="step",
    )(*in_hbm(small_operands), *in_hbm(pair_set))


def update_kernel(grads, small, egrad, logit, weight, momentum, average, *refs):
    inputs, refs = refs[:24], refs[24:]
    logits_out, egrad_out = refs[:2]
    pair_outs, outputs, refs = refs[2:5], refs[5:29], refs[29:]
    held, refs = refs[:24], refs[24:]
    logits_held, egrad_held, pair_held, in_sem, out_sem, pair_sem = refs

    loads = [pltpu.make_async_copy(src, dst, in_sem.at[n]) for n, (src, dst) in enumerate(zip(inputs, held))]
    for copy in loads:
        copy.start()

    def put(which, at, grad, rate):
        weight, momentum, average = held[3 * which:3 * which + 3]
        values = nesterov(weight[at], momentum[at], average[at], grad, rate)
        for ref, value in zip((weight, momentum, average), values):
            ref[at] = value

    def small_ones():
        for copy in loads:
            copy.wait()
        tiles = slice(KTILES * ROWS, KTILES * ROWS + AUX)
        whole = jnp.concatenate([grads[0, tiles], grads[1, tiles]], axis=0).astype(F32).reshape(2 * AUX * 16, 128)
        for k in range(EMB):
            put(0, (k,), whole[FPAD * k:FPAD * k + FIELDS, 0:UDEV], RATE)
        for layer in range(2):
            put(1, (layer,), whole[UNITS * (layer + 1):UNITS * (layer + 2), 0:UDEV], RATE)
        everything = (slice(None), slice(None))
        offset_weight = held[12][...]
        put(2, everything, small[SMALL:SMALL + 3, 0:UDEV], FAST_RATE)
        put(3, everything, small[SMALL + 3:SMALL + 4, 0:UDEV], RATE)
        put(4, everything, small[15:16, 2 * FPAD:2 * FPAD + 1], RATE)
        put(5, everything, small[0:EMB, 2 * FPAD:2 * FPAD + EMB], RATE)
        put(6, everything, small[0:REDUCED, 0:FIELDS], FAST_RATE)
        put(7, everything, small[0:REDUCED, FPAD:FPAD + FIELDS], FAST_RATE)
        logits_held[...] = logit[3:4, :] + offset_weight
        for k in range(EMB):
            egrad_held[k] = egrad[k, :, :].astype(F32)[0:FIELDS]
        ends = zip((logits_held, egrad_held) + tuple(held), (logits_out, egrad_out) + tuple(outputs))
        ends = [pltpu.make_async_copy(src, dst, out_sem.at[n]) for n, (src, dst) in enumerate(ends)]
        for copy in ends:
            copy.start()
        return ends

    stores = []
    for k in range(ROWS):
        slot = k % BUFFERS
        if k >= BUFFERS:
            for copy in stores[3 * (k - BUFFERS):3 * (k - BUFFERS + 1)]:
                copy.wait()
        for c in range(2):
            for j in range(3):
                first = HALF * c + 128 * j
                last = min(first + 128, PAIRS)
                tiles = [grads[c, KTILES * k + 3 * r + j] for r in range(UNITS // 16)]
                grad = jnp.concatenate(tiles, axis=0).astype(F32)[:, 0:last - first]
                at = (k, slice(None), slice(first, last))
                values = nesterov(weight[at], momentum[at], average[at], grad, RATE)
                for n, value in enumerate(values):
                    pair_held[slot, n, :, first:last] = value
        for n in range(3):
            stores.append(pltpu.make_async_copy(pair_held.at[slot, n], pair_outs[n].at[k], pair_sem.at[slot, n]))
            stores[-1].start()
        if k == 1:
            lasts = small_ones()
    for copy in lasts + stores[3 * (ROWS - BUFFERS):]:
        copy.wait()


def update(grads, small, egrad, logit, sets):
    vmem = pl.BlockSpec(memory_space=pltpu.VMEM)
    hbm = pl.BlockSpec(memory_space=pltpu.HBM)
    pair, others = sets[0], [array for arrays in sets[1:] for array in arrays]
    shapes = [(1, BATCH), (EMB, FIELDS, BATCH)] + [array.shape for array in pair] + [array.shape for array in others]
    return pl.pallas_call(
        update_kernel,
        in_specs=[vmem] * 7 + [hbm] * 24,
        out_specs=[hbm] * 29,
        out_shape=[jax.ShapeDtypeStruct(shape, F32) for shape in shapes],
        scratch_shapes=[
            *(pltpu.VMEM(array.shape, F32) for array in others),
            pltpu.VMEM((1, BATCH), F32), pltpu.VMEM((EMB, FIELDS, BATCH), F32),
            pltpu.VMEM((BUFFERS, 3, UNITS, PAIRS), F32),
            pltpu.SemaphoreType.DMA((24,)), pltpu.SemaphoreType.DMA((26,)), pltpu.SemaphoreType.DMA((BUFFERS, 3)),
        ],
        compiler_params=pltpu.CompilerParams(vmem_limit_bytes=18 * MIB),
        name="update",
    )(grads, small, egrad, logit, *pair, *in_hbm(others[:12]), *others[12:15], *in_hbm(others[15:]))


def per_device(
    id_lists, id_counts, embed_rows, logit_grad,
    bilinear, bilinear_momentum, bilinear_average,
    squeezer, squeezer_momentum, squeezer_average,
    exciter, exciter_momentum, exciter_average,
    pairwise, pairwise_momentum, pairwise_average,
    fieldwise, fieldwise_momentum, fieldwise_average,
    hidden, hidden_momentum, hidden_average,
    biases, biases_momentum, biases_average,
    readout, readout_momentum, readout_average,
    offset, offset_momentum, offset_average,
):
    turn = lambda *arrays: tuple(array.swapaxes(-1, -2) for array in arrays)
    pair_set = turn(pairwise, pairwise_momentum, pairwise_average)
    grads, small, egrad, logit, *held = step(
        id_lists, id_counts, embed_rows, pair_set, fieldwise, hidden, biases, readout, logit_grad, bilinear, squeezer, exciter
    )
    row = lambda *arrays: tuple(array.reshape(1, -1) for array in arrays)
    outs = update(
        grads, small, egrad, logit,
        [
            held,
            (fieldwise, fieldwise_momentum, fieldwise_average),
            (hidden, hidden_momentum, hidden_average),
            (biases, biases_momentum, biases_average),
            row(readout, readout_momentum, readout_average),
            row(offset, offset_momentum, offset_average),
            (bilinear, bilinear_momentum, bilinear_average),
            turn(squeezer, squeezer_momentum, squeezer_average),
            (exciter, exciter_momentum, exciter_average),
        ],
    )
    logits, egrad_full = outs[0].reshape(-1), outs[1]
    pair, field, hid, bias, read, off, bil, squ, exc = (tuple(outs[2 + 3 * i:5 + 3 * i]) for i in range(9))
    flat = lambda arrays: tuple(array.reshape(-1) for array in arrays)
    return (logits, egrad_full) + bil + turn(*squ) + exc + turn(*pair) + field + hid + bias + flat(read) + flat(off)


def solution(mesh):
    whole = (P(),) * 3
    rows = (P("mp", None, None),) * 3
    units = (P(None, None, "mp"),) * 3
    vectors = (P(None, "mp"),) * 3
    line = (P("mp"),) * 3
    weights = whole + whole + whole + rows + units + units + vectors + line + whole
    return jax.shard_map(
        per_device,
        mesh=mesh,
        in_specs=(P(None, None, "dp"), P(None, "dp"), P("dp", None), P("dp")) + weights,
        out_specs=(P("dp"), P(None, None, "dp")) + weights,
        check_vma=False,
    )
```

```python
import jax
import jax.numpy as jnp
import numpy as np
from jax import lax
from jax.experimental import pallas as pl
from jax.experimental.pallas import tpu as pltpu
from jax.sharding import PartitionSpec as P

MOMENTUM = 0.9
RATE = 0.01
FAST_RATE = 0.05
DECAY = 0.8
HIGHEST = lax.Precision.HIGHEST
F32 = jnp.float32
LOW = jnp.bfloat16
MESH = pl.DeviceIdType.MESH
MIB = 1024 * 1024

EMB = 10
FIELDS = 39
FPAD = 40
REDUCED = 13
UNITS = 400
ZROWS = 112
ZPARTS = ((0, 64), (64, 48))
UDEV = 100
SLOTS = 8
BATCH = 256
FETCH = 1024
PAIRS = 741
PPAD = 768
HALF = 384
ROWS = 5
TILES = 416
HALVES = TILES // 2
CHUNKS = (112, 96)
KTILES = 75
BUFFERS = 3
AUX = 38
SMALL = 16
STEPS = 4095


def dot(left, right, contract, precision=None):
    return lax.dot_general(
        left, right, ((contract[0], contract[1]), ((), ())),
        precision=precision, preferred_element_type=F32,
    )


def nn(left, right, precision=None):
    return dot(left, right, ((1,), (0,)), precision)


def nt(left, right, precision=None):
    return dot(left, right, ((1,), (1,)), precision)


def tn(left, right, precision=None):
    return dot(left, right, ((0,), (0,)), precision)


def in_hbm(arrays):
    return tuple(pltpu.with_memory_space_constraint(array, pltpu.HBM) for array in arrays)


def nesterov(weight, momentum, average, grad, step_rate):
    velocity = MOMENTUM * momentum + grad
    updated = weight - step_rate * (grad + MOMENTUM * velocity)
    smoothed = DECAY * average + (1.0 - DECAY) * updated
    return (velocity, smoothed, updated)


def pool(ids_ref, count_ref, rows_ref, counts, table, out_ref, between):
    rows = rows_ref[...].astype(F32)
    largest = jnp.maximum(jnp.max(jnp.abs(rows), keepdims=True), 1e-30)
    fixed = jnp.round(rows * (STEPS / largest)).astype(jnp.int32) + (STEPS + 1)
    for chunk in range(8):
        part = fixed[:, 128 * chunk:128 * (chunk + 1)]
        for k in range(EMB // 2):
            table[k, chunk:chunk + 1, :] = part[2 * k:2 * k + 1, :] * 65536 + part[2 * k + 1:2 * k + 2, :]
    counts[0:FIELDS, :] = count_ref[...]
    counts[FIELDS:FPAD, :] = jnp.ones((1, BATCH), jnp.int32)
    ids_ref[FIELDS] = jnp.full((SLOTS, BATCH), 8 * FETCH, jnp.int32)
    sublane = lax.broadcasted_iota(jnp.int32, (8, 128), 0)
    unit = largest * (1.0 / STEPS)

    def group(g, carry):
        fields = pl.ds(pl.multiple_of(8 * g, 8), 8)
        for h in range(2):
            lanes = slice(128 * h, 128 * (h + 1))
            live = counts[fields, lanes]
            found = [[] for _ in range(EMB // 2)]
            for row in range(8):
                ids = jnp.where(live[row:row + 1, :] > sublane, ids_ref[8 * g + row, :, lanes], 8 * FETCH)
                totals = [None] * (EMB // 2)
                for slot in range(SLOTS):
                    wide = jnp.broadcast_to(ids[slot:slot + 1, :], (8, 128))
                    lane = wide & 127
                    hit = (wide >> 7) == sublane
                    for k in range(EMB // 2):
                        value = jnp.take_along_axis(table[k], lane, axis=1, mode="promise_in_bounds")
                        value = jnp.where(hit, value, 0)
                        totals[k] = value if totals[k] is None else totals[k] + value
                for k in range(EMB // 2):
                    found[k].append(jnp.sum(totals[k], axis=0, keepdims=True))
            factor = unit / live.astype(F32)
            for k in range(EMB // 2):
                both = jnp.concatenate(found[k], axis=0)
                for part, word in enumerate(((both >> 16) & 65535, both & 65535)):
                    total = (word - (STEPS + 1) * live).astype(F32)
                    out_ref[2 * k + part, fields, lanes] = (total * factor).astype(LOW).astype(F32)
        return carry

    lax.fori_loop(0, 2, group, 0)
    between()
    lax.fori_loop(2, FPAD // 8, group, 0)
    out_ref[:, FPAD - 8:FPAD, :] = jnp.where(
        lax.broadcasted_iota(jnp.int32, (EMB, 8, BATCH), 1) == 7, 0.0, out_ref[:, FPAD - 8:FPAD, :]
    )


def gate_of(before):
    return 0.5 + 0.5 * jnp.tanh(0.5 * before)


def silu_slope(before, gate):
    return gate * (1.0 + before * (1.0 - gate))


def softplus(value):
    return jnp.maximum(value, 0.0) + jnp.log1p(jnp.exp(-jnp.abs(value)))


def two_terms(value):
    high = value.astype(LOW)
    return high, (value - high.astype(F32)).astype(LOW)


def split(value):
    high = value.astype(LOW).astype(F32)
    return jnp.concatenate([high, value - high], axis=0).astype(LOW)


def step_kernel(*refs):
    hbm, pairs_in, refs = refs[:20], refs[20:23], refs[23:]
    gout_ref, small_ref, egrad_ref, logit_ref, *pairs_out = refs[:7]
    loaded, refs = refs[7:27], refs[27:]
    pair_ref = pairs_out[0]
    (
        ids_ref, count_ref, rows_ref, hidden_ref,
        field_ref, bias_ref, readout_ref, grad_ref, squ_ref, exc_ref,
        first_ref, second_ref, first_t_ref, second_t_ref, place_ref, place_t_ref, same_ref, rows_of_ref, cols_of_ref, bil_ref,
    ) = loaded
    (
        emb_ref, counts, table, w_low, w_turned, left, right, feats, feats_peer, source, scale_s, sq_s, z1_s, z2_s,
        squ_pad, exc_pad, fpad, fplaced, fplaced_t, hid_all, vec_all, hid_full, hid_turned,
        pre_part, rs_in, pre_full, gf, gf_peer,
        acc, box1, box2, aux, aux_in,
        dsrc, eterm, zsend, zrecv, zsend2, zrecv2, zsend3, zrecv3, small_z, small_x, small_y, small_c,
        load_sem, pair_sem, hid_send, hid_recv, vec_send, vec_recv, twin_sem, feat_sem,
        rsz_send, rsz_recv, agz_send, agz_recv,
        gf_sem, aux_sem, red_send, red_recv, own_sem, gat_send, gat_recv, core_send, core_recv,
        zs_send, zs_recv, smz_send, smz_recv, smx_send, smx_recv, smy_send, smy_recv, smc_sem,
    ) = refs
    dp = lax.axis_index("dp")
    me = lax.axis_index("mp")
    core = dp % 2
    yy = (dp // 2) % 4
    xx = dp // 8

    def at_dp(x, y, c):
        return (x * 4 + y) * 2 + c

    rings = (
        [((xx + off) % 4, at_dp((xx + off) % 4, yy, core)) for off in (1, 3, 2)],
        [((yy + off) % 4, at_dp(xx, (yy + off) % 4, core)) for off in (1, 3, 2)],
    )
    places = (xx, yy)
    twin = at_dp(xx, yy, 1 - core)
    peers = [(me + off) % 4 for off in (1, 3, 2)]
    stream = me // 2
    columns = (me % 2) * ROWS
    half = ((me + 1) // 2) % 2
    near = me + 1 - 2 * (me % 2)
    cross = 3 - me

    def remote(src, dst, send, recv, **where):
        return pltpu.make_async_remote_copy(
            src_ref=src, dst_ref=dst, send_sem=send, recv_sem=recv, device_id=where, device_id_type=MESH
        )

    targets = (ids_ref.at[pl.ds(0, FIELDS)],) + loaded[1:]
    loads = [pltpu.make_async_copy(src, dst, load_sem.at[n]) for n, (src, dst) in enumerate(zip(hbm, targets))]
    for copy in loads:
        copy.start()
    pair_loads = [
        pltpu.make_async_copy(src, dst, pair_sem.at[n]) for n, (src, dst) in enumerate(zip(pairs_in, pairs_out))
    ]
    barrier = pltpu.get_barrier_semaphore()
    for peer in peers:
        pl.semaphore_signal(barrier, inc=1, device_id={"mp": peer}, device_id_type=MESH)
    for dev in [dev for ring in rings for _, dev in ring] + [twin]:
        pl.semaphore_signal(barrier, inc=1, device_id={"dp": dev}, device_id_type=MESH)

    lanes_me = pl.ds(pl.multiple_of(128 * me, 128), 128)
    hid_copies = []
    for n, peer in enumerate(peers):
        mine = hid_all.at[core, :, lanes_me]
        hid_copies.append(remote(mine, mine, hid_send.at[n], hid_recv.at[n], mp=peer))
        mine = vec_all.at[:, lanes_me]
        hid_copies.append(remote(mine, mine, vec_send.at[n], vec_recv.at[n], mp=peer))

    def share_hidden():
        for copy in loads[3:]:
            copy.wait()
        fpad[...] = jnp.zeros_like(fpad)
        fpad[:, 0:UDEV] = hidden_ref[core]
        hid_all[core, :, lanes_me] = fpad[...].astype(LOW)
        fpad[0:8, :] = jnp.zeros((8, 128), F32)
        fpad[0:3, 0:UDEV] = bias_ref[...]
        fpad[3:4, 0:UDEV] = readout_ref[...].astype(LOW).astype(F32)
        vec_all[:, lanes_me] = fpad[0:8, :]
        pl.semaphore_wait(barrier, 10)
        for copy in hid_copies:
            copy.start()

    for copy in loads[:3]:
        copy.wait()
    for copy in pair_loads:
        copy.start()
    pool(ids_ref, count_ref, rows_ref, counts, table, emb_ref, share_hidden)

    squ_pad[...] = jnp.zeros_like(squ_pad)
    squ_pad[0:REDUCED, 0:FIELDS] = squ_ref[...]
    exc_pad[...] = jnp.zeros_like(exc_pad)
    exc_pad[0:REDUCED, 0:FIELDS] = exc_ref[...]
    squeezer = squ_pad[:, 0:FPAD]
    exciter = exc_pad[:, 0:FPAD]
    emb = emb_ref[...]
    squeezed = jnp.sum(emb, axis=0) * (1.0 / EMB)
    z1 = nn(squeezer, squeezed, HIGHEST)
    z2 = tn(exciter, z1 * gate_of(z1), HIGHEST)
    scales = softplus(z2)
    sq_s[...] = squeezed
    z1_s[...] = z1
    z2_s[...] = z2
    scale_s[...] = scales
    factor = jnp.where(stream == 0, jnp.ones_like(scales), scales)
    for k in range(EMB):
        source[k] = emb_ref[k] * factor

    for k in range(ROWS):
        projected = source[0] * bil_ref[0, columns + k]
        for l in range(1, EMB):
            projected = projected + source[l] * bil_ref[l, columns + k]
        left_k = nn(first_ref[...], split(projected))
        right_k = nn(second_ref[...], split(source[columns + k]))
        left[k] = left_k.astype(LOW)
        right[k] = right_k.astype(LOW)
        feats[k] = (left_k * right_k).astype(LOW)
    feat_copy = remote(
        feats.at[:, pl.ds(pl.multiple_of(HALF * (1 - core), HALF), HALF), :], feats_peer,
        feat_sem.at[0], feat_sem.at[1], dp=twin,
    )
    feat_copy.start()
    fpad[0:8, :] = jnp.zeros((8, 128), F32)
    for k in range(EMB):
        fpad[FPAD * k:FPAD * k + FIELDS, 0:UDEV] = field_ref[k]
        fpad[FPAD * k + FIELDS:FPAD * (k + 1), :] = jnp.zeros((1, 128), F32)
    field_low = fpad[...].astype(LOW)
    place_own = place_ref[lanes_me, :]
    fplaced_t[...] = nt(place_t_ref[:, lanes_me], field_low).astype(LOW)
    emb_low = emb.reshape(EMB * FPAD, BATCH).astype(LOW)
    pre = nn(fplaced_t[...], emb_low)
    pair_loads[0].wait()
    for k in range(ROWS):
        w_low[k, :, 640:PPAD] = jnp.zeros((UNITS, PPAD - 640), LOW)
        w_low[k, :, 0:PAIRS] = pair_ref[k].astype(LOW)
        pre = pre + nn(w_low[k], feats[k])
    pre_part[0:UNITS, :] = pre.astype(LOW)
    pre_part[UNITS:4 * ZROWS, :] = jnp.zeros((4 * ZROWS - UNITS, BATCH), LOW)

    rs_copies = []
    for part, (low_row, count) in enumerate(ZPARTS):
        for n, peer in enumerate(peers):
            rows = pl.ds(pl.multiple_of(ZROWS * peer + low_row, 16), count)
            box = rs_in.at[n, pl.ds(low_row, count)]
            rs_copies.append(remote(pre_part.at[rows], box, rsz_send.at[part, n], rsz_recv.at[part, n], mp=peer))
            rs_copies[-1].start()
    for copy in hid_copies:
        copy.wait()
    layer = hid_all.at[core]
    hid_twin = remote(layer, layer, twin_sem.at[0], twin_sem.at[1], dp=twin)
    hid_twin.start()
    fplaced[...] = nn(field_low, place_own).astype(LOW)
    ag_copies = []
    for part, (low_row, count) in enumerate(ZPARTS):
        for copy in rs_copies[3 * part:3 * part + 3]:
            copy.wait()
        own_rows = pl.ds(pl.multiple_of(ZROWS * me + low_row, 16), count)
        total = pre_part[own_rows, :].astype(F32)
        for n in range(3):
            total = total + rs_in[n, low_row:low_row + count].astype(F32)
        pre_full[own_rows, :] = total.astype(LOW)
        mine = pre_full.at[own_rows]
        for n, peer in enumerate(peers):
            ag_copies.append(remote(mine, mine, agz_send.at[part, n], agz_recv.at[part, n], mp=peer))
            ag_copies[-1].start()

    hid_twin.wait()
    for layer in range(2):
        hid_full[layer] = nn(hid_all[layer], place_ref[...]).astype(LOW)
        hid_turned[layer] = nt(place_t_ref[...], hid_all[layer]).astype(LOW)
    vec_rows = nn(vec_all[...], place_ref[...].astype(F32), HIGHEST)
    vec_cols = nt(place_t_ref[...].astype(F32), vec_all[...], HIGHEST)
    for copy in ag_copies:
        copy.wait()

    pre_first = pre_full[0:UNITS, :].astype(F32) + vec_cols[:, 0:1]
    gate_first = gate_of(pre_first)
    act_first = (pre_first * gate_first).astype(LOW)
    pre_second = nn(hid_turned[0], act_first) + vec_cols[:, 1:2]
    gate_second = gate_of(pre_second)
    act_second = (pre_second * gate_second).astype(LOW)
    pre_third = nn(hid_turned[1], act_second) + vec_cols[:, 2:3]
    gate_third = gate_of(pre_third)
    act_third = (pre_third * gate_third).astype(LOW)
    upstream = grad_ref[...].astype(F32).reshape(1, BATCH)
    grad_third = ((vec_cols[:, 3:4] * upstream) * silu_slope(pre_third, gate_third)).astype(LOW)
    grad_second = (nn(hid_full[1], grad_third) * silu_slope(pre_second, gate_second)).astype(LOW)
    grad_first = (nn(hid_full[0], grad_second) * silu_slope(pre_first, gate_first)).astype(LOW)
    gf[...] = grad_first
    gf_copy = remote(gf, gf_peer, gf_sem.at[0], gf_sem.at[1], dp=twin)
    gf_copy.start()

    first_mine = nn(place_own, grad_first).astype(LOW)
    second_mine = nn(place_own, grad_second).astype(LOW)
    third_mine = nn(place_own, grad_third).astype(LOW)
    aux[0:25] = nt(emb_low, first_mine).astype(LOW).reshape(25, 16, 128)
    aux[25:50] = nt(act_first, second_mine).astype(LOW).reshape(25, 16, 128)
    aux[50:75] = nt(act_second, third_mine).astype(LOW).reshape(25, 16, 128)
    aux[75] = jnp.zeros((16, 128), LOW)
    aux_copy = remote(
        aux.at[pl.ds(AUX * (1 - core), AUX)], aux_in, aux_sem.at[0], aux_sem.at[1], dp=twin
    )
    aux_copy.start()

    feat_copy.wait()
    own_half = pl.ds(pl.multiple_of(HALF * core, HALF), HALF)
    gf_copy.wait()
    for k in range(ROWS):
        grad = (nt(gf[...], feats[k, own_half, :]) + nt(gf_peer[...], feats_peer[k])).astype(LOW)
        tiles = [grad[:, 128 * j:128 * (j + 1)].reshape(25, 16, 128) for j in range(3)]
        acc[KTILES * k:KTILES * (k + 1)] = jnp.stack(tiles, axis=1).reshape(KTILES, 16, 128)
    acc[KTILES * ROWS + AUX:TILES] = jnp.zeros((TILES - KTILES * ROWS - AUX, 16, 128), LOW)

    offsets = (0, CHUNKS[0])
    starts = [[HALVES * h + offsets[c] for c in range(2)] for h in range(2)]

    def size_of(t, c):
        return CHUNKS[c] // (4, 16)[t]

    def box_of(t, h, n, c):
        return (box1, box2)[t].at[h, n, pl.ds(offsets[c] // (4, 16)[t], size_of(t, c))]

    def reduce_send(t, c):
        size = size_of(t, c)
        copies = []
        for n in range(3):
            for h in range(2):
                place, dev = rings[(h + t) % 2][n]
                src = acc.at[pl.ds(starts[h][c] + place * size, size)]
                copies.append(
                    remote(src, box_of(t, h, n, c), red_send.at[t, h, c, n], red_recv.at[t, h, c, n], dp=dev)
                )
                copies[-1].start()
        for h in range(2):
            starts[h][c] = starts[h][c] + places[(h + t) % 2] * size
        return copies

    def reduce_add(t, c, copies):
        for copy in copies:
            copy.wait()
        for h in range(2):
            keep = pl.ds(starts[h][c], size_of(t, c))
            total = acc[keep].astype(F32)
            for n in range(3):
                total = total + box_of(t, h, n, c)[...].astype(F32)
            acc[keep] = total.astype(LOW)

    own_copies = []
    core_copies = []

    def pass_on(h, c, slot, start, count):
        where = gout_ref.at[core, pl.ds(start, count)]
        copy = remote(where, where, core_send.at[h, c, slot], core_recv.at[h, c, slot], dp=twin)
        copy.start()
        core_copies.append(copy)

    def gather_send(t, c):
        size = size_of(t, c)
        copies = []
        for n in range(3):
            for h in range(2):
                _, dev = rings[(h + t) % 2][n]
                where = gout_ref.at[core, pl.ds(starts[h][c], size)]
                src = acc.at[pl.ds(starts[h][c], size)] if t == 1 else where
                copy = remote(src, where, gat_send.at[t, h, c, n], gat_recv.at[t, h, c, n], dp=dev)
                copy.start()
                sender = rings[(h + t) % 2][(1, 0, 2)[n]][0]
                came = starts[h][c] + (sender - places[(h + t) % 2]) * size
                copies.append((copy, h, n, came))
        for h in range(2):
            if t == 1:
                where = pl.ds(starts[h][c], size)
                own = pltpu.make_async_copy(acc.at[where], gout_ref.at[core, where], own_sem.at[h, c])
                own.start()
                own_copies.append(own)
            starts[h][c] = starts[h][c] - places[(h + t) % 2] * size
        return copies

    def gather_wide(c, copies):
        for copy, _, _, _ in copies:
            copy.wait()
        for own in own_copies[2 * c:2 * c + 2]:
            own.wait()
        wide = gather_send(0, c)
        for h in range(2):
            pass_on(h, c, 3, starts[h][c] + places[h] * size_of(0, c), size_of(0, c))
        return wide

    def gather_end(c, copies):
        for copy, h, n, came in copies:
            copy.wait()
            pass_on(h, c, n, came, size_of(0, c))

    moving = [reduce_send(0, 0)]
    aux_copy.wait()
    aux_mine = aux[pl.ds(AUX * core, AUX)].astype(F32) + aux_in[...].astype(F32)
    acc[KTILES * ROWS:KTILES * ROWS + AUX] = aux_mine.astype(LOW)
    moving.append(reduce_send(0, 1))
    act_mine = nn(place_own, act_third).astype(LOW)
    ones = jnp.ones((16, BATCH), LOW)
    upstream_rows = jnp.broadcast_to(upstream, (16, BATCH)).astype(LOW)
    row_iota = lax.broadcasted_iota(jnp.int32, (16, 128), 0)
    vec_grads = jnp.where(row_iota == 0, nt(ones, first_mine), 0.0)
    vec_grads = vec_grads + jnp.where(row_iota == 1, nt(ones, second_mine), 0.0)
    vec_grads = vec_grads + jnp.where(row_iota == 2, nt(ones, third_mine), 0.0)
    vec_grads = vec_grads + jnp.where(row_iota == 3, nt(upstream_rows, act_mine), 0.0)

    dprojected = []
    dchosen = []
    for k in range(ROWS):
        w_turned[k] = jnp.transpose(w_low[k])
        dfeat = nn(w_turned[k], gf[...])
        dprojected.append(nn(first_t_ref[...], (dfeat * right[k].astype(F32)).astype(LOW)))
        dchosen.append(nn(second_t_ref[...], (dfeat * left[k].astype(F32)).astype(LOW)))
    for l in range(EMB):
        total = dprojected[0] * bil_ref[l, columns]
        for k in range(1, ROWS):
            total = total + dprojected[k] * bil_ref[l, columns + k]
        dsrc[l] = total
    for k in range(ROWS):
        dsrc[columns + k] = dsrc[columns + k] + dchosen[k]
    eterm[...] = nn(fplaced[...], gf[...]).reshape(EMB, FPAD, BATCH)
    lanes_away = pl.ds(pl.multiple_of(128 * (1 - half), 128), 128)
    lanes_own = pl.ds(pl.multiple_of(128 * half, 128), 128)
    zsend[0] = dsrc[:, :, lanes_away].reshape(EMB * FPAD, 128).astype(LOW)
    zsend[1] = eterm[:, :, lanes_away].reshape(EMB * FPAD, 128).astype(LOW)
    z_copies = [remote(zsend.at[n], zrecv.at[n], zs_send.at[n], zs_recv.at[n], mp=near) for n in range(2)]
    for copy in z_copies:
        copy.start()
    source_high, source_rest = two_terms(source[...].reshape(EMB * FPAD, BATCH))
    dproj_high, dproj_rest = two_terms(jnp.concatenate(dprojected, axis=0))
    products = nt(source_high, dproj_high) + nt(source_high, dproj_rest) + nt(source_rest, dproj_high)
    products = products * same_ref[...].astype(F32)
    bil_rows = nn(nn(rows_of_ref[...].astype(F32), products, HIGHEST), cols_of_ref[me % 2].astype(F32), HIGHEST)
    bil_rows = jnp.where(row_iota == 15, jnp.sum(upstream) * 0.25, bil_rows)
    reduce_add(0, 0, moving[0])
    moving[0] = reduce_send(1, 0)

    z_copies[0].wait()
    back = dsrc[:, :, lanes_own] + zrecv[0].astype(F32).reshape(EMB, FPAD, 128)
    emb_half = emb_ref[:, :, lanes_own]
    z1 = z1_s[:, lanes_own]
    z2 = z2_s[:, lanes_own]
    dscale = jnp.sum(back * emb_half, axis=0)
    dz2 = dscale * gate_of(z2)
    gate = gate_of(z1)
    dexciter = nt(z1 * gate, dz2, HIGHEST)
    dz1 = nn(exciter, dz2, HIGHEST) * silu_slope(z1, gate)
    dsqueezer = nt(dz1, sq_s[:, lanes_own], HIGHEST)
    weighted = jnp.where(stream == 0, jnp.zeros((1, 1), F32), jnp.ones((1, 1), F32))

    small_z[me] = jnp.concatenate([dsqueezer * weighted, dexciter * weighted, bil_rows[:, 0:128 - 2 * FPAD]], axis=1)
    small = []
    for n, peer in enumerate(peers):
        small.append(remote(small_z.at[me], small_z.at[me], smz_send.at[n], smz_recv.at[n], mp=peer))
        small[n].start()
    dsqueezed = tn(squeezer, dz1, HIGHEST) * (1.0 / EMB)
    through = back * scale_s[:, lanes_own][None] + dsqueezed[None]
    z_copies[1].wait()
    term = eterm[:, :, lanes_own] + zrecv[1].astype(F32).reshape(EMB, FPAD, 128)
    mine = term + jnp.where(stream == 0, back, through)
    zsend2[...] = mine.reshape(EMB * FPAD, 128).astype(LOW)
    z_copy = remote(zsend2, zrecv2, zs_send.at[2], zs_recv.at[2], mp=cross)
    z_copy.start()

    reduce_add(0, 1, moving[1])
    moving[1] = reduce_send(1, 1)
    for copy in small:
        copy.wait()
    small_x[xx, 0:SMALL] = small_z[0] + small_z[1] + small_z[2] + small_z[3]
    small_x[xx, SMALL:SMALL + 8] = vec_grads[0:8]
    small = []
    for n, (_, dev) in enumerate(rings[0]):
        small.append(remote(small_x.at[xx], small_x.at[xx], smx_send.at[n], smx_recv.at[n], dp=dev))
        small[n].start()
    reduce_add(1, 0, moving[0])
    moving[0] = gather_send(1, 0)
    reduce_add(1, 1, moving[1])
    moving[1] = gather_send(1, 1)
    for copy in small:
        copy.wait()
    small_y[yy] = small_x[0] + small_x[1] + small_x[2] + small_x[3]
    small = []
    for n, (_, dev) in enumerate(rings[1]):
        small.append(remote(small_y.at[yy], small_y.at[yy], smy_send.at[n], smy_recv.at[n], dp=dev))
        small[n].start()
    moving[0] = gather_wide(0, moving[0])
    moving[1] = gather_wide(1, moving[1])
    logit_ref[...] = nn(vec_rows.astype(LOW), act_third)
    z_copy.wait()
    whole = (zsend2[...].astype(F32) + zrecv2[...].astype(F32)).astype(LOW)
    zsend3[...] = whole
    z_copy = remote(zsend3, zrecv3, zs_send.at[3], zs_recv.at[3], mp=near)
    z_copy.start()
    egrad_ref[:, :, lanes_own] = whole.reshape(EMB, FPAD, 128)
    gather_end(0, moving[0])
    for copy in small:
        copy.wait()
    small_c[core] = small_y[0] + small_y[1] + small_y[2] + small_y[3]
    small = remote(small_c.at[core], small_c.at[core], smc_sem.at[0], smc_sem.at[1], dp=twin)
    small.start()
    z_copy.wait()
    egrad_ref[:, :, lanes_away] = zrecv3[...].reshape(EMB, FPAD, 128)
    gather_end(1, moving[1])
    small.wait()
    small_ref[...] = small_c[0] + small_c[1]
    for copy in core_copies + pair_loads[1:]:
        copy.wait()


def step(id_lists, id_counts, embed_rows, pair_set, fieldwise, hidden, biases, readout, logit_grad, bilinear, squeezer, exciter):
    first_index, second_index = np.triu_indices(FIELDS, 1)
    first = np.zeros((PPAD, FPAD), np.float32)
    second = np.zeros((PPAD, FPAD), np.float32)
    first[np.arange(PAIRS), first_index] = 1.0
    second[np.arange(PAIRS), second_index] = 1.0
    place = np.zeros((512, UNITS), np.float32)
    unit = np.arange(UNITS)
    place[128 * (unit // UDEV) + unit % UDEV, unit] = 1.0
    pair_field = np.arange(EMB * FPAD)
    same = (pair_field[:, None] % FPAD == pair_field[None, :ROWS * FPAD] % FPAD).astype(np.float32)
    rows_of = (np.arange(16)[:, None] == pair_field[None, :] // FPAD).astype(np.float32)
    cols_of = np.stack([
        (pair_field[:ROWS * FPAD, None] // FPAD + ROWS * part == np.arange(128)[None, :]).astype(np.float32) for part in range(2)
    ])
    constants = (
        np.concatenate([first, first], axis=1), np.concatenate([second, second], axis=1), first.T, second.T, place, place.T,
        same, rows_of, cols_of,
    )
    constants = [jnp.asarray(value, LOW) for value in constants]
    small_operands = (
        id_lists.transpose(1, 0, 2), id_counts, embed_rows.T, hidden,
        fieldwise, biases, readout.reshape(1, UDEV), logit_grad, squeezer.T, exciter,
        *constants, bilinear,
    )
    vmem = pl.BlockSpec(memory_space=pltpu.VMEM)
    hbm = pl.BlockSpec(memory_space=pltpu.HBM)
    anywhere = pl.BlockSpec(memory_space=pl.ANY)
    low = lambda *shape: pltpu.VMEM(shape, LOW)
    full = lambda *shape: pltpu.VMEM(shape, F32)
    dma = lambda *shape: pltpu.SemaphoreType.DMA(shape)
    return pl.pallas_call(
        step_kernel,
        out_shape=(
            pltpu.VMEM((2, TILES, 16, 128), LOW),
            jax.ShapeDtypeStruct((SMALL + 8, 128), F32),
            jax.ShapeDtypeStruct((EMB, FPAD, BATCH), LOW),
            jax.ShapeDtypeStruct((8, BATCH), F32),
        ) + (pltpu.VMEM(pair_set[0].shape, F32),) * 3,
        in_specs=[hbm] * 23,
        out_specs=(anywhere, vmem, vmem, vmem) + (vmem,) * 3,
        scratch_shapes=[
            pltpu.VMEM((FPAD, SLOTS, BATCH), jnp.int32),
            *(pltpu.VMEM(array.shape, array.dtype) for array in small_operands[1:-1]),
            pltpu.SMEM((EMB, EMB), F32),
            full(EMB, FPAD, BATCH), pltpu.VMEM((FPAD, BATCH), jnp.int32), pltpu.VMEM((EMB // 2, 8, 128), jnp.int32),
            low(ROWS, UNITS, PPAD), low(ROWS, PPAD, UNITS),
            low(ROWS, PPAD, BATCH), low(ROWS, PPAD, BATCH), low(ROWS, PPAD, BATCH), low(ROWS, HALF, BATCH),
            full(EMB, FPAD, BATCH), full(FPAD, BATCH), full(FPAD, BATCH), full(16, BATCH), full(FPAD, BATCH),
            full(16, 128), full(16, 128), full(EMB * FPAD, 128), low(EMB * FPAD, UNITS), low(UNITS, EMB * FPAD),
            low(2, UNITS, 512), full(8, 512), low(2, UNITS, UNITS), low(2, UNITS, UNITS),
            low(4 * ZROWS, BATCH), low(3, ZROWS, BATCH), low(4 * ZROWS, BATCH), low(UNITS, BATCH), low(UNITS, BATCH),
            low(TILES, 16, 128), low(2, 3, HALVES // 4, 16, 128), low(2, 3, HALVES // 16, 16, 128),
            low(2 * AUX, 16, 128), low(AUX, 16, 128),
            full(EMB, FPAD, BATCH), full(EMB, FPAD, BATCH),
            low(2, EMB * FPAD, 128), low(2, EMB * FPAD, 128), low(EMB * FPAD, 128), low(EMB * FPAD, 128),
            low(EMB * FPAD, 128), low(EMB * FPAD, 128),
            full(4, SMALL, 128), full(4, SMALL + 8, 128), full(4, SMALL + 8, 128), full(2, SMALL + 8, 128),
            dma(20), dma(3), dma(3), dma(3), dma(3), dma(3), dma(2), dma(2),
            dma(2, 3), dma(2, 3), dma(2, 3), dma(2, 3),
            dma(2), dma(2), dma(2, 2, 2, 3), dma(2, 2, 2, 3), dma(2, 2), dma(2, 2, 2, 3), dma(2, 2, 2, 3),
            dma(2, 2, 4), dma(2, 2, 4),
            dma(4), dma(4), dma(3), dma(3), dma(3), dma(3), dma(3), dma(3), dma(2),
        ],
        compiler_params=pltpu.CompilerParams(
            collective_id=0, has_side_effects=True, vmem_limit_bytes=32 * MIB
        ),
        name="step",
    )(*in_hbm(small_operands), *in_hbm(pair_set))


def update_kernel(grads, small, egrad, logit, weight, momentum, average, *refs):
    inputs, refs = refs[:24], refs[24:]
    logits_out, egrad_out = refs[:2]
    pair_outs, outputs, refs = refs[2:5], refs[5:29], refs[29:]
    held, refs = refs[:24], refs[24:]
    logits_held, egrad_held, pair_held, in_sem, out_sem, pair_sem = refs

    loads = [pltpu.make_async_copy(src, dst, in_sem.at[n]) for n, (src, dst) in enumerate(zip(inputs, held))]
    for copy in loads:
        copy.start()

    def put(which, at, grad, rate):
        weight, momentum, average = held[3 * which:3 * which + 3]
        values = nesterov(weight[at], momentum[at], average[at], grad, rate)
        for ref, value in zip((weight, momentum, average), values):
            ref[at] = value

    def small_ones():
        for copy in loads:
            copy.wait()
        tiles = slice(KTILES * ROWS, KTILES * ROWS + AUX)
        whole = jnp.concatenate([grads[0, tiles], grads[1, tiles]], axis=0).astype(F32).reshape(2 * AUX * 16, 128)
        for k in range(EMB):
            put(0, (k,), whole[FPAD * k:FPAD * k + FIELDS, 0:UDEV], RATE)
        for layer in range(2):
            put(1, (layer,), whole[UNITS * (layer + 1):UNITS * (layer + 2), 0:UDEV], RATE)
        everything = (slice(None), slice(None))
        offset_weight = held[12][...]
        put(2, everything, small[SMALL:SMALL + 3, 0:UDEV], FAST_RATE)
        put(3, everything, small[SMALL + 3:SMALL + 4, 0:UDEV], RATE)
        put(4, everything, small[15:16, 2 * FPAD:2 * FPAD + 1], RATE)
        put(5, everything, small[0:EMB, 2 * FPAD:2 * FPAD + EMB], RATE)
        put(6, everything, small[0:REDUCED, 0:FIELDS], FAST_RATE)
        put(7, everything, small[0:REDUCED, FPAD:FPAD + FIELDS], FAST_RATE)
        logits_held[...] = logit[3:4, :] + offset_weight
        for k in range(EMB):
            egrad_held[k] = egrad[k, :, :].astype(F32)[0:FIELDS]
        ends = zip((logits_held, egrad_held) + tuple(held), (logits_out, egrad_out) + tuple(outputs))
        ends = [pltpu.make_async_copy(src, dst, out_sem.at[n]) for n, (src, dst) in enumerate(ends)]
        for copy in ends:
            copy.start()
        return ends

    stores = []
    for k in range(ROWS):
        slot = k % BUFFERS
        if k >= BUFFERS:
            for copy in stores[3 * (k - BUFFERS):3 * (k - BUFFERS + 1)]:
                copy.wait()
        for c in range(2):
            for j in range(3):
                first = HALF * c + 128 * j
                last = min(first + 128, PAIRS)
                tiles = [grads[c, KTILES * k + 3 * r + j] for r in range(UNITS // 16)]
                grad = jnp.concatenate(tiles, axis=0).astype(F32)[:, 0:last - first]
                at = (k, slice(None), slice(first, last))
                values = nesterov(weight[at], momentum[at], average[at], grad, RATE)
                for n, value in enumerate(values):
                    pair_held[slot, n, :, first:last] = value
        for n in range(3):
            stores.append(pltpu.make_async_copy(pair_held.at[slot, n], pair_outs[n].at[k], pair_sem.at[slot, n]))
            stores[-1].start()
        if k == 1:
            lasts = small_ones()
    for copy in lasts + stores[3 * (ROWS - BUFFERS):]:
        copy.wait()


def update(grads, small, egrad, logit, sets):
    vmem = pl.BlockSpec(memory_space=pltpu.VMEM)
    hbm = pl.BlockSpec(memory_space=pltpu.HBM)
    pair, others = sets[0], [array for arrays in sets[1:] for array in arrays]
    shapes = [(1, BATCH), (EMB, FIELDS, BATCH)] + [array.shape for array in pair] + [array.shape for array in others]
    return pl.pallas_call(
        update_kernel,
        in_specs=[vmem] * 7 + [hbm] * 24,
        out_specs=[hbm] * 29,
        out_shape=[jax.ShapeDtypeStruct(shape, F32) for shape in shapes],
        scratch_shapes=[
            *(pltpu.VMEM(array.shape, F32) for array in others),
            pltpu.VMEM((1, BATCH), F32), pltpu.VMEM((EMB, FIELDS, BATCH), F32),
            pltpu.VMEM((BUFFERS, 3, UNITS, PAIRS), F32),
            pltpu.SemaphoreType.DMA((24,)), pltpu.SemaphoreType.DMA((26,)), pltpu.SemaphoreType.DMA((BUFFERS, 3)),
        ],
        compiler_params=pltpu.CompilerParams(vmem_limit_bytes=18 * MIB),
        name="update",
    )(grads, small, egrad, logit, *pair, *in_hbm(others[:12]), *others[12:15], *in_hbm(others[15:]))


def per_device(
    id_lists, id_counts, embed_rows, logit_grad,
    bilinear, bilinear_momentum, bilinear_average,
    squeezer, squeezer_momentum, squeezer_average,
    exciter, exciter_momentum, exciter_average,
    pairwise, pairwise_momentum, pairwise_average,
    fieldwise, fieldwise_momentum, fieldwise_average,
    hidden, hidden_momentum, hidden_average,
    biases, biases_momentum, biases_average,
    readout, readout_momentum, readout_average,
    offset, offset_momentum, offset_average,
):
    turn = lambda *arrays: tuple(array.swapaxes(-1, -2) for array in arrays)
    pair_set = turn(pairwise, pairwise_momentum, pairwise_average)
    grads, small, egrad, logit, *held = step(
        id_lists, id_counts, embed_rows, pair_set, fieldwise, hidden, biases, readout, logit_grad, bilinear, squeezer, exciter
    )
    row = lambda *arrays: tuple(array.reshape(1, -1) for array in arrays)
    outs = update(
        grads, small, egrad, logit,
        [
            held,
            (fieldwise, fieldwise_momentum, fieldwise_average),
            (hidden, hidden_momentum, hidden_average),
            (biases, biases_momentum, biases_average),
            row(readout, readout_momentum, readout_average),
            row(offset, offset_momentum, offset_average),
            (bilinear, bilinear_momentum, bilinear_average),
            turn(squeezer, squeezer_momentum, squeezer_average),
            (exciter, exciter_momentum, exciter_average),
        ],
    )
    logits, egrad_full = outs[0].reshape(-1), outs[1]
    pair, field, hid, bias, read, off, bil, squ, exc = (tuple(outs[2 + 3 * i:5 + 3 * i]) for i in range(9))
    flat = lambda arrays: tuple(array.reshape(-1) for array in arrays)
    return (logits, egrad_full) + bil + turn(*squ) + exc + turn(*pair) + field + hid + bias + flat(read) + flat(off)


def solution(mesh):
    whole = (P(),) * 3
    rows = (P("mp", None, None),) * 3
    units = (P(None, None, "mp"),) * 3
    vectors = (P(None, "mp"),) * 3
    line = (P("mp"),) * 3
    weights = whole + whole + whole + rows + units + units + vectors + line + whole
    return jax.shard_map(
        per_device,
        mesh=mesh,
        in_specs=(P(None, None, "dp"), P(None, "dp"), P("dp", None), P("dp")) + weights,
        out_specs=(P("dp"), P(None, None, "dp")) + weights,
        check_vma=False,
    )
```
